32 devices in a mesh: seq: 2 (over y), ctx: 16 (over z, x, core).
Axes of the slice: x: 2, y: 2, z: 4, core: 2. Of those that a mesh axis runs over, the one named last changes fastest.
Arguments:
- inputs: bfloat16 [2, 4096, 768], P('seq', 'ctx'), may hold values from -6 to 6
- cotangent: bfloat16 [2, 4096, 768], P('seq', 'ctx'), may hold values from -6 to 6
- gain_attn: bfloat16 [768], P(('seq', 'ctx')), may hold values from 0.099609375 to 1.8984375
- w_query: bfloat16 [768, 768], P(('seq', 'ctx')), may hold values from -0.09375 to 0.09375
- w_key: bfloat16 [768, 768], P(('seq', 'ctx')), may hold values from -0.09375 to 0.09375
- w_value: bfloat16 [768, 768], P(('seq', 'ctx')), may hold values from -0.21875 to 0.21875
- w_output: bfloat16 [768, 768], P(('seq', 'ctx')), may hold values from -1.75 to 1.75
- bias_table: bfloat16 [32, 12], replicated, may hold values from 89 to 107
- gain_ffn: bfloat16 [768], P(('seq', 'ctx')), may hold values from 0.099609375 to 1.8984375
- w_router: bfloat16 [768, 16], P(('seq', 'ctx')), may hold values from -0.109375 to 0.109375
- w_in: bfloat16 [16, 768, 3072], P('ctx'), may hold values from -0.21875 to 0.21875
- w_out: bfloat16 [16, 3072, 768], P('ctx'), may hold values from -1.75 to 1.75
- segments: int32 [2, 4096], P('seq', 'ctx'), may hold values from 0 to 15, never falling along the last dimension, each value on 1 to 512 neighbouring positions
- routes: int32 [2, 4096, 1], P('seq', 'ctx'), may hold values from 0 to 15; in each aligned block of 256 rows (0 to 255, 256 to 511, ..., all dimensions but the last counted through in order) at most 18 rows name the same one
Outputs:
- output: bfloat16 [2, 4096, 768], P('seq', 'ctx')
- grad_inputs: bfloat16 [2, 4096, 768], P('seq', 'ctx')
- grad_gain_attn: float32 [768], P(('seq', 'ctx'))
- grad_w_query: float32 [768, 768], P(('seq', 'ctx'))
- grad_w_key: float32 [768, 768], P(('seq', 'ctx'))
- grad_w_value: float32 [768, 768], P(('seq', 'ctx'))
- grad_w_output: float32 [768, 768], P(('seq', 'ctx'))
- grad_bias_table: float32 [32, 12], replicated
- grad_gain_ffn: float32 [768], P(('seq', 'ctx'))
- grad_w_router: float32 [768, 16], P(('seq', 'ctx'))
- grad_w_in: float32 [16, 768, 3072], P('ctx')
- grad_w_out: float32 [16, 3072, 768], P('ctx')
The draws below stay inside these ranges and needn't reach their ends.
Inputs may be any that keep to these rules, and one draw needn't show every extreme that they name: `segments`: segment numbers never fall along a sequence; each document spans 1 to 512 positions, and one in each sequence exactly 512. `routes`: within each aligned block of 256 positions no expert is chosen more than 18 times; some expert is chosen exactly 18 times in some blocks.
All inputs are finite; a program needn't handle non-finite values.
Results may differ from the reference program's by a relative error of at most 0.015.
The reference program's roundings to bfloat16 on the way count: a program that leaves them out, or rounds other values in their place, can miss the bound.
Values may be sent and summed in bfloat16 or wider, within the bound.
No kernel may reach another device: no remote copies, remote signals or barrier semaphores. Data moves between devices by JAX's collectives and lax.ppermute only.
A program may use at most 192 MiB of HBM per device.

```python
import math
import jax
import jax.numpy as jnp
import numpy as np
from jax import lax

D = 768
HEADS = 12
HEAD_DIM = 64
FF = 3072
BUCKETS = 32
TOK_DEV = 256
REACH = 2
EXPERTS = 16
SEQS = 2
SEQLEN = 4096
DOC_MAX = 512
DOCS = 16
CAP = 18
N_CTX = 16


def draw_bias_table(key, part):
    key = jax.random.fold_in(key, 11)
    head_key, entry_key = jax.random.split(key)
    levels = jax.random.uniform(head_key, (1, HEADS), jnp.float32, 92.0, 104.0)
    entries = jnp.clip(jax.random.normal(entry_key, (BUCKETS, HEADS), jnp.float32), -3.0, 3.0)
    return (levels + entries).astype(jnp.bfloat16)


def block_scale(stream_key, shape, pieces, smallest, top_value):
    gain = 1.0
    for position, blocks in pieces:
        steps = jax.random.uniform(jax.random.fold_in(jax.random.fold_in(stream_key, 6), position), (blocks,), jnp.float32, smallest / len(pieces), top_value / len(pieces))
        gain = gain * jnp.repeat(jnp.exp(steps), shape[position] // blocks).reshape((-1,) + (1,) * (len(shape) - 1 - position))
    return gain


def profile(count, total, bound, skew):
    portions = [(1 << 20) // math.isqrt(rank ** skew) + 1 for rank in range(2, count + 1)]
    rest, given = total - bound - (count - 1), [1] * (count - 1)
    while rest > 0:
        candidates = [i for i in range(count - 1) if given[i] < bound]
        pool, remaining = sum([portions[i] for i in candidates]), rest
        for i in candidates:
            addition = min(bound - given[i], max(1, remaining * portions[i] // pool), rest)
            given[i] = given[i] + addition
            rest = rest - addition
    return np.array([bound] + given)


def ragged_sizes(key, amount, total, bound, lean):
    if amount == 2:
        one = jax.random.randint(key, (), max(1, total - bound), min(bound, total - 1) + 1)
        return jnp.stack([one, total - one])
    tallies = jnp.asarray(profile(amount, total, bound, lean), jnp.int32)
    couples = (amount - 1) // 2
    giver, receiver = tallies[1:1 + 2 * couples:2], tallies[2:2 + 2 * couples:2]
    room = jnp.minimum(giver - 1, bound - receiver)
    passed = jax.random.randint(jax.random.fold_in(key, 1), (couples,), 0, 1 << 20) % (room + 1)
    tallies = tallies.at[1:1 + 2 * couples:2].set(giver - passed).at[2:2 + 2 * couples:2].set(receiver + passed)
    return tallies[jax.random.permutation(jax.random.fold_in(key, 2), amount)]


def deal_out(rng, own, number, rows, count, top, bound, skew):
    ranking = jax.random.permutation(rng, count)
    heavy_load, usual = shares(count, rows * top, bound, skew, True), shares(count, rows * top, bound, skew, False)
    places = jnp.arange(count)

    def named(lengths, turn):
        used = int((lengths > 0).sum())
        fixed = max(1, used // 4)
        passed = fixed + (places - fixed + turn * (used - fixed)) % max(1, count - fixed)
        return jnp.zeros((count,), jnp.int32).at[ranking[jnp.where(places < fixed, places, passed)]].set(jnp.asarray(lengths, jnp.int32))

    lengths = jnp.where(number % 4 == 0, named(heavy_load, number // 4), named(usual, number - number // 4 - 1))
    mixed = jax.random.permutation(jax.random.fold_in(own, 3), count)
    source_of, receiver = mixed[0:count // 2 * 2:2], mixed[1:count // 2 * 2:2]
    slack = jnp.minimum(lengths[source_of] - 1, bound - lengths[receiver]) // 2
    slack = jnp.where((source_of == ranking[0]) | (receiver == ranking[0]) | (lengths[receiver] == 0), 0, jnp.maximum(slack, 0))
    passed = jax.random.randint(jax.random.fold_in(own, 4), (count // 2,), 0, 1 << 20) % (slack + 1)
    lengths = lengths.at[source_of].add(-passed).at[receiver].add(passed)
    members = jnp.searchsorted(jnp.cumsum(lengths), jnp.arange(rows * top), side="right").astype(jnp.int32)
    table = members.reshape(top, rows).T
    table = table[jax.random.permutation(jax.random.fold_in(own, 1), rows)]
    turn = jax.random.randint(jax.random.fold_in(own, 2), (rows, 1), 0, top)
    return jnp.take_along_axis(table, (jnp.arange(top)[None, :] + turn) % top, axis=1)


def shares(number_of, total, most, lean, full):
    weights = [(1 << 20) // math.isqrt(grade ** lean) + 1 for grade in range(1, number_of + 1)]
    largest = most if full else min(most, max(-(-total // number_of), total * weights[0] // sum(weights)))
    least = 1 if total - largest >= number_of - 1 else 0
    given, surplus = [largest] + [least] * (number_of - 1), total - largest - least * (number_of - 1)
    while surplus > 0:
        candidates = [i for i in range(1, number_of) if given[i] < largest] or [i for i in range(1, number_of) if given[i] < most]
        pool, remaining = sum([weights[i] for i in candidates]), surplus
        for i in candidates:
            addition = min(most - given[i], max(1, remaining * weights[i] // pool), surplus)
            given[i] = given[i] + addition
            surplus = surplus - addition
    return np.array(given)


def noise(own_key, dims, spread, limit, shards=(), kind=jnp.bfloat16):
    level = block_scale(own_key, dims, shards, -0.22, 0.18) if shards else 1.0
    drawn = jax.random.normal(own_key, dims, jnp.float32) * spread * level
    return jnp.minimum(jnp.maximum(drawn, -limit), limit).astype(kind)


def setup_inputs(seed: int = 0) -> dict:
    splits = jax.random.split(jax.random.key(seed), 15)
    inputs = noise(splits[0], (SEQS, SEQLEN, D), 1.0, 6.0, ((0, 2), (1, 16)))
    cotangent = noise(splits[1], (SEQS, SEQLEN, D), 1.0, 6.0, ((0, 2), (1, 16)))
    gain_attn = jnp.clip(1.0 + 0.18 * jax.random.normal(splits[2], (D,), jnp.float32), 0.099609375, 1.8984375).astype(jnp.bfloat16)
    w_query = noise(splits[3], (D, D), (5 * D) ** -0.5, 0.09375, ((0, 32),))
    w_key = noise(splits[4], (D, D), (5 * D) ** -0.5, 0.09375, ((0, 32),))
    w_value = noise(splits[5], (D, D), D ** -0.5, 0.21875, ((0, 32),))
    w_output = noise(splits[6], (D, D), (D // 64) ** -0.5, 1.75, ((0, 32),))
    bias_table = draw_bias_table(jax.random.fold_in(splits[14], 71), 0)
    gain_ffn = jnp.clip(1.0 + 0.18 * jax.random.normal(splits[8], (D,), jnp.float32), 0.099609375, 1.8984375).astype(jnp.bfloat16)
    w_router = noise(splits[9], (D, EXPERTS), (4 * D) ** -0.5, 0.109375, ((0, 32),))
    w_in = noise(splits[10], (EXPERTS, D, FF), D ** -0.5, 0.21875, ((0, 16),))
    w_out = noise(splits[11], (EXPERTS, FF, D), (max(1, FF // (EXPERTS * EXPERTS))) ** -0.5, 1.75, ((0, 16),))
    segments = jax.vmap(lambda own: jnp.searchsorted(jnp.cumsum(ragged_sizes(own, DOCS, SEQLEN, DOC_MAX, 1)), jnp.arange(SEQLEN), side="right"))(jax.random.split(splits[12], SEQS)).reshape((SEQS, SEQLEN)).astype(jnp.int32)
    routes_keys = jax.random.split(jax.random.fold_in(splits[13], 1), SEQS * SEQLEN // TOK_DEV)
    routes_turns = jax.random.permutation(jax.random.fold_in(splits[13], 3), SEQS * SEQLEN // TOK_DEV)
    routes = jax.vmap(lambda own, number: deal_out(jax.random.fold_in(splits[13], 2), own, number, TOK_DEV, EXPERTS, 1, CAP, 1))(routes_keys, routes_turns).reshape((SEQS, SEQLEN, 1))
    return {"inputs": inputs, "cotangent": cotangent, "gain_attn": gain_attn, "w_query": w_query, "w_key": w_key, "w_value": w_value, "w_output": w_output, "bias_table": bias_table, "gain_ffn": gain_ffn, "w_router": w_router, "w_in": w_in, "w_out": w_out, "segments": segments, "routes": routes}


EPSILON = 1e-06
NEGATIVE = -1e+30
THRESHOLDS = (12, 16, 23, 32, 46, 64, 91)

@jax.custom_vjp
def low(v):
    return lax.optimization_barrier(v.astype(jnp.bfloat16)).astype(jnp.float32)

@jax.custom_vjp
def low_back(v):
    return v

def low_keep(v):
    return (low(v), None)

def low_pass(kept, grad):
    return (grad,)

def back_keep(v):
    return (v, None)

def back_low(kept, grad):
    return (low(grad),)
low.defvjp(low_keep, low_pass)
low_back.defvjp(back_keep, back_low)

def bucket_of(offset_pos):
    distance = jnp.abs(offset_pos)
    far_bucket = jnp.full(distance.shape, 8, jnp.int32)
    for border in THRESHOLDS:
        far_bucket = far_bucket + (distance >= border).astype(jnp.int32)
    near_bucket = jnp.where(distance < 8, distance, far_bucket)
    return near_bucket + jnp.where(offset_pos > 0, 16, 0).astype(jnp.int32)

def relative_grid(shift_rows, query_count, key_count):
    query_pos = lax.broadcasted_iota(jnp.int32, (query_count, key_count), 0)
    key_pos = lax.broadcasted_iota(jnp.int32, (query_count, key_count), 1)
    return key_pos - query_pos + shift_rows

def rms_scale(values):
    return lax.rsqrt(lax.optimization_barrier(jnp.mean(values * values, axis=-1, keepdims=True)) + EPSILON)

def attention(query_matrix, key_matrix, value_matrix, bucket_table, segments):
    blocks = SEQLEN // TOK_DEV
    margin = REACH * TOK_DEV
    window = (2 * REACH + 1) * TOK_DEV
    key_pad = jnp.pad(key_matrix.reshape(SEQS, SEQLEN, HEADS, HEAD_DIM), ((0, 0), (margin, margin), (0, 0), (0, 0)))
    value_pad = jnp.pad(value_matrix.reshape(SEQS, SEQLEN, HEADS, HEAD_DIM), ((0, 0), (margin, margin), (0, 0), (0, 0)))
    seg_pad = jnp.pad(segments, ((0, 0), (margin, margin)), constant_values=-1)
    query_blocks = query_matrix.reshape(SEQS * blocks, TOK_DEV, HEADS, HEAD_DIM)
    seg_blocks = segments.reshape(SEQS * blocks, TOK_DEV)
    seq_ids = jnp.repeat(jnp.arange(SEQS, dtype=jnp.int32), blocks)
    block_ids = jnp.tile(jnp.arange(blocks, dtype=jnp.int32), SEQS)
    bias_tile = jnp.take(bucket_table.T, bucket_of(relative_grid(-margin, TOK_DEV, window)), axis=1)

    def one_block(block_item):
        query_tile, seg_query, seq_id, block_id = block_item
        zero_index = jnp.zeros((), jnp.int32)
        block_start = (block_id * TOK_DEV).astype(jnp.int32)
        key_win = lax.dynamic_slice(key_pad, (seq_id, block_start, zero_index, zero_index), (1, window, HEADS, HEAD_DIM))[0]
        value_win = lax.dynamic_slice(value_pad, (seq_id, block_start, zero_index, zero_index), (1, window, HEADS, HEAD_DIM))[0]
        seg_win = lax.dynamic_slice(seg_pad, (seq_id, block_start), (1, window))[0]
        raw_scores = jnp.einsum('qhd,khd->hqk', query_tile, key_win, precision=lax.Precision.HIGHEST) + bias_tile
        raw_scores = low_back(raw_scores)
        same_doc = seg_query[:, None] == seg_win[None, :]
        scores = jnp.where(same_doc[None], raw_scores, NEGATIVE)
        prob_low = low(jax.nn.softmax(scores, axis=-1))
        return jnp.einsum('hqk,khd->qhd', prob_low, value_win, precision=lax.Precision.HIGHEST)
    outcome = lax.map(jax.checkpoint(one_block), (query_blocks, seg_blocks, seq_ids, block_ids))
    return outcome.reshape(SEQS, SEQLEN, HEADS * HEAD_DIM)

def reference(inputs, cotangent, gain_attn, w_query, w_key, w_value, w_output, bias_table, gain_ffn, w_router, w_in, w_out, segments, routes):
    highest_precision = lax.Precision.HIGHEST
    route_ids = routes[..., 0].reshape(SEQS, N_CTX, TOK_DEV)
    route_hot = (route_ids[..., None] == jnp.arange(EXPERTS, dtype=jnp.int32)).astype(jnp.int32)
    slot_index = lax.optimization_barrier(jnp.sum((jnp.cumsum(route_hot, axis=2) - route_hot) * route_hot, axis=3))
    target = route_ids * CAP + slot_index
    dispatch = (target[..., None] == jnp.arange(EXPERTS * CAP, dtype=jnp.int32)).astype(jnp.float32)
    route_float = route_hot.astype(jnp.float32).reshape(SEQS, SEQLEN, EXPERTS)

    def forward(tokens, gain_one, query_weight, key_weight, value_weight, output_weight, bucket_table, gain_two, router_weight, expert_in, expert_out):
        normed_one = tokens * rms_scale(tokens)
        first_residual = low(normed_one * gain_one)
        query_matrix = low(low_back(jnp.einsum('igb,bt->igt', first_residual, query_weight, precision=highest_precision)))
        key_matrix = low(low_back(jnp.einsum('igb,bt->igt', first_residual, key_weight, precision=highest_precision)))
        value_matrix = low(low_back(jnp.einsum('igb,bt->igt', first_residual, value_weight, precision=highest_precision)))
        context_rows = low(low_back(attention(query_matrix, key_matrix, value_matrix, bucket_table, segments)))
        attention_result = low_back(jnp.einsum('igb,bt->igt', context_rows, output_weight, precision=highest_precision))
        middle = tokens + attention_result
        normed_two = middle * rms_scale(middle)
        second_residual = low(normed_two * gain_two)
        router_scores = low_back(jnp.einsum('igb,bt->igt', second_residual, router_weight, precision=highest_precision))
        route_prob = jax.nn.softmax(router_scores, axis=-1)
        gate_prob = lax.optimization_barrier(jnp.sum(route_prob * route_float, axis=-1))
        hidden_blocks = second_residual.reshape(SEQS, N_CTX, TOK_DEV, D)
        dispatched = jnp.einsum('sctr,sctd->scrd', dispatch, hidden_blocks, precision=highest_precision)
        dispatched = low_back(dispatched.reshape(SEQS, N_CTX, EXPERTS, CAP, D))
        before = low_back(jnp.einsum('scekd,edf->scekf', dispatched, expert_in, precision=highest_precision))
        active = low(jax.nn.gelu(before, approximate=True))
        produced = low(low_back(jnp.einsum('scekf,efd->scekd', active, expert_out, precision=highest_precision)))
        combined = jnp.einsum('sctr,scrd->sctd', dispatch, produced.reshape(SEQS, N_CTX, EXPERTS * CAP, D), precision=highest_precision)
        combined = combined.reshape(SEQS, SEQLEN, D)
        return middle + gate_prob[..., None] * combined
    operands = tuple((operand.astype(jnp.float32) for operand in (inputs, gain_attn, w_query, w_key, w_value, w_output, bias_table, gain_ffn, w_router, w_in, w_out)))
    output, pullback = jax.vjp(forward, *operands)
    grads = pullback(cotangent.astype(jnp.float32))
    return (output.astype(jnp.bfloat16), grads[0].astype(jnp.bfloat16), grads[1], grads[2], grads[3], grads[4], grads[5], grads[6], grads[7], grads[8], grads[9], grads[10])
```

```python
import functools

import jax
import jax.numpy as jnp
from jax import lax
from jax.experimental import pallas as pl
from jax.experimental.pallas import tpu as pltpu
from jax.sharding import PartitionSpec as P

EPSILON = 1e-06
NEGATIVE = -1e30
THRESHOLDS = (12, 16, 23, 32, 46, 64, 91)
AXES = ("seq", "ctx")
BLK = 256
LANES = 128
FAR = 91
GELU_A = 0.7978845608028654
GELU_B = 0.044715

BF16 = jnp.bfloat16
F32 = jnp.float32
VMEM = pltpu.VMEM


def params(mib=48):
    return pltpu.CompilerParams(vmem_limit_bytes=mib * 1024 * 1024)


def whole(shape):
    return pl.BlockSpec(shape, lambda *_: (0,) * len(shape))


def smem():
    return pl.BlockSpec(memory_space=pltpu.SMEM)


def nn(a, b):
    return lax.dot_general(a, b, (((1,), (0,)), ((), ())), preferred_element_type=F32)


def nt(a, b):
    return lax.dot_general(a, b, (((1,), (1,)), ((), ())), preferred_element_type=F32)


def tn(a, b):
    return lax.dot_general(a, b, (((0,), (0,)), ((), ())), preferred_element_type=F32)


def iota(shape, dim):
    return lax.broadcasted_iota(jnp.int32, shape, dim)


def bucket_of(offset_pos):
    distance = jnp.abs(offset_pos)
    far_bucket = jnp.full(distance.shape, 8, jnp.int32)
    for border in THRESHOLDS:
        far_bucket = far_bucket + (distance >= border).astype(jnp.int32)
    near_bucket = jnp.where(distance < 8, distance, far_bucket)
    return near_bucket + jnp.where(offset_pos > 0, 16, 0).astype(jnp.int32)


def three_parts(value):
    high = value.astype(BF16)
    rest = value - high.astype(F32)
    middle = rest.astype(BF16)
    return high, middle, (rest - middle.astype(F32)).astype(BF16)


def pack_rows(target_row, rows, cap, depth, count, extra=None):
    total = count * depth
    width = rows.shape[0]
    place = iota((total, width), 0) - target_row
    parts = rows.shape[1] // LANES
    message = jnp.zeros((total, LANES), F32)
    for part in range(parts):
        hot = (place == part * cap).astype(BF16)
        message = message + nn(hot, rows[:, part * LANES : (part + 1) * LANES])
    if extra is not None:
        base_row, slot_col, value = extra
        ours = iota((total, width), 0) - base_row
        lane_hot = iota((width, LANES), 1) == slot_col
        for part, piece in enumerate(three_parts(value)):
            hot = (ours == parts * cap + part).astype(BF16)
            message = message + nn(hot, jnp.where(lane_hot, piece, jnp.zeros_like(piece)))
    return message.astype(BF16)


def unpack_rows(target_col, message, parts, cap):
    place = iota((target_col.shape[0], message.shape[0]), 1) - target_col
    pieces = []
    for part in range(parts):
        hot = (place == part * cap).astype(BF16)
        pieces.append(nn(hot, message))
    return pieces


def unpack_value(base_col, slot_col, message, parts, cap):
    place = iota((base_col.shape[0], message.shape[0]), 1) - base_col
    hot = ((place >= parts * cap) & (place < parts * cap + 3)).astype(BF16)
    values = nn(hot, message)
    return jnp.sum(jnp.where(iota(values.shape, 1) == slot_col, values, 0.0), axis=1, keepdims=True)


def pack_kernel(cap, depth, count, target_ref, rows_ref, out_ref):
    out_ref[...] = pack_rows(target_ref[...], rows_ref[...], cap, depth, count)


def unpack_kernel(cap, target_ref, message_ref, out_ref):
    parts = out_ref.shape[1] // LANES
    pieces = unpack_rows(target_ref[...], message_ref[...], parts, cap)
    for part, piece in enumerate(pieces):
        out_ref[:, part * LANES : (part + 1) * LANES] = piece.astype(BF16)


def qkv_kernel(x_ref, gain_ref, wq_ref, wk_ref, wv_ref, hid_ref, q_ref, k_ref, v_ref):
    tokens = x_ref[...].astype(F32)
    scale = lax.rsqrt(jnp.mean(tokens * tokens, axis=-1, keepdims=True) + EPSILON)
    hidden = (tokens * scale * gain_ref[...]).astype(BF16)
    hid_ref[...] = hidden
    q_ref[...] = nn(hidden, wq_ref[...]).astype(BF16)
    k_ref[...] = nn(hidden, wk_ref[...]).astype(BF16)
    v_ref[...] = nn(hidden, wv_ref[...]).astype(BF16)


def own_half(value, turn):
    lane = iota(value.shape, 1)
    keep = (lane < LANES // 2) if turn == 0 else (lane >= LANES // 2)
    return jnp.where(keep, value, jnp.zeros_like(value))


def scores_of(query, keys, bias, left, right, mask):
    raw = nt(query, keys)
    near = bias.shape[1]
    edge = (keys.shape[0] - near) // 2
    raw = jnp.concatenate(
        [
            raw[:, :edge] + left,
            raw[:, edge : edge + near] + bias.astype(F32),
            raw[:, edge + near :] + right,
        ],
        axis=1,
    )
    return jnp.where(mask, raw, NEGATIVE)


def attend_kernel(
    far_ref, q_ref, k_ref, v_ref, bias_ref, segq_ref, segk_ref, ctx_ref, low_ref, lse_ref
):
    pair = pl.program_id(0)
    blocks = q_ref.shape[0] // BLK
    window = 5 * BLK
    lane = iota((BLK, LANES), 1)
    for block in range(blocks):
        rows = slice(block * BLK, (block + 1) * BLK)
        cols = slice(block * BLK, block * BLK + window)
        query = q_ref[rows, :]
        keys = k_ref[cols, :]
        values = v_ref[cols, :]
        mask = segq_ref[rows, :] == segk_ref[:, cols]
        outs = []
        logs = jnp.zeros((BLK, LANES), F32)
        for turn in range(2):
            head = pair * 2 + turn
            scores = scores_of(
                own_half(query, turn), keys, bias_ref[turn], far_ref[0, head], far_ref[1, head], mask
            )
            top = jnp.max(scores, axis=1, keepdims=True)
            weight = jnp.exp(scores - top)
            total = jnp.sum(weight, axis=1, keepdims=True)
            outs.append(nn((weight * (1.0 / total)).astype(BF16), values))
            logs = jnp.where(lane == turn, top + jnp.log(total), logs)
        context = jnp.where(lane < LANES // 2, outs[0], outs[1])
        ctx_ref[rows, :] = context
        low_ref[rows, :] = context.astype(BF16)
        lse_ref[rows, :] = logs


def rolled_left(value, steps):
    return value if steps == 0 else pltpu.roll(value, value.shape[1] - steps, 1)


def diagonal_sums(value):
    eight = jnp.zeros((8, value.shape[1]), F32)
    for first in range(0, value.shape[0], 8):
        eight = eight + rolled_left(value[first : first + 8], first)
    one = jnp.zeros((1, value.shape[1]), F32)
    for row in range(8):
        one = one + rolled_left(eight[row : row + 1], row)
    return one


def own_backward_kernel(
    far_ref,
    q_ref,
    k_ref,
    v_ref,
    gctx_ref,
    ctx_ref,
    lse_ref,
    bias_ref,
    hot_ref,
    segq_ref,
    segk_ref,
    dq_ref,
    dk_ref,
    dv_ref,
    tab_ref,
):
    pair = pl.program_id(0)
    blocks = q_ref.shape[0] // BLK
    window = 5 * BLK
    near = bias_ref.shape[2]
    edge = (window - near) // 2
    lane = iota((BLK, LANES), 1)
    dk_ref[...] = jnp.zeros_like(dk_ref)
    dv_ref[...] = jnp.zeros_like(dv_ref)
    near_sum = [jnp.zeros((BLK, near), F32), jnp.zeros((BLK, near), F32)]
    left_sum = [jnp.zeros((BLK, edge), F32), jnp.zeros((BLK, edge), F32)]
    right_sum = [jnp.zeros((BLK, edge), F32), jnp.zeros((BLK, edge), F32)]
    for block in range(blocks):
        rows = slice(block * BLK, (block + 1) * BLK)
        cols = slice(block * BLK, block * BLK + window)
        keys = k_ref[cols, :]
        values = v_ref[cols, :]
        mask = segq_ref[rows, :] == segk_ref[:, cols]
        mine = slice((blocks - block) * BLK, (2 * blocks - block) * BLK)
        gctx_all = gctx_ref[rows, :]
        product = gctx_all.astype(F32) * ctx_ref[rows, :]
        logs = lse_ref[rows, :]
        outs = []
        for turn in range(2):
            head = pair * 2 + turn
            query = own_half(q_ref[rows, :], turn)
            gctx = own_half(gctx_all, turn)
            scores = scores_of(
                query, keys, bias_ref[turn], far_ref[0, head], far_ref[1, head], mask
            )
            probs = jnp.exp(scores - logs[:, turn : turn + 1])
            delta = jnp.sum(own_half(product, turn), axis=1, keepdims=True)
            grads = (probs * (nt(gctx, values) - delta)).astype(BF16)
            outs.append(nn(grads, keys))
            dk_ref[...] += tn(grads[:, mine], query)
            dv_ref[...] += tn(probs[:, mine].astype(BF16), gctx)
            wide = grads.astype(F32)
            left_sum[turn] = left_sum[turn] + wide[:, :edge]
            near_sum[turn] = near_sum[turn] + wide[:, edge : edge + near]
            right_sum[turn] = right_sum[turn] + wide[:, edge + near :]
        dq_ref[rows, :] = jnp.where(lane < LANES // 2, outs[0], outs[1]).astype(BF16)
    apart = iota((BLK, near), 1) - (2 * BLK - edge) - iota((BLK, near), 0)
    tab_lane = iota((1, LANES), 1)
    for turn in range(2):
        total = near_sum[turn]
        left = jnp.sum(left_sum[turn]) + jnp.sum(jnp.where(apart <= -FAR, total, 0.0))
        right = jnp.sum(right_sum[turn]) + jnp.sum(jnp.where(apart >= FAR, total, 0.0))
        close = jnp.where(jnp.abs(apart) < FAR, total, 0.0)
        diagonal = diagonal_sums(close)
        sums = lax.dot_general(
            diagonal,
            hot_ref[...],
            (((1,), (0,)), ((), ())),
            precision=lax.Precision.HIGHEST,
            preferred_element_type=F32,
        )
        sums = sums + jnp.where(tab_lane == 15, left, 0.0) + jnp.where(tab_lane == 31, right, 0.0)
        tab_ref[0, turn : turn + 1, :] = sums


def halo_backward_kernel(
    far_ref,
    qp_ref,
    qn_ref,
    k_ref,
    v_ref,
    gp_ref,
    gn_ref,
    lse_ref,
    delta_ref,
    biasp_ref,
    biasn_ref,
    segq_ref,
    segk_ref,
    dka_ref,
    dva_ref,
    dk_ref,
    dv_ref,
):
    pair = pl.program_id(0)
    own = k_ref.shape[0]
    half = LANES
    total_k = dka_ref[...]
    total_v = dva_ref[...]
    parts = []
    for side in range(2):
        q_side = qp_ref if side == 0 else qn_ref
        g_side = gp_ref if side == 0 else gn_ref
        for block in range(2):
            far_block = block == side
            rows = slice(block * BLK, (block + 1) * BLK)
            if far_block:
                cols = slice(0, BLK) if side == 0 else slice(own - BLK, own)
            else:
                cols = slice(0, own)
            parts.append((side, rows, cols, far_block, q_side, g_side))
    add_k = [jnp.zeros((BLK, LANES), F32), jnp.zeros((BLK, LANES), F32)]
    add_v = [jnp.zeros((BLK, LANES), F32), jnp.zeros((BLK, LANES), F32)]
    for side, rows, cols, far_block, q_side, g_side in parts:
        keys = k_ref[cols, :]
        values = v_ref[cols, :]
        mask = segk_ref[cols, :] == segq_ref[side, :, rows]
        count = cols.stop - cols.start
        for turn in range(2):
            head = pair * 2 + turn
            query = own_half(q_side[rows, :], turn)
            gctx = own_half(g_side[rows, :], turn)
            raw = nt(keys, query)
            far = far_ref[1 - side, head]
            if far_block:
                raw = raw + far
            elif side == 0:
                raw = jnp.concatenate(
                    [raw[:half] + biasp_ref[turn].astype(F32), raw[half:] + far], axis=0
                )
            else:
                raw = jnp.concatenate(
                    [raw[: count - half] + far, raw[count - half :] + biasn_ref[turn].astype(F32)],
                    axis=0,
                )
            scores = jnp.where(mask, raw, NEGATIVE)
            logs = lse_ref[side, pl.ds(head, 1), rows]
            delta = delta_ref[side, pl.ds(head, 1), rows]
            probs = jnp.exp(scores - logs)
            grads = (probs * (nt(values, gctx) - delta)).astype(BF16)
            got_k = nn(grads, query)
            got_v = nn(probs.astype(BF16), gctx)
            for index in range(count // BLK):
                place = (cols.start // BLK) + index
                part = slice(index * BLK, (index + 1) * BLK)
                add_k[place] = add_k[place] + got_k[part]
                add_v[place] = add_v[place] + got_v[part]
    dk_ref[...] = (total_k + jnp.concatenate(add_k, axis=0)).astype(BF16)
    dv_ref[...] = (total_v + jnp.concatenate(add_v, axis=0)).astype(BF16)


def delta_kernel(core_ref, mine_ref, came_ref, ctx_ref, gctx_ref, delta_ref):
    core = core_ref[0]
    tok = mine_ref.shape[0]
    width = mine_ref.shape[1]
    gctx_ref[pl.ds(pl.multiple_of(core * tok, tok), tok), :] = mine_ref[...]
    gctx_ref[pl.ds(pl.multiple_of((1 - core) * tok, tok), tok), :] = came_ref[...]
    product = gctx_ref[...].astype(F32) * ctx_ref[...]
    head_rows = delta_ref.shape[0]
    pick = (iota((head_rows, width), 1) // (LANES // 2) == iota((head_rows, width), 0)).astype(F32)
    delta_ref[...] = lax.dot_general(
        pick,
        product,
        (((1,), (1,)), ((), ())),
        precision=lax.Precision.HIGHEST,
        preferred_element_type=F32,
    )


def before_kernel(
    cap,
    depth,
    experts,
    core_ref,
    x_ref,
    own_ref,
    came_ref,
    wo_ref,
    gain_ref,
    wr_ref,
    target_ref,
    base_ref,
    route_ref,
    slot_ref,
    mid_ref,
    hid_ref,
    prob_ref,
    msg_ref,
):
    core = core_ref[0]
    tok = x_ref.shape[0]
    width = own_ref.shape[1]
    rows = pl.ds(pl.multiple_of(core * tok, tok), tok)
    own_w = wo_ref[pl.ds(pl.multiple_of(core * width, width), width), :]
    other_w = wo_ref[pl.ds(pl.multiple_of((1 - core) * width, width), width), :]
    attended = nn(own_ref[rows, :], own_w) + nn(came_ref[rows, :], other_w)
    middle = x_ref[...].astype(F32) + attended
    mid_ref[...] = middle
    scale = lax.rsqrt(jnp.mean(middle * middle, axis=-1, keepdims=True) + EPSILON)
    hidden = (middle * scale * gain_ref[...]).astype(BF16)
    hid_ref[...] = hidden
    logits = nn(hidden, wr_ref[...])
    lane = iota(logits.shape, 1)
    logits = jnp.where(lane < experts, logits, NEGATIVE)
    weight = jnp.exp(logits - jnp.max(logits, axis=1, keepdims=True))
    probs = weight / jnp.sum(weight, axis=1, keepdims=True)
    prob_ref[...] = probs
    gate = jnp.sum(jnp.where(lane == route_ref[...], probs, 0.0), axis=1, keepdims=True)
    msg_ref[...] = pack_rows(
        target_ref[...], hidden, cap, depth, experts, (base_ref[...], slot_ref[...], gate)
    )


def expert_kernel(
    cap,
    depth,
    count,
    msg_ref,
    cot_ref,
    win_ref,
    wout_ref,
    target_col_ref,
    target_row_ref,
    base_col_ref,
    base_row_ref,
    slot_ref,
    rows_ref,
    grad_ref,
    made_msg_ref,
    back_msg_ref,
    made_acc,
    back_acc,
):
    step = pl.program_id(0)
    parts = rows_ref.shape[1] // LANES

    @pl.when(step == 0)
    def _():
        message = msg_ref[...]
        for part, piece in enumerate(unpack_rows(target_col_ref[...], message, parts, cap)):
            rows_ref[:, part * LANES : (part + 1) * LANES] = piece.astype(BF16)
        gate = unpack_value(base_col_ref[...], slot_ref[...], message, parts, cap)
        grad_ref[...] = (gate * cot_ref[...].astype(F32)).astype(BF16)
        made_acc[...] = jnp.zeros_like(made_acc)
        back_acc[...] = jnp.zeros_like(back_acc)

    w_in = win_ref[0]
    w_out = wout_ref[0]
    before = nn(rows_ref[...], w_in)
    grad_active = nt(grad_ref[...], w_out)
    inner = jnp.tanh(GELU_A * (before + GELU_B * before * before * before))
    active = (0.5 * before * (1.0 + inner)).astype(BF16)
    made_acc[...] += nn(active, w_out)
    slope = 0.5 * (1.0 + inner) + 0.5 * before * (1.0 - inner * inner) * (
        GELU_A * (1.0 + 3.0 * GELU_B * before * before)
    )
    grad_before = (grad_active * slope).astype(BF16)
    back_acc[...] += nt(grad_before, w_in)

    @pl.when(step == pl.num_programs(0) - 1)
    def _():
        produced = made_acc[...].astype(BF16)
        grad_gate = jnp.sum(
            cot_ref[...].astype(F32) * produced.astype(F32), axis=1, keepdims=True
        )
        back_msg_ref[...] = pack_rows(
            target_row_ref[...],
            back_acc[...].astype(BF16),
            cap,
            depth,
            count,
            (base_row_ref[...], slot_ref[...], grad_gate),
        )
        made_msg_ref[...] = pack_rows(target_row_ref[...], produced, cap, depth, count)


def expert_grads_kernel(rows_ref, grad_ref, win_ref, wout_ref, din_ref, dout_ref):
    w_in = win_ref[0]
    w_out = wout_ref[0]
    rows = rows_ref[...]
    grad = grad_ref[...]
    before = nn(rows, w_in)
    grad_active = nt(grad, w_out)
    inner = jnp.tanh(GELU_A * (before + GELU_B * before * before * before))
    active = (0.5 * before * (1.0 + inner)).astype(BF16)
    slope = 0.5 * (1.0 + inner) + 0.5 * before * (1.0 - inner * inner) * (
        GELU_A * (1.0 + 3.0 * GELU_B * before * before)
    )
    grad_before = (grad_active * slope).astype(BF16)
    din_ref[0] = tn(rows, grad_before)
    dout_ref[0] = tn(active, grad)


def after_kernel(
    cap,
    core_ref,
    msg_ref,
    cot_ref,
    mid_ref,
    hid_ref,
    prob_ref,
    gain_ref,
    wr_ref,
    wo_ref,
    target_ref,
    base_ref,
    route_ref,
    slot_ref,
    gmid_ref,
    gattn_ref,
    mine_ref,
    theirs_ref,
    small_ref,
):
    core = core_ref[0]
    message = msg_ref[...]
    parts = cot_ref.shape[1] // LANES
    width = mine_ref.shape[1]
    came = jnp.concatenate(unpack_rows(target_ref[...], message, parts, cap), axis=1)
    grad_gate = unpack_value(base_ref[...], slot_ref[...], message, parts, cap)
    probs = prob_ref[...]
    lane = iota(probs.shape, 1)
    chosen = lane == route_ref[...]
    gate = jnp.sum(jnp.where(chosen, probs, 0.0), axis=1, keepdims=True)
    grad_logits = (grad_gate * probs * (chosen.astype(F32) - gate)).astype(BF16)
    grad_hidden = came + nt(grad_logits, wr_ref[...])
    middle = mid_ref[...]
    scale = lax.rsqrt(jnp.mean(middle * middle, axis=-1, keepdims=True) + EPSILON)
    normed = middle * scale
    rows = small_ref.shape[0] - 8
    small_ref[:rows, :] = tn(grad_logits, hid_ref[...])[:rows, :]
    gain_row = jnp.sum(grad_hidden * normed, axis=0, keepdims=True)
    small_ref[rows:, :] = jnp.broadcast_to(gain_row, (8, gain_row.shape[1]))
    grad_normed = grad_hidden * gain_ref[...]
    grad_middle = cot_ref[...].astype(F32) + scale * (
        grad_normed - normed * jnp.mean(grad_normed * normed, axis=-1, keepdims=True)
    )
    gmid_ref[...] = grad_middle
    low = grad_middle.astype(BF16)
    gattn_ref[...] = low
    own_w = wo_ref[pl.ds(pl.multiple_of(core * width, width), width), :]
    other_w = wo_ref[pl.ds(pl.multiple_of((1 - core) * width, width), width), :]
    theirs_ref[...] = nt(low, other_w).astype(BF16)
    mine_ref[...] = nt(low, own_w).astype(BF16)


def output_kernel(cap, msg_ref, mid_ref, prob_ref, target_ref, route_ref, out_ref):
    parts = out_ref.shape[1] // LANES
    combined = jnp.concatenate(unpack_rows(target_ref[...], msg_ref[...], parts, cap), axis=1)
    probs = prob_ref[...]
    chosen = iota(probs.shape, 1) == route_ref[...]
    gate = jnp.sum(jnp.where(chosen, probs, 0.0), axis=1, keepdims=True)
    out_ref[...] = (mid_ref[...] + gate * combined).astype(BF16)


class Place:
    def __init__(self):
        self.n_seq = lax.axis_size("seq")
        self.n_ctx = lax.axis_size("ctx")
        self.count = self.n_seq * self.n_ctx
        self.index = lax.axis_index("seq") * self.n_ctx + lax.axis_index("ctx")
        self.core = self.index % 2
        ctx_bits = (self.n_ctx - 1).bit_length()
        self.bits = (self.count - 1).bit_length()
        self.far_bits = list(range(ctx_bits - 1, 1, -1))
        self.near_bits = [1]
        self.seq_bits = list(range(self.bits - 1, ctx_bits - 1, -1))

    def swap(self, value, bit):
        pairs = [(i, i ^ (1 << bit)) for i in range(self.count)]
        return lax.ppermute(value, AXES, pairs)

    def bit(self, which):
        return (self.index >> which) & 1

    def shift(self, value, steps):
        pairs = []
        for row in range(self.n_seq):
            for col in range(self.n_ctx):
                if 0 <= col + steps < self.n_ctx:
                    pairs.append((row * self.n_ctx + col, row * self.n_ctx + col + steps))
        return lax.ppermute(value, AXES, pairs)

    def ordered(self, own, came, bit, axis, join):
        mine = self.bit(bit) == 1
        return join([jnp.where(mine, came, own), jnp.where(mine, own, came)], axis=axis)

    def gather(self, block, order):
        done = []
        for bit in order:
            came = self.swap(block, bit)
            axis = sum(1 for other in done if other > bit)
            block = self.ordered(block, came, bit, axis, jnp.stack)
            done.append(bit)
        return block.reshape((-1,) + block.shape[len(done) + 1 :])

    def scatter(self, value, order):
        left = sorted(order, reverse=True)
        value = value.reshape((2,) * len(left) + (-1,) + value.shape[1:])
        for bit in order:
            axis = left.index(bit)
            mine = self.bit(bit)
            gone = lax.dynamic_index_in_dim(value, 1 - mine, axis, keepdims=False).astype(BF16)
            kept = lax.dynamic_index_in_dim(value, mine, axis, keepdims=False)
            value = kept + self.swap(gone, bit).astype(F32)
            left.remove(bit)
        return value

    def total(self, value):
        for bit in range(self.bits):
            value = value + self.swap(value, bit)
        return value


def call(kernel, outs, *args, grid=None, in_specs=None, out_specs=None, scratch=(), mib=48):
    if in_specs is None:
        in_specs = [whole(a.shape) for a in args]
    if out_specs is None:
        out_specs = [whole(o[0]) for o in outs]
    shapes = [jax.ShapeDtypeStruct(*o) for o in outs]
    return pl.pallas_call(
        kernel,
        out_shape=shapes,
        grid=grid if grid is not None else (1,),
        in_specs=in_specs,
        out_specs=out_specs,
        scratch_shapes=list(scratch),
        compiler_params=params(mib),
    )(*args)


def local(
    inputs,
    cotangent,
    gain_attn,
    w_query,
    w_key,
    w_value,
    w_output,
    bias_table,
    gain_ffn,
    w_router,
    w_in,
    w_out,
    segments,
    routes,
):
    place = Place()
    core = place.core
    core_arg = core.reshape(1).astype(jnp.int32)
    x = inputs[0]
    tok, width = x.shape
    heads = bias_table.shape[1]
    mine_heads = heads // 2
    half = width // 2
    pairs = half // LANES
    experts = w_router.shape[1]
    hidden_units = w_in.shape[2]
    rows_dev = w_query.shape[0]
    cap = max(2, (9 * tok + 8 * experts - 1) // (8 * experts))
    parts = width // LANES
    depth = -(-(parts * cap + 3) // 16) * 16
    n_ctx = place.n_ctx
    slots = n_ctx * cap
    chip_bits = place.far_bits + place.near_bits + place.seq_bits
    order_a = place.far_bits + place.near_bits + place.seq_bits
    order_b = place.far_bits + place.seq_bits + place.near_bits
    order_c = place.near_bits + place.seq_bits + place.far_bits

    small_w = jnp.concatenate(
        [
            w_router,
            gain_attn[:, None],
            gain_ffn[:, None],
            jnp.zeros((rows_dev, LANES - experts - 2), BF16),
        ],
        axis=1,
    )
    stacked = jnp.concatenate([w_query, w_key, w_value], axis=0).reshape(3, rows_dev, 2, half)
    theirs = lax.dynamic_index_in_dim(stacked, 1 - core, 2, keepdims=False)
    ours = lax.dynamic_index_in_dim(stacked, core, 2, keepdims=False)
    came = place.swap(theirs, 0)
    start = place.ordered(ours, came, 0, 1, jnp.concatenate)
    small_all = place.gather(small_w, [0] + order_a)
    wq = place.gather(start[0], order_a)
    wk = place.gather(start[1], order_b)
    wv = place.gather(start[2], order_c)

    code = (segments[0] + 1).astype(BF16)
    x_ext = jnp.concatenate([x, jnp.broadcast_to(code[:, None], (tok, LANES))], axis=1)
    before_x = place.shift(x_ext, 2)
    after_x = place.shift(x_ext, -2)
    three = jnp.stack([before_x, x_ext, after_x])
    three_came = place.swap(three, 0)
    x_all = place.ordered(three, three_came, 0, 1, jnp.concatenate).reshape(6 * tok, width + LANES)
    seg_all = x_all[:, width].astype(jnp.int32)
    seg_col = seg_all[:, None]
    seg_row = seg_all[None, :]

    near = 2 * BLK
    apart = iota((BLK, near), 1) - LANES - iota((BLK, near), 0)
    bucket_ids = bucket_of(apart)
    table_mine = lax.dynamic_slice_in_dim(bias_table, core * mine_heads, mine_heads, 1)
    bias = jnp.zeros((mine_heads, BLK, near), BF16)
    for bucket in range(bias_table.shape[0]):
        bias = jnp.where(bucket_ids[None] == bucket, table_mine[bucket][:, None, None], bias)
    bias_prev = jnp.swapaxes(bias[:, :, near - LANES :], 1, 2)
    bias_next = jnp.swapaxes(bias[:, :, :LANES], 1, 2)
    far_bias = jnp.stack([table_mine[15], table_mine[31]]).astype(F32)
    hot = (
        bucket_of(iota((near, LANES), 0) - LANES) == iota((near, LANES), 1)
    ).astype(F32)

    route = routes[0, :, 0]
    route_hot = (route[:, None] == iota((tok, experts), 1)).astype(jnp.int32)
    slot = jnp.sum((jnp.cumsum(route_hot, axis=0) - route_hot) * route_hot, axis=1)
    base = route * depth
    target = base + slot
    e_src = jnp.arange(slots, dtype=jnp.int32) // cap
    e_slot = jnp.arange(slots, dtype=jnp.int32) % cap
    e_base = e_src * depth
    e_target = e_base + e_slot

    def exchange(message):
        message = message.reshape(n_ctx, depth, LANES)
        message = lax.all_to_all(message, "ctx", split_axis=0, concat_axis=0, tiled=True)
        return message.reshape(n_ctx * depth, LANES)

    gain_one = small_all[:, experts].astype(F32)[None, :]
    gain_two = small_all[:, experts + 1].astype(F32)[None, :]
    router = jnp.where(iota(small_all.shape, 1) < experts, small_all, 0).astype(BF16)

    rows_all = 6 * tok
    hid_all, q_all, k_all, v_all = call(
        qkv_kernel,
        [((rows_all, width), BF16)] + [((rows_all, half), BF16)] * 3,
        x_all,
        gain_one,
        wq,
        wk,
        wv,
        grid=(rows_all // BLK,),
        in_specs=[
            pl.BlockSpec((BLK, width), lambda i: (i, 0)),
            whole((1, width)),
            whole((width, half)),
            whole((width, half)),
            whole((width, half)),
        ],
        out_specs=[pl.BlockSpec((BLK, width), lambda i: (i, 0))]
        + [pl.BlockSpec((BLK, half), lambda i: (i, 0))] * 3,
    )
    own_rows = 2 * tok
    hid_one = hid_all[own_rows : 2 * own_rows]

    own_block = pl.BlockSpec((own_rows, LANES), lambda p: (1, p))
    all_block = pl.BlockSpec((rows_all, LANES), lambda p: (0, p))
    out_block = pl.BlockSpec((own_rows, LANES), lambda p: (0, p))
    bias_block = pl.BlockSpec((2, BLK, near), lambda p: (p, 0, 0))
    segq_block = pl.BlockSpec((own_rows, 1), lambda p: (1, 0))
    segk_block = whole((1, rows_all))
    ctx_f, ctx_low, lse = call(
        attend_kernel,
        [((own_rows, half), F32), ((own_rows, half), BF16), ((own_rows, half), F32)],
        far_bias,
        q_all,
        k_all,
        v_all,
        bias,
        seg_col,
        seg_row,
        grid=(pairs,),
        in_specs=[smem(), own_block, all_block, all_block, bias_block, segq_block, segk_block],
        out_specs=[out_block] * 3,
    )

    cot = cotangent[0]
    cot_msg = call(
        functools.partial(pack_kernel, cap, depth, experts),
        [((experts * depth, LANES), BF16)],
        target[None, :],
        cot,
    )[0]
    cot_msg, _ = lax.optimization_barrier((cot_msg, wv))
    cot_in = exchange(cot_msg)
    cot_rows = call(
        functools.partial(unpack_kernel, cap), [((slots, width), BF16)], e_target[:, None], cot_in
    )[0]

    wo_start = place.ordered(w_output, place.swap(w_output, 0), 0, 0, jnp.concatenate)
    wo = place.gather(wo_start, order_b)

    ctx_came = place.swap(ctx_low, 0)
    mid, hid_two, probs, msg = call(
        functools.partial(before_kernel, cap, depth, experts),
        [
            ((tok, width), F32),
            ((tok, width), BF16),
            ((tok, LANES), F32),
            ((experts * depth, LANES), BF16),
        ],
        core_arg,
        x,
        ctx_low,
        ctx_came,
        wo,
        gain_two,
        router,
        target[None, :],
        base[None, :],
        route[:, None],
        slot[:, None],
        in_specs=[smem()]
        + [
            whole(s)
            for s in (
                (tok, width),
                (own_rows, half),
                (own_rows, half),
                (width, width),
                (1, width),
                (width, LANES),
                (1, tok),
                (1, tok),
                (tok, 1),
                (tok, 1),
            )
        ],
    )
    msg_in = exchange(msg)

    fblk = 512
    win_block = pl.BlockSpec((1, width, fblk), lambda i: (0, 0, i))
    wout_block = pl.BlockSpec((1, fblk, width), lambda i: (0, i, 0))
    e_rows, e_grad, made_msg, back_msg = call(
        functools.partial(expert_kernel, cap, depth, n_ctx),
        [
            ((slots, width), BF16),
            ((slots, width), BF16),
            ((n_ctx * depth, LANES), BF16),
            ((n_ctx * depth, LANES), BF16),
        ],
        msg_in,
        cot_rows,
        w_in,
        w_out,
        e_target[:, None],
        e_target[None, :],
        e_base[:, None],
        e_base[None, :],
        e_slot[:, None],
        grid=(hidden_units // fblk,),
        in_specs=[
            whole((n_ctx * depth, LANES)),
            whole((slots, width)),
            win_block,
            wout_block,
            whole((slots, 1)),
            whole((1, slots)),
            whole((slots, 1)),
            whole((1, slots)),
            whole((slots, 1)),
        ],
        scratch=[VMEM((slots, width), F32), VMEM((slots, width), F32)],
    )
    back_in = exchange(back_msg)
    made_msg, _ = lax.optimization_barrier((made_msg, back_in))
    made_in = exchange(made_msg)

    pair_rows = jnp.concatenate([e_rows, e_grad], axis=1)
    for bit in place.seq_bits:
        pair_rows = jnp.concatenate([pair_rows, place.swap(pair_rows, bit)], axis=0)
    all_slots = pair_rows.shape[0]
    grad_w_in, grad_w_out = call(
        expert_grads_kernel,
        [(w_in.shape, F32), (w_out.shape, F32)],
        pair_rows,
        pair_rows,
        w_in,
        w_out,
        grid=(hidden_units // fblk,),
        in_specs=[
            pl.BlockSpec((all_slots, width), lambda i: (0, 0)),
            pl.BlockSpec((all_slots, width), lambda i: (0, 1)),
            win_block,
            wout_block,
        ],
        out_specs=[win_block, wout_block],
    )

    grad_mid, grad_attn, gctx_mine, gctx_theirs, small_grads = call(
        functools.partial(after_kernel, cap),
        [
            ((tok, width), F32),
            ((tok, width), BF16),
            ((tok, half), BF16),
            ((tok, half), BF16),
            ((experts + 8, width), F32),
        ],
        core_arg,
        back_in,
        cot,
        mid,
        hid_two,
        probs,
        gain_two,
        router,
        wo,
        target[:, None],
        base[:, None],
        route[:, None],
        slot[:, None],
        in_specs=[smem()]
        + [
            whole(s)
            for s in (
                (experts * depth, LANES),
                (tok, width),
                (tok, width),
                (tok, width),
                (tok, LANES),
                (1, width),
                (width, LANES),
                (width, width),
                (tok, 1),
                (tok, 1),
                (tok, 1),
                (tok, 1),
            )
        ],
    )
    output = call(
        functools.partial(output_kernel, cap),
        [((tok, width), BF16)],
        made_in,
        mid,
        probs,
        target[:, None],
        route[:, None],
    )[0]

    gctx_came = place.swap(gctx_theirs, 0)
    gctx, delta = call(
        delta_kernel,
        [((own_rows, half), BF16), ((8, own_rows), F32)],
        core_arg,
        gctx_mine,
        gctx_came,
        ctx_f,
        in_specs=[smem(), whole((tok, half)), whole((tok, half)), whole((own_rows, half))],
    )
    lse_rows = lse.reshape(own_rows, pairs, LANES)[:, :, :2].reshape(own_rows, mine_heads).T
    lse_rows = jnp.pad(lse_rows, ((0, 8 - mine_heads), (0, 0)))
    lse_halo = jnp.stack([place.shift(lse_rows, 2), place.shift(lse_rows, -2)])
    gctx_prev = place.shift(gctx, 2)
    gctx_next = place.shift(gctx, -2)
    delta_halo = jnp.stack([place.shift(delta, 2), place.shift(delta, -2)])

    dq, dk_own, dv_own, tab = call(
        own_backward_kernel,
        [
            ((own_rows, half), BF16),
            ((own_rows, half), F32),
            ((own_rows, half), F32),
            ((pairs, 8, LANES), F32),
        ],
        far_bias,
        q_all,
        k_all,
        v_all,
        gctx,
        ctx_f,
        lse,
        bias,
        hot,
        seg_col,
        seg_row,
        grid=(pairs,),
        in_specs=[
            smem(),
            own_block,
            all_block,
            all_block,
            out_block,
            out_block,
            out_block,
            bias_block,
            whole((near, LANES)),
            segq_block,
            segk_block,
        ],
        out_specs=[out_block] * 3 + [pl.BlockSpec((1, 8, LANES), lambda p: (p, 0, 0))],
    )
    seg_halo = jnp.stack([seg_row[:, :own_rows], seg_row[:, 2 * own_rows :]])
    dk, dv = call(
        halo_backward_kernel,
        [((own_rows, half), BF16)] * 2,
        far_bias,
        q_all,
        q_all,
        k_all,
        v_all,
        gctx_prev,
        gctx_next,
        lse_halo,
        delta_halo,
        bias_prev,
        bias_next,
        seg_halo,
        seg_col,
        dk_own,
        dv_own,
        grid=(pairs,),
        in_specs=[
            smem(),
            pl.BlockSpec((own_rows, LANES), lambda p: (0, p)),
            pl.BlockSpec((own_rows, LANES), lambda p: (2, p)),
            own_block,
            own_block,
            out_block,
            out_block,
            whole((2, 8, own_rows)),
            whole((2, 8, own_rows)),
            pl.BlockSpec((2, LANES, BLK), lambda p: (p, 0, 0)),
            pl.BlockSpec((2, LANES, BLK), lambda p: (p, 0, 0)),
            whole((2, 1, own_rows)),
            segq_block,
            out_block,
            out_block,
        ],
        out_specs=[out_block] * 2,
    )

    rs_a = order_a[::-1]
    rs_b = order_b[::-1]
    rs_c = order_c[::-1]
    ga_send = lax.dynamic_slice_in_dim(grad_attn, (1 - core) * half, half, 1)
    ga_mine = lax.dynamic_slice_in_dim(grad_attn, core * half, half, 1)
    ga_cols = place.ordered(ga_mine, place.swap(ga_send, 0), 0, 0, jnp.concatenate)
    ctx_full = place.ordered(ctx_low, ctx_came, 0, 1, jnp.concatenate)
    sum_o = place.scatter(tn(ctx_full, ga_cols), rs_b)
    sum_q = place.scatter(tn(hid_one, dq), rs_a)
    sum_k = place.scatter(tn(hid_one, dk), rs_b)
    sum_v = place.scatter(tn(hid_one, dv), rs_c)

    def finish(value):
        value = value.reshape((4, 2) + (rows_dev, half))
        gone = lax.dynamic_index_in_dim(value, 1 - core, 1, keepdims=False)
        kept = lax.dynamic_index_in_dim(value, core, 1, keepdims=False)
        return place.ordered(kept, place.swap(gone, 0), 0, 2, jnp.concatenate)

    sums = finish(jnp.stack([sum_q, sum_k, sum_v, sum_o]))

    part = nt(dq, wq) + nt(dk, wk) + nt(dv, wv)
    part = part.reshape(2, tok, width)
    part_came = place.swap(lax.dynamic_index_in_dim(part, 1 - core, 0, keepdims=False), 0)
    grad_hidden = lax.dynamic_index_in_dim(part, core, 0, keepdims=False) + part_came
    tokens = x.astype(F32)
    scale_one = lax.rsqrt(jnp.mean(tokens * tokens, axis=-1, keepdims=True) + EPSILON)
    normed_one = tokens * scale_one
    grad_gain_one = jnp.sum(grad_hidden * normed_one, axis=0)
    grad_normed = grad_hidden * gain_one
    grad_tokens = grad_mid + scale_one * (
        grad_normed - normed_one * jnp.mean(grad_normed * normed_one, axis=-1, keepdims=True)
    )

    table_rows = tab[:, :2, : bias_table.shape[0]].reshape(mine_heads, bias_table.shape[0])
    table_both = jnp.zeros((2, mine_heads, bias_table.shape[0]), F32)
    table_both = lax.dynamic_update_index_in_dim(table_both, table_rows, core, 0)
    table_flat = jnp.pad(table_both.reshape(1, -1), ((0, 0), (0, width - heads * bias_table.shape[0])))
    early = place.total(
        jnp.concatenate(
            [small_grads[: experts + 1], table_flat, jnp.zeros((6, width), F32)], axis=0
        )
    )
    late = place.total(jnp.broadcast_to(grad_gain_one[None], (8, width)))
    start_row = place.index * rows_dev
    grad_router = lax.dynamic_slice_in_dim(early[:experts], start_row, rows_dev, 1).T
    grad_gain_two = lax.dynamic_slice_in_dim(early[experts], start_row, rows_dev, 0)
    grad_gain_attn = lax.dynamic_slice_in_dim(late[0], start_row, rows_dev, 0)
    table_sum = early[experts + 1, : heads * bias_table.shape[0]].reshape(heads, -1).T

    return (
        output[None],
        grad_tokens.astype(BF16)[None],
        grad_gain_attn,
        sums[0],
        sums[1],
        sums[2],
        sums[3],
        table_sum,
        grad_gain_two,
        grad_router,
        grad_w_in,
        grad_w_out,
    )


def solution(mesh):
    rows = P(("seq", "ctx"), None)
    flat = P(("seq", "ctx"))
    tokens = P("seq", "ctx", None)
    expert = P("ctx", None, None)
    return jax.shard_map(
        local,
        mesh=mesh,
        in_specs=(
            tokens,
            tokens,
            flat,
            rows,
            rows,
            rows,
            rows,
            P(),
            flat,
            rows,
            expert,
            expert,
            P("seq", "ctx"),
            tokens,
        ),
        out_specs=(
            tokens,
            tokens,
            flat,
            rows,
            rows,
            rows,
            rows,
            P(),
            flat,
            rows,
            expert,
            expert,
        ),
        check_vma=False,
    )
```

```python
import functools

import jax
import jax.numpy as jnp
from jax import lax
from jax.experimental import pallas as pl
from jax.experimental.pallas import tpu as pltpu
from jax.sharding import PartitionSpec as P

EPSILON = 1e-06
NEGATIVE = -1e30
THRESHOLDS = (12, 16, 23, 32, 46, 64, 91)
AXES = ("seq", "ctx")
BLK = 256
LANES = 128
FAR = 91
GELU_A = 0.7978845608028654
GELU_B = 0.044715

BF16 = jnp.bfloat16
F32 = jnp.float32
VMEM = pltpu.VMEM


def params(mib=48):
    return pltpu.CompilerParams(vmem_limit_bytes=mib * 1024 * 1024)


def whole(shape):
    return pl.BlockSpec(shape, lambda *_: (0,) * len(shape))


def smem():
    return pl.BlockSpec(memory_space=pltpu.SMEM)


def anywhere():
    return pl.BlockSpec(memory_space=pl.ANY)


def nn(a, b):
    return lax.dot_general(a, b, (((1,), (0,)), ((), ())), preferred_element_type=F32)


def nt(a, b):
    return lax.dot_general(a, b, (((1,), (1,)), ((), ())), preferred_element_type=F32)


def tn(a, b):
    return lax.dot_general(a, b, (((0,), (0,)), ((), ())), preferred_element_type=F32)


def iota(shape, dim):
    return lax.broadcasted_iota(jnp.int32, shape, dim)


def bucket_of(offset_pos):
    distance = jnp.abs(offset_pos)
    far_bucket = jnp.full(distance.shape, 8, jnp.int32)
    for border in THRESHOLDS:
        far_bucket = far_bucket + (distance >= border).astype(jnp.int32)
    near_bucket = jnp.where(distance < 8, distance, far_bucket)
    return near_bucket + jnp.where(offset_pos > 0, 16, 0).astype(jnp.int32)


def three_parts(value):
    high = value.astype(BF16)
    rest = value - high.astype(F32)
    middle = rest.astype(BF16)
    return high, middle, (rest - middle.astype(F32)).astype(BF16)


def fill_message(out_ref, flat_ref, msg_ref, cap, depth, values=None):
    groups = flat_ref.shape[0] // cap
    parts = flat_ref.shape[1] // LANES
    for group in range(groups):
        for part in range(parts):
            first = group * depth + part * cap
            msg_ref[first : first + cap, :] = flat_ref[
                group * cap : (group + 1) * cap, part * LANES : (part + 1) * LANES
            ]
        first = group * depth + parts * cap
        msg_ref[first : (group + 1) * depth, :] = jnp.zeros(
            ((group + 1) * depth - first, LANES), F32
        )
        if values is not None:
            for part, piece in enumerate(values):
                msg_ref[first + part : first + part + 1, :] = piece[group : group + 1, :]
    out_ref[...] = msg_ref[...].astype(BF16)


def read_message(message, flat_ref, msg_ref, cap, depth):
    groups = flat_ref.shape[0] // cap
    parts = flat_ref.shape[1] // LANES
    msg_ref[...] = message.astype(F32)
    values = []
    for group in range(groups):
        for part in range(parts):
            first = group * depth + part * cap
            flat_ref[group * cap : (group + 1) * cap, part * LANES : (part + 1) * LANES] = msg_ref[
                first : first + cap, :
            ]
        first = group * depth + parts * cap
        values.append(jnp.sum(msg_ref[first : first + 3, :], axis=0, keepdims=True))
    return jnp.concatenate(values, axis=0)


def values_in(group_hot, slot_hot, value):
    return [
        nn(group_hot, jnp.where(slot_hot, piece, jnp.zeros_like(piece)))
        for piece in three_parts(value)
    ]


def values_out(group_hot, slot_hot, values):
    spread = sum(nn(group_hot, piece) for piece in three_parts(values))
    return jnp.sum(jnp.where(slot_hot, spread, 0.0), axis=1, keepdims=True)


def slot_places(count, groups, cap):
    row = iota((count, 1), 0)
    group = jnp.zeros((count, 1), jnp.int32)
    for border in range(1, groups):
        group = group + (row >= border * cap).astype(jnp.int32)
    by_row = (iota((count, groups), 1) == group).astype(BF16)
    first = iota((groups, count), 0) * cap
    place = iota((groups, count), 1)
    by_col = ((place >= first) & (place < first + cap)).astype(BF16)
    slot_hot = iota((count, LANES), 1) == row - group * cap
    return by_row, by_col, slot_hot


def message_kernel(cap, depth, rows_ref, meta_ref, later_ref, out_ref, flat, msg):
    del later_ref
    hot = (iota((flat.shape[0], rows_ref.shape[0]), 0) == meta_ref[0:1, :]).astype(BF16)
    flat[...] = nn(hot, rows_ref[...])
    fill_message(out_ref, flat, msg, cap, depth)


def rows_kernel(cap, depth, message_ref, out_ref, flat, msg):
    read_message(message_ref[...], flat, msg, cap, depth)
    out_ref[...] = flat[...].astype(BF16)


def picked_rows(columns, first, count=8):
    pick = (iota((count, LANES), 1) == iota((count, LANES), 0) + first).astype(BF16)
    return nt(pick, columns)


def qkv_kernel(experts, x_ref, wa_ref, wb_ref, hid_ref, q_ref, k_ref, v_ref, gain_ref):
    half = q_ref.shape[1]
    split = wa_ref.shape[1]
    cut = split - half
    gains = picked_rows(wb_ref[:, split - LANES :], experts)
    gain_ref[...] = gains
    tokens = x_ref[...].astype(F32)
    scale = lax.rsqrt(jnp.mean(tokens * tokens, axis=-1, keepdims=True) + EPSILON)
    hidden = (tokens * scale * gains[0:1, :]).astype(BF16)
    hid_ref[...] = hidden
    first = nn(hidden, wa_ref[...]).astype(BF16)
    second = nn(hidden, wb_ref[:, : split - LANES]).astype(BF16)
    q_ref[...] = first[:, :half]
    k_ref[:, :cut] = first[:, half:]
    k_ref[:, cut:] = second[:, : half - cut]
    v_ref[...] = second[:, half - cut :]


def bias_kernel(table_ref, later_ref, bias_ref, prev_ref, next_ref):
    del later_ref
    heads, near = bias_ref.shape[0], bias_ref.shape[2]
    wide = near + BLK
    table = table_ref[...]
    buckets = table.shape[1]
    apart = iota((buckets, wide), 1) - (wide // 2)
    ahead = nn(table, (bucket_of(apart) == iota((buckets, wide), 0)).astype(BF16))
    behind = nn(table, (bucket_of(-apart) == iota((buckets, wide), 0)).astype(BF16))
    for head in range(heads):
        row = pltpu.roll(ahead[head : head + 1, :], wide - (wide // 2 - LANES), 1)
        full = jnp.broadcast_to(row, (BLK, wide))
        full = pltpu.roll(full, 0, 1, stride=1, stride_axis=0)
        bias_ref[head] = full[:, :near].astype(BF16)
        row = behind[head : head + 1, :]
        for out_ref, ahead_by in ((prev_ref, BLK), (next_ref, -LANES)):
            moved = pltpu.roll(row, (wide // 2 + ahead_by) % wide, 1)
            full = jnp.broadcast_to(moved, (LANES, wide))
            full = pltpu.roll(full, 0, 1, stride=1, stride_axis=0)
            out_ref[head] = full[:, :BLK].astype(BF16)


def own_half(value, turn):
    lane = iota(value.shape, 1)
    keep = (lane < LANES // 2) if turn == 0 else (lane >= LANES // 2)
    return jnp.where(keep, value, jnp.zeros_like(value))


def scores_of(query, keys, bias, left, right, mask):
    raw = nt(query, keys)
    near = bias.shape[1]
    edge = (keys.shape[0] - near) // 2
    raw = jnp.concatenate(
        [
            raw[:, :edge] + left,
            raw[:, edge : edge + near] + bias.astype(F32),
            raw[:, edge + near :] + right,
        ],
        axis=1,
    )
    return jnp.where(mask, raw, NEGATIVE)


def attend_kernel(
    far_ref, q_ref, k_ref, v_ref, bias_ref, code_ref, ctx_ref, low_ref, lse_ref, lse_row_ref
):
    pair = pl.program_id(0)
    own = q_ref.shape[0]
    window = 5 * BLK
    lane = iota((BLK, LANES), 1)
    code_row = picked_rows(code_ref[...], 0)
    lse_row_ref[...] = jnp.zeros_like(lse_row_ref)
    for block in range(own // BLK):
        rows = slice(block * BLK, (block + 1) * BLK)
        cols = slice(block * BLK, block * BLK + window)
        query = q_ref[rows, :]
        keys = k_ref[cols, :]
        values = v_ref[cols, :]
        code_col = code_ref[own + block * BLK : own + (block + 1) * BLK, 0:1].astype(F32)
        mask = code_col == code_row[0:1, cols]
        outs = []
        logs = jnp.zeros((BLK, LANES), F32)
        for turn in range(2):
            head = pair * 2 + turn
            scores = scores_of(
                own_half(query, turn), keys, bias_ref[turn], far_ref[0, head], far_ref[1, head], mask
            )
            top = jnp.max(scores, axis=1, keepdims=True)
            weight = jnp.exp(scores - top)
            total = jnp.sum(weight, axis=1, keepdims=True)
            outs.append(nn((weight * (1.0 / total)).astype(BF16), values))
            logs = jnp.where(lane == turn, top + jnp.log(total), logs)
        context = jnp.where(lane < LANES // 2, outs[0], outs[1])
        ctx_ref[rows, :] = context
        low_ref[rows, :] = context.astype(BF16)
        lse_ref[rows, :] = logs
        lse_row_ref[0, 0:2, rows] = jnp.transpose(logs)[0:2, :]


def rolled_left(value, steps):
    return value if steps == 0 else pltpu.roll(value, value.shape[1] - steps, 1)


def diagonal_sums(value):
    eight = jnp.zeros((8, value.shape[1]), F32)
    for first in range(0, value.shape[0], 8):
        eight = eight + rolled_left(value[first : first + 8], first)
    one = jnp.zeros((1, value.shape[1]), F32)
    for row in range(8):
        one = one + rolled_left(eight[row : row + 1], row)
    return one


def own_backward_kernel(
    far_ref,
    q_ref,
    k_ref,
    v_ref,
    gctx_ref,
    ctx_ref,
    lse_ref,
    bias_ref,
    code_ref,
    dq_ref,
    dk_ref,
    dv_ref,
    tab_ref,
):
    pair = pl.program_id(0)
    blocks = q_ref.shape[0] // BLK
    window = 5 * BLK
    near = bias_ref.shape[2]
    edge = (window - near) // 2
    lane = iota((BLK, LANES), 1)
    own = q_ref.shape[0]
    code_row = picked_rows(code_ref[...], 0)
    dk_ref[...] = jnp.zeros_like(dk_ref)
    dv_ref[...] = jnp.zeros_like(dv_ref)
    near_sum = [jnp.zeros((BLK, near), F32), jnp.zeros((BLK, near), F32)]
    left_sum = [jnp.zeros((BLK, edge), F32), jnp.zeros((BLK, edge), F32)]
    right_sum = [jnp.zeros((BLK, edge), F32), jnp.zeros((BLK, edge), F32)]
    for block in range(blocks):
        rows = slice(block * BLK, (block + 1) * BLK)
        cols = slice(block * BLK, block * BLK + window)
        keys = k_ref[cols, :]
        values = v_ref[cols, :]
        code_col = code_ref[own + block * BLK : own + (block + 1) * BLK, 0:1].astype(F32)
        mask = code_col == code_row[0:1, cols]
        mine = slice((blocks - block) * BLK, (2 * blocks - block) * BLK)
        gctx_all = gctx_ref[rows, :]
        product = gctx_all.astype(F32) * ctx_ref[rows, :]
        logs = lse_ref[rows, :]
        outs = []
        for turn in range(2):
            head = pair * 2 + turn
            query = own_half(q_ref[rows, :], turn)
            gctx = own_half(gctx_all, turn)
            scores = scores_of(
                query, keys, bias_ref[turn], far_ref[0, head], far_ref[1, head], mask
            )
            probs = jnp.exp(scores - logs[:, turn : turn + 1])
            delta = jnp.sum(own_half(product, turn), axis=1, keepdims=True)
            grads = (probs * (nt(gctx, values) - delta)).astype(BF16)
            outs.append(nn(grads, keys))
            dk_ref[...] += tn(grads[:, mine], query)
            dv_ref[...] += tn(probs[:, mine].astype(BF16), gctx)
            wide = grads.astype(F32)
            left_sum[turn] = left_sum[turn] + wide[:, :edge]
            near_sum[turn] = near_sum[turn] + wide[:, edge : edge + near]
            right_sum[turn] = right_sum[turn] + wide[:, edge + near :]
        dq_ref[rows, :] = jnp.where(lane < LANES // 2, outs[0], outs[1]).astype(BF16)
    apart = iota((BLK, near), 1) - (2 * BLK - edge) - iota((BLK, near), 0)
    tab_lane = iota((1, LANES), 1)
    hot = (bucket_of(iota((near, LANES), 0) - LANES) == iota((near, LANES), 1)).astype(F32)
    for turn in range(2):
        total = near_sum[turn]
        left = jnp.sum(left_sum[turn]) + jnp.sum(jnp.where(apart <= -FAR, total, 0.0))
        right = jnp.sum(right_sum[turn]) + jnp.sum(jnp.where(apart >= FAR, total, 0.0))
        close = jnp.where(jnp.abs(apart) < FAR, total, 0.0)
        diagonal = diagonal_sums(close)
        sums = lax.dot_general(
            diagonal,
            hot,
            (((1,), (0,)), ((), ())),
            precision=lax.Precision.HIGHEST,
            preferred_element_type=F32,
        )
        sums = sums + jnp.where(tab_lane == 15, left, 0.0) + jnp.where(tab_lane == 31, right, 0.0)
        tab_ref[0, turn : turn + 1, :] = sums


def halo_backward_kernel(
    far_ref,
    qp_ref,
    qn_ref,
    k_ref,
    v_ref,
    gp_ref,
    gn_ref,
    lp_ref,
    ln_ref,
    deltap_ref,
    deltan_ref,
    biasp_ref,
    biasn_ref,
    code_ref,
    dka_ref,
    dva_ref,
    tab_in_ref,
    dk_ref,
    dv_ref,
    tab_ref,
):
    pair = pl.program_id(0)
    own = k_ref.shape[0]
    half = LANES
    code_row = picked_rows(code_ref[...], 0)
    tab_ref[...] = tab_in_ref[...]
    total_k = dka_ref[...]
    total_v = dva_ref[...]
    parts = []
    for side in range(2):
        q_side = qp_ref if side == 0 else qn_ref
        g_side = gp_ref if side == 0 else gn_ref
        for block in range(2):
            far_block = block == side
            rows = slice(block * BLK, (block + 1) * BLK)
            if far_block:
                cols = slice(0, BLK) if side == 0 else slice(own - BLK, own)
            else:
                cols = slice(0, own)
            parts.append((side, rows, cols, far_block, q_side, g_side))
    add_k = [jnp.zeros((BLK, LANES), F32), jnp.zeros((BLK, LANES), F32)]
    add_v = [jnp.zeros((BLK, LANES), F32), jnp.zeros((BLK, LANES), F32)]
    for side, rows, cols, far_block, q_side, g_side in parts:
        keys = k_ref[cols, :]
        values = v_ref[cols, :]
        count = cols.stop - cols.start
        lse_ref = lp_ref if side == 0 else ln_ref
        delta_ref = deltap_ref if side == 0 else deltan_ref
        code_col = code_ref[own + cols.start : own + cols.stop, 0:1].astype(F32)
        first = 2 * own * side + rows.start
        mask = code_col == code_row[0:1, first : first + BLK]
        for turn in range(2):
            head = pair * 2 + turn
            query = own_half(q_side[rows, :], turn)
            gctx = own_half(g_side[rows, :], turn)
            raw = nt(keys, query)
            far = far_ref[1 - side, head]
            if far_block:
                raw = raw + far
            elif side == 0:
                raw = jnp.concatenate(
                    [raw[:half] + biasp_ref[turn].astype(F32), raw[half:] + far], axis=0
                )
            else:
                raw = jnp.concatenate(
                    [raw[: count - half] + far, raw[count - half :] + biasn_ref[turn].astype(F32)],
                    axis=0,
                )
            scores = jnp.where(mask, raw, NEGATIVE)
            logs = lse_ref[0, turn : turn + 1, rows]
            delta = delta_ref[pl.ds(head, 1), rows]
            probs = jnp.exp(scores - logs)
            grads = (probs * (nt(values, gctx) - delta)).astype(BF16)
            got_k = nn(grads, query)
            got_v = nn(probs.astype(BF16), gctx)
            for index in range(count // BLK):
                place = (cols.start // BLK) + index
                part = slice(index * BLK, (index + 1) * BLK)
                add_k[place] = add_k[place] + got_k[part]
                add_v[place] = add_v[place] + got_v[part]
    dk_ref[...] = (total_k + jnp.concatenate(add_k, axis=0)).astype(BF16)
    dv_ref[...] = (total_v + jnp.concatenate(add_v, axis=0)).astype(BF16)


def delta_kernel(core_ref, mine_ref, came_ref, ctx_ref, gctx_ref, delta_ref):
    core = core_ref[0]
    tok = mine_ref.shape[0]
    width = mine_ref.shape[1]
    gctx_ref[pl.ds(pl.multiple_of(core * tok, tok), tok), :] = mine_ref[...]
    gctx_ref[pl.ds(pl.multiple_of((1 - core) * tok, tok), tok), :] = came_ref[...]
    product = gctx_ref[...].astype(F32) * ctx_ref[...]
    head_rows = delta_ref.shape[0]
    pick = (iota((head_rows, width), 1) // (LANES // 2) == iota((head_rows, width), 0)).astype(F32)
    delta_ref[...] = lax.dot_general(
        pick,
        product,
        (((1,), (1,)), ((), ())),
        precision=lax.Precision.HIGHEST,
        preferred_element_type=F32,
    )


def token_columns(meta_ref, probs):
    route_hot = iota(probs.shape, 1) == meta_ref[:, 1:2]
    slot_hot = iota((probs.shape[0], LANES), 1) == meta_ref[:, 2:3]
    gate = jnp.sum(jnp.where(route_hot, probs, 0.0), axis=1, keepdims=True)
    return route_hot, slot_hot, gate


def before_kernel(
    cap,
    depth,
    experts,
    core_ref,
    x_ref,
    own_ref,
    came_ref,
    wo_ref,
    small_ref,
    gain_ref,
    meta_col_ref,
    meta_row_ref,
    mid_ref,
    hid_ref,
    prob_ref,
    msg_out_ref,
    flat,
    msg,
):
    core = core_ref[0]
    tok = x_ref.shape[0]
    width = own_ref.shape[1]
    rows = pl.ds(pl.multiple_of(core * tok, tok), tok)
    own_w = wo_ref[pl.ds(pl.multiple_of(core * width, width), width), :]
    other_w = wo_ref[pl.ds(pl.multiple_of((1 - core) * width, width), width), :]
    attended = nn(own_ref[rows, :], own_w) + nn(came_ref[rows, :], other_w)
    middle = x_ref[...].astype(F32) + attended
    mid_ref[...] = middle
    scale = lax.rsqrt(jnp.mean(middle * middle, axis=-1, keepdims=True) + EPSILON)
    hidden = (middle * scale * gain_ref[1:2, :]).astype(BF16)
    hid_ref[...] = hidden
    logits = nn(hidden, small_ref[...])
    lane = iota(logits.shape, 1)
    logits = jnp.where(lane < experts, logits, NEGATIVE)
    weight = jnp.exp(logits - jnp.max(logits, axis=1, keepdims=True))
    probs = weight / jnp.sum(weight, axis=1, keepdims=True)
    prob_ref[...] = probs
    _, slot_hot, gate = token_columns(meta_col_ref, probs)
    route_rows = (iota((experts, tok), 0) == meta_row_ref[1:2, :]).astype(BF16)
    values = values_in(route_rows, slot_hot, gate)
    hot = (iota((flat.shape[0], tok), 0) == meta_row_ref[0:1, :]).astype(BF16)
    flat[...] = nn(hot, hidden)
    fill_message(msg_out_ref, flat, msg, cap, depth, values)


def gelu_parts(before):
    square = before * before
    inner = jnp.tanh(before * (GELU_A + (GELU_A * GELU_B) * square))
    half = 0.5 + 0.5 * inner
    slope = half + (before * (1.0 - inner * inner)) * (
        0.5 * GELU_A + (1.5 * GELU_A * GELU_B) * square
    )
    return before * half, slope


def expert_kernel(
    cap,
    depth,
    msg_ref,
    cot_ref,
    win_ref,
    wout_ref,
    earlier_a_ref,
    earlier_b_ref,
    rows_ref,
    grad_ref,
    act_ref,
    gbef_ref,
    made_ref,
    back_msg_ref,
    made_acc,
    back_acc,
    msg,
):
    del earlier_a_ref, earlier_b_ref
    step = pl.program_id(0)
    count = rows_ref.shape[0]
    groups = count // cap

    @pl.when(step == 0)
    def _():
        values = read_message(msg_ref[...], made_acc, msg, cap, depth)
        rows_ref[...] = made_acc[...].astype(BF16)
        by_row, _, slot_hot = slot_places(count, groups, cap)
        gate = values_out(by_row, slot_hot, values)
        grad_ref[...] = (gate * cot_ref[...].astype(F32)).astype(BF16)
        made_acc[...] = jnp.zeros_like(made_acc)
        back_acc[...] = jnp.zeros_like(back_acc)

    w_in = win_ref[0]
    w_out = wout_ref[0]
    before = nn(rows_ref[...], w_in)
    grad_active = nt(grad_ref[...], w_out)
    active, slope = gelu_parts(before)
    active = active.astype(BF16)
    grad_before = (grad_active * slope).astype(BF16)
    act_ref[...] = active
    gbef_ref[...] = grad_before
    made_acc[...] += nn(active, w_out)
    back_acc[...] += nt(grad_before, w_in)

    @pl.when(step == pl.num_programs(0) - 1)
    def _():
        produced = made_acc[...].astype(BF16)
        made_ref[...] = produced
        grad_gate = jnp.sum(
            cot_ref[...].astype(F32) * produced.astype(F32), axis=1, keepdims=True
        )
        _, by_col, slot_hot = slot_places(count, groups, cap)
        values = values_in(by_col, slot_hot, grad_gate)
        fill_message(back_msg_ref, back_acc, msg, cap, depth, values)


def spread_kernel(cap, depth, rows_ref, later_ref, out_ref, flat, msg):
    del later_ref
    flat[...] = rows_ref[...].astype(F32)
    fill_message(out_ref, flat, msg, cap, depth)


def expert_grads_kernel(
    cap,
    depth,
    rows_ref,
    grad_ref,
    act_ref,
    gbef_ref,
    msgs_ref,
    cots_ref,
    win_ref,
    wout_ref,
    din_ref,
    dout_ref,
    all_rows,
    all_grad,
    flat,
    msg,
):
    count = rows_ref.shape[0]
    size = msg.shape[0]

    @pl.when(pl.program_id(0) == 0)
    def _():
        all_rows[:count, :] = rows_ref[...]
        all_grad[:count, :] = grad_ref[...]
        by_row, _, slot_hot = slot_places(count, count // cap, cap)
        for other in range(msgs_ref.shape[0] // size):
            message = msgs_ref[other * size : (other + 1) * size, :]
            values = read_message(message, flat, msg, cap, depth)
            gate = values_out(by_row, slot_hot, values)
            first = (other + 1) * count
            all_rows[first : first + count, :] = flat[...].astype(BF16)
            cots = cots_ref[other * count : (other + 1) * count, :].astype(F32)
            all_grad[first : first + count, :] = (gate * cots).astype(BF16)

    w_in = win_ref[0]
    w_out = wout_ref[0]
    active, slope = gelu_parts(nn(all_rows[count:, :], w_in))
    grad_before = (nt(all_grad[count:, :], w_out) * slope).astype(BF16)
    actives = jnp.concatenate([act_ref[...], active.astype(BF16)], axis=0)
    grads = jnp.concatenate([gbef_ref[...], grad_before], axis=0)
    din_ref[0] = tn(all_rows[...], grads)
    dout_ref[0] = tn(actives, all_grad[...])


def sums_kernel(
    chip_rows,
    bits_ref,
    hid_ref,
    dq_ref,
    dk_ref,
    dv_ref,
    extra_ref,
    senda_ref,
    keepa_ref,
    sendb_ref,
    keepb_ref,
    total,
):
    rows = hid_ref.shape[1]
    half = dq_ref.shape[1]
    split = keepa_ref.shape[1]
    cut = split - half
    hidden = hid_ref[...]
    bit_a = bits_ref[0]
    bit_b = bits_ref[1]
    chunk = keepa_ref.shape[0]
    total[:, :half] = tn(hidden, dq_ref[...])
    total[:, half:] = tn(hidden, dk_ref[:, :cut])
    keepa_ref[...] = total[pl.ds(pl.multiple_of(bit_a * chunk, chunk), chunk), :]
    senda_ref[...] = total[pl.ds(pl.multiple_of((1 - bit_a) * chunk, chunk), chunk), :].astype(BF16)
    total[:, : half - cut] = tn(hidden, dk_ref[:, cut:])
    total[:, half - cut : split - LANES] = tn(hidden, dv_ref[...])
    total[:, split - LANES :] = extra_ref[...]
    chunk = chip_rows
    for index in range(rows // (2 * chunk)):
        first = index * 2 * chunk
        out = slice(index * chunk, (index + 1) * chunk)
        keepb_ref[out, :] = total[pl.ds(pl.multiple_of(first + bit_b * chunk, 8), chunk), :]
        gone = total[pl.ds(pl.multiple_of(first + (1 - bit_b) * chunk, 8), chunk), :]
        sendb_ref[out, :] = gone.astype(BF16)


def input_kernel(core_ref, dq_ref, dk_ref, dv_ref, wa_ref, wb_ref, later_ref, keep_ref, send_ref):
    del later_ref
    core = core_ref[0]
    half = dq_ref.shape[1]
    split = wa_ref.shape[1]
    cut = split - half
    tok = keep_ref.shape[0]
    for out_ref, which in ((send_ref, 1 - core), (keep_ref, core)):
        rows = pl.ds(pl.multiple_of(which * tok, tok), tok)
        out_ref[...] = (
            nt(dq_ref[rows, :], wa_ref[:, :half])
            + nt(dk_ref[rows, :cut], wa_ref[:, half:])
            + nt(dk_ref[rows, cut:], wb_ref[:, : half - cut])
            + nt(dv_ref[rows, :], wb_ref[:, half - cut : split - LANES])
        )


def after_kernel(
    cap,
    depth,
    experts,
    core_ref,
    msg_in_ref,
    cot_ref,
    mid_ref,
    hid_ref,
    prob_ref,
    small_ref,
    gain_ref,
    wo_ref,
    meta_ref,
    earlier_ref,
    gmid_ref,
    gmine_ref,
    gtheirs_ref,
    mine_ref,
    theirs_ref,
    sums_ref,
    flat,
    msg,
    low_scr,
):
    del earlier_ref
    core = core_ref[0]
    width = mine_ref.shape[1]
    tok = cot_ref.shape[0]
    values = read_message(msg_in_ref[...], flat, msg, cap, depth)
    hot = (iota((tok, flat.shape[0]), 1) == meta_ref[:, 0:1]).astype(BF16)
    came = nn(hot, flat[...].astype(BF16))
    probs = prob_ref[...]
    route_hot, slot_hot, gate = token_columns(meta_ref, probs)
    by_route = (iota((tok, experts), 1) == meta_ref[:, 1:2]).astype(BF16)
    grad_gate = values_out(by_route, slot_hot, values)
    grad_logits = (grad_gate * probs * (route_hot.astype(F32) - gate)).astype(BF16)
    grad_hidden = came + nt(grad_logits, small_ref[...])
    middle = mid_ref[...]
    scale = lax.rsqrt(jnp.mean(middle * middle, axis=-1, keepdims=True) + EPSILON)
    normed = middle * scale
    grad_normed = grad_hidden * gain_ref[1:2, :]
    grad_middle = cot_ref[...].astype(F32) + scale * (
        grad_normed - normed * jnp.mean(grad_normed * normed, axis=-1, keepdims=True)
    )
    gmid_ref[...] = grad_middle
    low = grad_middle.astype(BF16)
    low_scr[...] = low
    gmine_ref[...] = low_scr[:, pl.ds(pl.multiple_of(core * width, width), width)]
    gtheirs_ref[...] = low_scr[:, pl.ds(pl.multiple_of((1 - core) * width, width), width)]
    own_w = wo_ref[pl.ds(pl.multiple_of(core * width, width), width), :]
    other_w = wo_ref[pl.ds(pl.multiple_of((1 - core) * width, width), width), :]
    theirs_ref[...] = nt(low, other_w).astype(BF16)
    mine_ref[...] = nt(low, own_w).astype(BF16)
    router = tn(hid_ref[...], grad_logits)
    gain = lax.dot_general(
        grad_hidden * normed,
        jnp.ones((tok, LANES), F32),
        (((0,), (0,)), ((), ())),
        precision=lax.Precision.HIGHEST,
        preferred_element_type=F32,
    )
    lane = iota(router.shape, 1)
    sums_ref[...] = jnp.where(lane < experts, router, jnp.where(lane == experts, gain, 0.0))


def output_kernel(cap, depth, msg_in_ref, mid_ref, prob_ref, meta_ref, out_ref, flat, msg):
    tok = out_ref.shape[0]
    read_message(msg_in_ref[...], flat, msg, cap, depth)
    hot = (iota((tok, flat.shape[0]), 1) == meta_ref[:, 0:1]).astype(BF16)
    combined = nn(hot, flat[...].astype(BF16))
    _, _, gate = token_columns(meta_ref, prob_ref[...])
    out_ref[...] = (mid_ref[...] + gate * combined).astype(BF16)


class Place:
    def __init__(self):
        self.n_seq = lax.axis_size("seq")
        self.n_ctx = lax.axis_size("ctx")
        self.count = self.n_seq * self.n_ctx
        self.index = lax.axis_index("seq") * self.n_ctx + lax.axis_index("ctx")
        self.core = self.index % 2
        ctx_bits = (self.n_ctx - 1).bit_length()
        self.bits = (self.count - 1).bit_length()
        self.far_bits = list(range(ctx_bits - 1, 1, -1))
        self.near_bits = [1]
        self.seq_bits = list(range(self.bits - 1, ctx_bits - 1, -1))

    def swap(self, value, bit):
        pairs = [(i, i ^ (1 << bit)) for i in range(self.count)]
        return lax.ppermute(value, AXES, pairs)

    def bit(self, which):
        return (self.index >> which) & 1

    def shift(self, value, steps):
        pairs = []
        for row in range(self.n_seq):
            for col in range(self.n_ctx):
                if 0 <= col + steps < self.n_ctx:
                    pairs.append((row * self.n_ctx + col, row * self.n_ctx + col + steps))
        return lax.ppermute(value, AXES, pairs)

    def ordered(self, own, came, bit, axis, join):
        mine = self.bit(bit) == 1
        return join([jnp.where(mine, came, own), jnp.where(mine, own, came)], axis=axis)

    def stage(self, block, bit, done):
        axis = sum(1 for other in done if other > bit)
        return self.ordered(block, self.swap(block, bit), bit, axis, jnp.stack), done + [bit]

    def gather(self, block, order, done=()):
        done = list(done)
        for bit in order:
            block, done = self.stage(block, bit, done)
        return block.reshape((-1,) + block.shape[len(done) + 1 :])

    def scatter_on(self, gone, kept, order, first, keep):
        value = kept + self.swap(gone, first).astype(F32)
        return value, self.scatter(value, order, keep)

    def scatter(self, value, order, keep=()):
        left = sorted(list(order) + list(keep), reverse=True)
        value = value.reshape((2,) * len(left) + (-1,) + value.shape[1:])
        for bit in order:
            axis = left.index(bit)
            mine = self.bit(bit)
            gone = lax.dynamic_index_in_dim(value, 1 - mine, axis, keepdims=False).astype(BF16)
            kept = lax.dynamic_index_in_dim(value, mine, axis, keepdims=False)
            value = kept + self.swap(gone, bit).astype(F32)
            left.remove(bit)
        return value.reshape((-1,) + value.shape[-1:])

    def total(self, value):
        for bit in range(1, self.bits):
            value = value + self.swap(value, bit)
        return value


def call(
    kernel,
    outs,
    *args,
    us=2.0,
    grid=None,
    in_specs=None,
    out_specs=None,
    scratch=(),
    smem_first=False,
    mib=58,
):
    if in_specs is None:
        in_specs = [whole(a.shape) for a in args]
        if smem_first:
            in_specs[0] = smem()
    if out_specs is None:
        out_specs = [whole(o[0]) for o in outs]
    shapes = [jax.ShapeDtypeStruct(*o) for o in outs]
    return pl.pallas_call(
        kernel,
        out_shape=shapes,
        grid=grid if grid is not None else (1,),
        in_specs=in_specs,
        out_specs=out_specs,
        scratch_shapes=list(scratch),
        compiler_params=params(mib),
        cost_estimate=pl.CostEstimate(
            flops=int(us * 1.15e9), transcendentals=0, bytes_accessed=0
        ),
    )(*args)


def local(
    inputs,
    cotangent,
    gain_attn,
    w_query,
    w_key,
    w_value,
    w_output,
    bias_table,
    gain_ffn,
    w_router,
    w_in,
    w_out,
    segments,
    routes,
):
    place = Place()
    core = place.core
    core_arg = core.reshape(1).astype(jnp.int32)
    x = inputs[0]
    cot = cotangent[0]
    tok, width = x.shape
    heads = bias_table.shape[1]
    buckets = bias_table.shape[0]
    mine_heads = heads // 2
    half = width // 2
    pairs = half // LANES
    experts = w_router.shape[1]
    hidden_units = w_in.shape[2]
    rows_dev = w_query.shape[0]
    cap = max(2, (9 * tok + 8 * experts - 1) // (8 * experts))
    parts = width // LANES
    depth = -(-(parts * cap + 3) // 16) * 16
    n_ctx = place.n_ctx
    slots = n_ctx * cap
    far, near_bits, seq_bits = place.far_bits, place.near_bits, place.seq_bits
    rows_all = 6 * tok
    own_rows = 2 * tok

    wo = lax.all_gather(w_output, AXES, axis=0, tiled=True)
    small_w = jnp.concatenate(
        [
            w_router,
            gain_attn[:, None],
            gain_ffn[:, None],
            jnp.zeros((rows_dev, LANES - experts - 2), BF16),
        ],
        axis=1,
    )
    both = [
        jnp.concatenate(
            [w[:, side * half : (side + 1) * half] for w in (w_query, w_key, w_value)] + [small_w],
            axis=1,
        )
        for side in range(2)
    ]
    ours = jnp.where(core == 0, both[0], both[1])
    theirs = jnp.where(core == 0, both[1], both[0])
    block = place.ordered(ours, place.swap(theirs, 0), 0, 0, jnp.concatenate)
    done = []
    for bit in far:
        block, done = place.stage(block, bit, done)
    split = block.shape[-1] // 2
    later_a, done_a = block[..., :split], done
    for bit in near_bits:
        later_a, done_a = place.stage(later_a, bit, done_a)
    w_a = place.gather(later_a, seq_bits, done_a)
    w_b = place.gather(block[..., split:], seq_bits + near_bits, done)

    code = (segments[0] + 1).astype(BF16)
    x_ext = jnp.concatenate([x, jnp.broadcast_to(code[:, None], (tok, LANES))], axis=1)
    before_x = place.shift(x_ext, 2)
    after_x = place.shift(x_ext, -2)
    three = jnp.stack([before_x, x_ext, after_x])
    three_came = place.swap(three, 0)
    x_all = place.ordered(three, three_came, 0, 1, jnp.concatenate).reshape(
        rows_all, width + LANES
    )
    code_block = pl.BlockSpec((rows_all, LANES), lambda *_: (0, parts))

    near = 2 * BLK
    table_mine = lax.dynamic_slice_in_dim(bias_table, core * mine_heads, mine_heads, 1)
    far_bias = jnp.stack([table_mine[15], table_mine[31]]).astype(F32)
    bias, bias_prev, bias_next = call(
        bias_kernel,
        [
            ((mine_heads, BLK, near), BF16),
            ((mine_heads, LANES, BLK), BF16),
            ((mine_heads, LANES, BLK), BF16),
        ],
        jnp.pad(table_mine.T, ((0, 8 - mine_heads), (0, 0))),
        x_all,
        us=3.0,
        in_specs=[whole((8, buckets)), anywhere()],
    )

    route = routes[0, :, 0]
    route_hot = (route[:, None] == iota((tok, experts), 1)).astype(F32)
    earlier = (iota((tok, tok), 1) < iota((tok, tok), 0)).astype(F32)
    slot = jnp.sum(jnp.dot(earlier, route_hot) * route_hot, axis=1).astype(jnp.int32)
    meta = jnp.stack([route * cap + slot, route, slot])
    meta_row = jnp.pad(meta, ((0, 5), (0, 0)))
    meta_col = jnp.pad(meta.T, ((0, 0), (0, LANES - 3)))

    def exchange(message):
        message = message.reshape(n_ctx, depth, LANES)
        message = lax.all_to_all(message, "ctx", split_axis=0, concat_axis=0, tiled=True)
        return message.reshape(n_ctx * depth, LANES)

    msg_shape = (n_ctx * depth, LANES)
    msg_scratch = [VMEM((slots, width), F32), VMEM(msg_shape, F32)]

    hid_all, q_all, k_all, v_all, gains = call(
        functools.partial(qkv_kernel, experts),
        [((rows_all, width), BF16)] + [((rows_all, half), BF16)] * 3 + [((8, width), F32)],
        x_all,
        w_a,
        w_b,
        us=6.0,
        grid=(rows_all // own_rows,),
        in_specs=[
            pl.BlockSpec((own_rows, width), lambda i: (i, 0)),
            whole((width, split)),
            whole((width, split)),
        ],
        out_specs=[pl.BlockSpec((own_rows, width), lambda i: (i, 0))]
        + [pl.BlockSpec((own_rows, half), lambda i: (i, 0))] * 3
        + [whole((8, width))],
    )

    cot_msg = call(
        functools.partial(message_kernel, cap, depth),
        [(msg_shape, BF16)],
        cot,
        meta_row,
        gains,
        in_specs=[whole((tok, width)), whole((8, tok)), anywhere()],
        scratch=msg_scratch,
    )[0]
    cot_in = exchange(cot_msg)
    cot_rows = call(
        functools.partial(rows_kernel, cap, depth),
        [((slots, width), BF16)],
        cot_in,
        scratch=msg_scratch,
    )[0]

    hid_block = pl.BlockSpec((own_rows, width), lambda *_: (1, 0))
    small_block = pl.BlockSpec((width, LANES), lambda *_: (0, split // LANES - 1))

    own_block = pl.BlockSpec((own_rows, LANES), lambda p: (1, p))
    all_block = pl.BlockSpec((rows_all, LANES), lambda p: (0, p))
    out_block = pl.BlockSpec((own_rows, LANES), lambda p: (0, p))
    bias_block = pl.BlockSpec((2, BLK, near), lambda p: (p, 0, 0))
    lse_block = pl.BlockSpec((1, 8, own_rows), lambda p: (p, 0, 0))
    ctx_f, ctx_low, lse, lse_rows = call(
        attend_kernel,
        [
            ((own_rows, half), F32),
            ((own_rows, half), BF16),
            ((own_rows, half), F32),
            ((pairs, 8, own_rows), F32),
        ],
        far_bias,
        q_all,
        k_all,
        v_all,
        bias,
        x_all,
        us=12.0,
        grid=(pairs,),
        in_specs=[smem(), own_block, all_block, all_block, bias_block, code_block],
        out_specs=[out_block] * 3 + [lse_block],
    )

    ctx_came = place.swap(ctx_low, 0)
    mid, hid_two, probs, msg = call(
        functools.partial(before_kernel, cap, depth, experts),
        [
            ((tok, width), F32),
            ((tok, width), BF16),
            ((tok, LANES), F32),
            (msg_shape, BF16),
        ],
        core_arg,
        x,
        ctx_low,
        ctx_came,
        wo,
        w_b,
        gains,
        meta_col,
        meta_row,
        us=4.0,
        in_specs=[
            smem(),
            whole((tok, width)),
            whole((own_rows, half)),
            whole((own_rows, half)),
            whole((width, width)),
            small_block,
            whole((8, width)),
            whole((tok, LANES)),
            whole((8, tok)),
        ],
        scratch=msg_scratch,
    )
    msg_in = exchange(msg)
    lse_prev = place.shift(lse_rows, 2)
    lse_next = place.shift(lse_rows, -2)

    fblk = 512
    win_block = pl.BlockSpec((1, width, fblk), lambda i: (0, 0, i))
    wout_block = pl.BlockSpec((1, fblk, width), lambda i: (0, i, 0))
    act_block = pl.BlockSpec((slots, fblk), lambda i: (0, i))
    e_rows, e_grad, e_act, e_gbef, made, back_msg = call(
        functools.partial(expert_kernel, cap, depth),
        [((slots, width), BF16)] * 2
        + [((slots, hidden_units), BF16)] * 2
        + [((slots, width), BF16), (msg_shape, BF16)],
        msg_in,
        cot_rows,
        w_in,
        w_out,
        lse_prev,
        lse_next,
        us=12.0,
        grid=(hidden_units // fblk,),
        in_specs=[
            whole(msg_shape),
            whole((slots, width)),
            win_block,
            wout_block,
            anywhere(),
            anywhere(),
        ],
        out_specs=[whole((slots, width))] * 2
        + [act_block] * 2
        + [whole((slots, width)), whole(msg_shape)],
        scratch=[VMEM((slots, width), F32)] + msg_scratch,
    )
    back_in = exchange(back_msg)

    def from_others(value):
        total = value
        for bit in seq_bits:
            total = jnp.concatenate([total, place.swap(total, bit)], axis=0)
        return total[value.shape[0] :]

    if place.n_seq == 2:
        msgs = place.swap(msg_in, seq_bits[0])
        cots = place.swap(cot_rows, seq_bits[0])
    else:
        msgs = from_others(msg_in)
        cots = from_others(cot_rows)
    all_slots = place.n_seq * slots
    grad_w_in, grad_w_out = call(
        functools.partial(expert_grads_kernel, cap, depth),
        [(w_in.shape, F32), (w_out.shape, F32)],
        e_rows,
        e_grad,
        e_act,
        e_gbef,
        msgs,
        cots,
        w_in,
        w_out,
        us=16.0,
        grid=(hidden_units // fblk,),
        in_specs=[
            whole((slots, width)),
            whole((slots, width)),
            act_block,
            act_block,
            whole(msgs.shape),
            whole(cots.shape),
            win_block,
            wout_block,
        ],
        out_specs=[win_block, wout_block],
        scratch=[VMEM((all_slots, width), BF16), VMEM((all_slots, width), BF16)] + msg_scratch,
    )

    grad_mid, gattn_mine, gattn_theirs, gctx_mine, gctx_theirs, extra = call(
        functools.partial(after_kernel, cap, depth, experts),
        [((tok, width), F32)] + [((tok, half), BF16)] * 4 + [((width, LANES), F32)],
        core_arg,
        back_in,
        cot,
        mid,
        hid_two,
        probs,
        w_b,
        gains,
        wo,
        meta_col,
        grad_w_out,
        us=5.0,
        in_specs=[
            smem(),
            whole(msg_shape),
            whole((tok, width)),
            whole((tok, width)),
            whole((tok, width)),
            whole((tok, LANES)),
            small_block,
            whole((8, width)),
            whole((width, width)),
            whole((tok, LANES)),
            anywhere(),
        ],
        scratch=msg_scratch + [VMEM((tok, width), BF16)],
    )

    gctx_came = place.swap(gctx_theirs, 0)
    gctx, delta = call(
        delta_kernel,
        [((own_rows, half), BF16), ((8, own_rows), F32)],
        core_arg,
        gctx_mine,
        gctx_came,
        ctx_f,
        us=2.0,
        smem_first=True,
    )
    gctx_prev = place.shift(gctx, 2)
    gctx_next = place.shift(gctx, -2)
    delta_prev = place.shift(delta, 2)
    delta_next = place.shift(delta, -2)

    dq, dk_own, dv_own, tab = call(
        own_backward_kernel,
        [
            ((own_rows, half), BF16),
            ((own_rows, half), F32),
            ((own_rows, half), F32),
            ((pairs, 8, LANES), F32),
        ],
        far_bias,
        q_all,
        k_all,
        v_all,
        gctx,
        ctx_f,
        lse,
        bias,
        x_all,
        us=15.0,
        grid=(pairs,),
        in_specs=[
            smem(),
            own_block,
            all_block,
            all_block,
            out_block,
            out_block,
            out_block,
            bias_block,
            code_block,
        ],
        out_specs=[out_block] * 3 + [pl.BlockSpec((1, 8, LANES), lambda p: (p, 0, 0))],
    )

    delta_block = whole((8, own_rows))
    halo_bias = pl.BlockSpec((2, LANES, BLK), lambda p: (p, 0, 0))
    tab_block = pl.BlockSpec((1, 8, LANES), lambda p: (p, 0, 0))
    dk, dv, tab = call(
        halo_backward_kernel,
        [((own_rows, half), BF16)] * 2 + [((pairs, 8, LANES), F32)],
        far_bias,
        q_all,
        q_all,
        k_all,
        v_all,
        gctx_prev,
        gctx_next,
        lse_prev,
        lse_next,
        delta_prev,
        delta_next,
        bias_prev,
        bias_next,
        x_all,
        dk_own,
        dv_own,
        tab,
        us=9.0,
        grid=(pairs,),
        in_specs=[
            smem(),
            pl.BlockSpec((own_rows, LANES), lambda p: (0, p)),
            pl.BlockSpec((own_rows, LANES), lambda p: (2, p)),
            own_block,
            own_block,
            out_block,
            out_block,
            lse_block,
            lse_block,
            delta_block,
            delta_block,
            halo_bias,
            halo_bias,
            code_block,
            out_block,
            out_block,
            tab_block,
        ],
        out_specs=[out_block] * 2 + [tab_block],
    )

    ga_cols = place.ordered(gattn_mine, place.swap(gattn_theirs, 0), 0, 0, jnp.concatenate)
    ctx_full = place.ordered(ctx_low, ctx_came, 0, 1, jnp.concatenate)
    back_far = far[::-1]
    head_bits = seq_bits + near_bits
    sum_o = place.scatter(tn(ctx_full, ga_cols), head_bits, back_far)
    chip_rows = 2 * rows_dev
    order_a = seq_bits + near_bits
    order_b = near_bits + seq_bits
    if chip_rows % 16 == 0:
        bits = jnp.stack([place.bit(order_a[0]), place.bit(order_b[0])]).astype(jnp.int32)
        gone_a, kept_a, gone_b, kept_b = call(
            functools.partial(sums_kernel, chip_rows),
            [
                ((width // 2, split), BF16),
                ((width // 2, split), F32),
                ((width // 2, split), BF16),
                ((width // 2, split), F32),
            ],
            bits,
            hid_all,
            dq,
            dk,
            dv,
            extra,
            us=4.0,
            in_specs=[
                smem(),
                hid_block,
                whole((own_rows, half)),
                whole((own_rows, half)),
                whole((own_rows, half)),
                whole((width, LANES)),
            ],
            scratch=[VMEM((width, split), F32)],
        )
        soon = gone_a
        later, sum_a = place.scatter_on(gone_a, kept_a, order_a[1:], order_a[0], back_far)
        _, sum_b = place.scatter_on(gone_b, kept_b, order_b[1:], order_b[0], back_far)
    else:
        hid_one = hid_all[own_rows : 2 * own_rows]
        cut = split - half
        total_a = tn(hid_one, jnp.concatenate([dq, dk[:, :cut]], axis=1))
        total_b = tn(hid_one, jnp.concatenate([dk[:, cut:], dv], axis=1))
        soon = later = total_a
        sum_a = place.scatter(total_a, order_a, back_far)
        sum_b = place.scatter(jnp.concatenate([total_b, extra], axis=1), order_b, back_far)
    sums = place.scatter(jnp.concatenate([sum_a, sum_b, sum_o], axis=1), back_far)
    sums = sums.reshape(2, rows_dev, sums.shape[1])
    gone = lax.dynamic_index_in_dim(sums, 1 - core, 0, keepdims=False)
    kept = lax.dynamic_index_in_dim(sums, core, 0, keepdims=False)
    came = place.swap(gone, 0)

    def columns(first):
        return place.ordered(
            kept[:, first : first + half], came[:, first : first + half], 0, 1, jnp.concatenate
        )

    sum_q, sum_k, sum_v = columns(0), columns(half), columns(2 * half)
    sum_out = columns(3 * half + LANES)
    extra_sum = kept[:, 3 * half : 3 * half + LANES] + came[:, 3 * half : 3 * half + LANES]
    grad_router = extra_sum[:, :experts]
    grad_gain_two = extra_sum[:, experts]
    weighted = (
        sum_q * w_query.astype(F32) + sum_k * w_key.astype(F32) + sum_v * w_value.astype(F32)
    )
    grad_gain_one = jnp.sum(weighted, axis=1) / gain_attn.astype(F32)

    part, part_gone = call(
        input_kernel,
        [((tok, width), F32), ((tok, width), F32)],
        core_arg,
        dq,
        dk,
        dv,
        w_a,
        w_b,
        later,
        us=4.0,
        in_specs=[smem()]
        + [whole((own_rows, half))] * 3
        + [whole((width, split))] * 2
        + [anywhere()],
    )
    grad_hidden = part + place.swap(part_gone, 0)
    tokens = x.astype(F32)
    scale_one = lax.rsqrt(jnp.mean(tokens * tokens, axis=-1, keepdims=True) + EPSILON)
    normed_one = tokens * scale_one
    grad_normed = grad_hidden * gains[0:1]
    grad_tokens = grad_mid + scale_one * (
        grad_normed - normed_one * jnp.mean(grad_normed * normed_one, axis=-1, keepdims=True)
    )

    made_msg = call(
        functools.partial(spread_kernel, cap, depth),
        [(msg_shape, BF16)],
        made,
        soon,
        in_specs=[whole((slots, width)), anywhere()],
        scratch=msg_scratch,
    )[0]
    made_in = exchange(made_msg)
    output = call(
        functools.partial(output_kernel, cap, depth),
        [((tok, width), BF16)],
        made_in,
        mid,
        probs,
        meta_col,
        scratch=msg_scratch,
    )[0]

    table = place.total(tab[:, :2].reshape(mine_heads, LANES))
    table = place.ordered(table, place.swap(table, 0), 0, 0, jnp.concatenate)
    table_sum = table[:, :buckets].T

    return (
        output[None],
        grad_tokens.astype(BF16)[None],
        grad_gain_one,
        sum_q,
        sum_k,
        sum_v,
        sum_out,
        table_sum,
        grad_gain_two,
        grad_router,
        grad_w_in,
        grad_w_out,
    )


def solution(mesh):
    rows = P(("seq", "ctx"), None)
    flat = P(("seq", "ctx"))
    tokens = P("seq", "ctx", None)
    expert = P("ctx", None, None)
    return jax.shard_map(
        local,
        mesh=mesh,
        in_specs=(
            tokens,
            tokens,
            flat,
            rows,
            rows,
            rows,
            rows,
            P(),
            flat,
            rows,
            expert,
            expert,
            P("seq", "ctx"),
            tokens,
        ),
        out_specs=(
            tokens,
            tokens,
            flat,
            rows,
            rows,
            rows,
            rows,
            P(),
            flat,
            rows,
            expert,
            expert,
        ),
        check_vma=False,
    )
```

```python
import functools

import jax
import jax.numpy as jnp
from jax import lax
from jax.experimental import pallas as pl
from jax.experimental.pallas import tpu as pltpu
from jax.sharding import PartitionSpec as P

EPSILON = 1e-06
NEGATIVE = -1e30
THRESHOLDS = (12, 16, 23, 32, 46, 64, 91)
AXES = ("seq", "ctx")
BLK = 256
LANES = 128
FAR = 91
CHUNK = 32
TABLE = 32
CODE_ROWS = 16
GELU_A = 0.7978845608028654
GELU_B = 0.044715

BF16 = jnp.bfloat16
F32 = jnp.float32
VMEM = pltpu.VMEM


def params(mib=48):
    return pltpu.CompilerParams(vmem_limit_bytes=mib * 1024 * 1024)


def whole(shape):
    return pl.BlockSpec(shape, lambda *_: (0,) * len(shape))


def smem():
    return pl.BlockSpec(memory_space=pltpu.SMEM)


def anywhere():
    return pl.BlockSpec(memory_space=pl.ANY)


def nn(a, b):
    return lax.dot_general(a, b, (((1,), (0,)), ((), ())), preferred_element_type=F32)


def nt(a, b):
    return lax.dot_general(a, b, (((1,), (1,)), ((), ())), preferred_element_type=F32)


def tn(a, b):
    return lax.dot_general(a, b, (((0,), (0,)), ((), ())), preferred_element_type=F32)


def iota(shape, dim):
    return lax.broadcasted_iota(jnp.int32, shape, dim)


def bucket_of(offset_pos):
    distance = jnp.abs(offset_pos)
    far_bucket = jnp.full(distance.shape, 8, jnp.int32)
    for border in THRESHOLDS:
        far_bucket = far_bucket + (distance >= border).astype(jnp.int32)
    near_bucket = jnp.where(distance < 8, distance, far_bucket)
    return near_bucket + jnp.where(offset_pos > 0, 16, 0).astype(jnp.int32)


def three_parts(value):
    high = value.astype(BF16)
    rest = value - high.astype(F32)
    middle = rest.astype(BF16)
    return high, middle, (rest - middle.astype(F32)).astype(BF16)


def fill_message(out_ref, flat_ref, msg_ref, cap, depth, values=None, turn=0, turns=1):
    groups = flat_ref.shape[0] // cap
    parts = flat_ref.shape[1] // LANES
    for group in range(groups):
        for part in range(parts):
            first = group * depth + part * cap
            msg_ref[first : first + cap, :] = flat_ref[
                group * cap : (group + 1) * cap, part * LANES : (part + 1) * LANES
            ]
        first = group * depth + parts * cap
        msg_ref[first : (group + 1) * depth, :] = jnp.zeros(
            ((group + 1) * depth - first, LANES), F32
        )
        if values is not None:
            for part, piece in enumerate(values):
                msg_ref[first + part : first + part + 1, :] = piece[group : group + 1, :]
    if turns == 1:
        out_ref[...] = msg_ref[...].astype(BF16)
        return
    for group in range(groups):
        first = (group * turns + turn) * depth
        out_ref[first : first + depth, :] = msg_ref[
            group * depth : (group + 1) * depth, :
        ].astype(BF16)


def read_message(message_ref, flat_ref, msg_ref, cap, depth, turn=0, turns=1, start=0):
    groups = flat_ref.shape[0] // cap
    parts = flat_ref.shape[1] // LANES
    for group in range(groups):
        first = start + (group * turns + turn) * depth
        msg_ref[group * depth : (group + 1) * depth, :] = message_ref[
            first : first + depth, :
        ].astype(F32)
    values = []
    for group in range(groups):
        for part in range(parts):
            first = group * depth + part * cap
            flat_ref[group * cap : (group + 1) * cap, part * LANES : (part + 1) * LANES] = msg_ref[
                first : first + cap, :
            ]
        first = group * depth + parts * cap
        values.append(jnp.sum(msg_ref[first : first + 3, :], axis=0, keepdims=True))
    return jnp.concatenate(values, axis=0)


def values_in(group_hot, slot_hot, value):
    return [
        nn(group_hot, jnp.where(slot_hot, piece, jnp.zeros_like(piece)))
        for piece in three_parts(value)
    ]


def values_out(group_hot, slot_hot, values):
    spread = sum(nn(group_hot, piece) for piece in three_parts(values))
    return jnp.sum(jnp.where(slot_hot, spread, 0.0), axis=1, keepdims=True)


def slot_places(count, groups, cap):
    row = iota((count, 1), 0)
    group = jnp.zeros((count, 1), jnp.int32)
    for border in range(1, groups):
        group = group + (row >= border * cap).astype(jnp.int32)
    by_row = (iota((count, groups), 1) == group).astype(BF16)
    first = iota((groups, count), 0) * cap
    place = iota((groups, count), 1)
    by_col = ((place >= first) & (place < first + cap)).astype(BF16)
    slot_hot = iota((count, LANES), 1) == row - group * cap
    return by_row, by_col, slot_hot


def message_kernel(cap, depth, rows_ref, meta_ref, later_ref, out_ref, flat, msg):
    del later_ref
    hot = (iota((flat.shape[0], rows_ref.shape[0]), 0) == meta_ref[0:1, :]).astype(BF16)
    flat[...] = nn(hot, rows_ref[...])
    fill_message(out_ref, flat, msg, cap, depth)


def rows_kernel(cap, depth, message_ref, out_ref, flat, msg):
    read_message(message_ref, flat, msg, cap, depth)
    out_ref[...] = flat[...].astype(BF16)


def picked_rows(columns, first, count=8):
    pick = (iota((count, LANES), 1) == iota((count, LANES), 0) + first).astype(BF16)
    return nt(pick, columns)


def extend_kernel(x_ref, seg_ref, out_ref):
    tok, width = x_ref.shape
    out_ref[:tok, :] = x_ref[...]
    code = (seg_ref[...] + 1).astype(F32)
    code = jnp.concatenate([code, jnp.zeros((1, width - tok), F32)], axis=1)
    out_ref[tok:, :] = jnp.broadcast_to(code, (CODE_ROWS, width)).astype(BF16)


def arrange_kernel(where_ref, *refs):
    count = len(refs) - 8
    pieces, (before_ref, own_ref, after_ref) = refs[:count], refs[count : count + 3]
    a_ref, b_ref, o_ref, three_ref = refs[count + 4 :]
    rows, split = pieces[0].shape[0], a_ref.shape[1]
    for other, ref in enumerate(pieces):
        place = pl.ds(pl.multiple_of((where_ref[5] ^ other) * rows, 16), rows)
        a_ref[place, :] = ref[:, :split]
        b_ref[place, :] = ref[:, split : 2 * split]
        o_ref[place, :] = ref[:, 2 * split :]
    tok = own_ref.shape[0]
    for place, ref in enumerate((before_ref, own_ref, after_ref)):
        three_ref[place * tok : (place + 1) * tok, :] = ref[...]


def stack_kernel(before_ref, own_ref, after_ref, out_ref):
    tok = own_ref.shape[0]
    for place, ref in enumerate((before_ref, own_ref, after_ref)):
        out_ref[place * tok : (place + 1) * tok, :] = ref[...]


def prepare_kernel(
    cap,
    experts,
    where_ref,
    table_ref,
    route_col_ref,
    route_row_ref,
    bias_ref,
    prev_ref,
    next_ref,
    far_ref,
    col_ref,
    row_ref,
):
    own_heads = bias_ref.shape[0]
    pick = iota((8, 2 * own_heads), 1) == iota((8, 2 * own_heads), 0) + where_ref[0] * own_heads
    table = nt(pick.astype(BF16), table_ref[...])
    far_ref[...] = jnp.concatenate(
        [table, jnp.zeros((8, LANES - table.shape[1]), F32)], axis=1
    )
    fill_bias(table.astype(BF16), bias_ref, prev_ref, next_ref)
    tok = route_col_ref.shape[0]
    route_col = route_col_ref[...]
    route_row = route_row_ref[...]
    hot_col = route_col == iota((tok, LANES), 1)
    earlier = (iota((tok, tok), 1) < iota((tok, tok), 0)).astype(BF16)
    count = nn(earlier, hot_col.astype(F32).astype(BF16))
    slot_col = jnp.sum(jnp.where(hot_col, count, 0.0), axis=1, keepdims=True).astype(jnp.int32)
    lane = iota((tok, LANES), 1)
    col_ref[...] = jnp.where(
        lane == 0,
        route_col * cap + slot_col,
        jnp.where(lane == 1, route_col, jnp.where(lane == 2, slot_col, 0)),
    )
    hot_row = iota((experts, tok), 0) == route_row
    later = (iota((tok, tok), 0) < iota((tok, tok), 1)).astype(BF16)
    count = nn(hot_row.astype(F32).astype(BF16), later)
    slot_row = jnp.sum(jnp.where(hot_row, count, 0.0), axis=0, keepdims=True).astype(jnp.int32)
    line = iota((8, tok), 0)
    row_ref[...] = jnp.where(
        line == 0,
        route_row * cap + slot_row,
        jnp.where(line == 1, route_row, jnp.where(line == 2, slot_row, 0)),
    )


def fill_bias(table, bias_ref, prev_ref, next_ref):
    heads, near = bias_ref.shape[0], bias_ref.shape[2]
    wide = near + BLK
    buckets = table.shape[1]
    apart = iota((buckets, wide), 1) - (wide // 2)
    ahead = nn(table, (bucket_of(apart) == iota((buckets, wide), 0)).astype(BF16))
    behind = nn(table, (bucket_of(-apart) == iota((buckets, wide), 0)).astype(BF16))
    for head in range(heads):
        row = pltpu.roll(ahead[head : head + 1, :], wide - (wide // 2 - LANES), 1)
        full = jnp.broadcast_to(row, (BLK, wide))
        full = pltpu.roll(full, 0, 1, stride=1, stride_axis=0)
        bias_ref[head] = full[:, :near].astype(BF16)
        row = behind[head : head + 1, :]
        for out_ref, ahead_by in ((prev_ref, BLK), (next_ref, -LANES)):
            moved = pltpu.roll(row, (wide // 2 + ahead_by) % wide, 1)
            full = jnp.broadcast_to(moved, (LANES, wide))
            full = pltpu.roll(full, 0, 1, stride=1, stride_axis=0)
            out_ref[head] = full[:, :BLK].astype(BF16)


def own_half(value, turn):
    lane = iota(value.shape, 1)
    keep = (lane < LANES // 2) if turn == 0 else (lane >= LANES // 2)
    return jnp.where(keep, value, jnp.zeros_like(value))


def masked_scores(raw, bias, left, right, mask):
    near = bias.shape[1]
    edge = (raw.shape[1] - near) // 2
    added = jnp.concatenate(
        [
            raw[:, :edge] + left,
            raw[:, edge : edge + near] + bias.astype(F32),
            raw[:, edge + near :] + right,
        ],
        axis=1,
    )
    return jnp.where(mask, added, NEGATIVE)


def join_weights(chip_rows, bits_ref, pieces, wa_ref, wb_ref):
    if len(pieces) == 2:
        wa_ref[...] = pieces[0][...]
        wb_ref[...] = pieces[1][...]
        return
    rows = pieces[0].shape[0]
    for turn in range(2):
        place = bits_ref[1] if turn == 0 else 1 - bits_ref[1]
        wa_ref[pl.ds(pl.multiple_of(place * rows, rows), rows), :] = pieces[turn][...]
        place = bits_ref[2] if turn == 0 else 1 - bits_ref[2]
        for group in range(rows // chip_rows):
            first = pl.multiple_of(group * 2 * chip_rows + place * chip_rows, 16)
            wb_ref[pl.ds(first, chip_rows), :] = pieces[2 + turn][
                group * chip_rows : (group + 1) * chip_rows, :
            ]


def forward_kernel(experts, chip_rows, count, far_ref, where_ref, *refs):
    forward_body(experts, chip_rows, far_ref, where_ref, refs[:count], *refs[count:])


def forward_body(
    experts,
    chip_rows,
    far_ref,
    where_ref,
    pieces,
    x_ref,
    came_ref,
    code_own_ref,
    code_came_ref,
    bias_ref,
    earlier_ref,
    hid_ref,
    q_ref,
    k_ref,
    v_ref,
    gain_ref,
    low_ref,
    lse_ref,
    wa_ref,
    wb_ref,
    code_ref,
    q_all,
    k_all,
    v_all,
    code_row,
    raw,
    prob,
):
    del earlier_ref
    step = pl.program_id(0)
    own, half = q_ref.shape
    split = wa_ref.shape[1]
    cut = split - half
    core = where_ref[0]
    tok = x_ref.shape[0] - CODE_ROWS

    @pl.when(step == 0)
    def _():
        join_weights(chip_rows, where_ref, pieces, wa_ref, wb_ref)
        for chip in range(3):
            for ref, which in ((code_own_ref, core), (code_came_ref, 1 - core)):
                first = pl.multiple_of(chip * own + which * tok, tok)
                row = chip * (tok + CODE_ROWS) + tok
                pick = (iota((CODE_ROWS, LANES), 0) == 0).astype(BF16)
                code_ref[pl.ds(first, tok), :] = tn(ref[row : row + CODE_ROWS, :], pick).astype(BF16)
        gain_ref[...] = picked_rows(wb_ref[:, split - LANES :], experts)
        code_row[...] = picked_rows(code_ref[...], 0)

    @pl.when(step < 3)
    def _():
        for ref, which in ((x_ref, core), (came_ref, 1 - core)):
            tokens = ref[:tok, :].astype(F32)
            scale = lax.rsqrt(jnp.mean(tokens * tokens, axis=-1, keepdims=True) + EPSILON)
            hid_ref[pl.ds(pl.multiple_of(which * tok, tok), tok), :] = (
                tokens * scale * gain_ref[0:1, :]
            ).astype(BF16)
        hidden = hid_ref[...]
        second = nn(hidden, wb_ref[:, : split - LANES]).astype(BF16)
        k_ref[:, :cut] = nn(hidden, wa_ref[:, half:]).astype(BF16)
        k_ref[:, cut:] = second[:, : half - cut]
        v_ref[...] = second[:, half - cut :]
        rows = pl.ds(pl.multiple_of(step * own, own), own)
        k_all[rows, :] = k_ref[...]
        v_all[rows, :] = v_ref[...]

        @pl.when(step == 1)
        def _():
            query = nn(hidden, wa_ref[:, :half]).astype(BF16)
            q_ref[...] = query
            q_all[...] = query

    @pl.when(step >= 3)
    def _():
        pair = step - 3
        lanes = pl.ds(pl.multiple_of(pair * LANES, LANES), LANES)
        window = 5 * BLK
        lane = iota((BLK, LANES), 1)
        lse_ref[...] = jnp.zeros_like(lse_ref)
        for block in range(own // BLK):
            rows = slice(block * BLK, (block + 1) * BLK)
            cols = slice(block * BLK, block * BLK + window)
            query = q_all[rows, lanes]
            keys = k_all[cols, lanes]
            values = v_all[cols, lanes]
            outs = []
            for turn in range(2):
                raw[turn] = nt(own_half(query, turn), keys)
            logs = jnp.zeros((BLK, LANES), F32)
            for turn in range(2):
                head = pair * 2 + turn
                found = []
                for first in range(0, BLK, CHUNK):
                    part = slice(first, first + CHUNK)
                    here = own + block * BLK + first
                    mask = code_ref[here : here + CHUNK, 0:1].astype(F32) == code_row[0:1, cols]
                    scores = masked_scores(
                        raw[turn, part, :],
                        bias_ref[turn, part, :],
                        far_ref[pl.ds(head, 1), 15:16],
                        far_ref[pl.ds(head, 1), 31:32],
                        mask,
                    )
                    top = jnp.max(scores, axis=1, keepdims=True)
                    weight = jnp.exp(scores - top)
                    total = jnp.sum(weight, axis=1, keepdims=True)
                    prob[turn, part, :] = (weight * (1.0 / total)).astype(BF16)
                    found.append(top + jnp.log(total))
                outs.append(nn(prob[turn], values))
                logs = jnp.where(lane == turn, jnp.concatenate(found, axis=0), logs)
            low_ref[rows, :] = jnp.where(lane < LANES // 2, outs[0], outs[1]).astype(BF16)
            lse_ref[0, 0:2, rows] = jnp.transpose(logs)[0:2, :]


def halo_query_kernel(hid_ref, wa_ref, q_ref):
    q_ref[...] = nn(hid_ref[...], wa_ref[:, : q_ref.shape[1]]).astype(BF16)


def turned(rows):
    parts = jnp.concatenate([piece.astype(F32) for piece in three_parts(rows)], axis=0)
    pick = iota((3 * rows.shape[0], LANES), 0) % rows.shape[0] == iota(
        (3 * rows.shape[0], LANES), 1
    )
    return tn(parts.astype(BF16), pick.astype(BF16))


def delta_rows(parts):
    parts = parts.astype(F32)
    return parts[0:8] + parts[8:16] + parts[16:24]


def rolled_left(value, steps):
    return value if steps == 0 else pltpu.roll(value, value.shape[1] - steps, 1)


def diagonal_sums(value):
    eight = jnp.zeros((8, value.shape[1]), F32)
    for first in range(0, value.shape[0], 8):
        eight = eight + rolled_left(value[first : first + 8], first)
    one = jnp.zeros((1, value.shape[1]), F32)
    for row in range(8):
        one = one + rolled_left(eight[row : row + 1], row)
    return one


def own_backward_kernel(
    far_ref,
    q_ref,
    k_ref,
    v_ref,
    msg_ref,
    lse_ref,
    bias_ref,
    code_ref,
    dq_ref,
    dk_ref,
    dv_ref,
    tab_ref,
    raw,
    grown,
    prob,
    grads,
    near_sum,
):
    pair = pl.program_id(0)
    own = q_ref.shape[0]
    blocks = own // BLK
    deep = msg_ref.shape[0] // blocks
    window = 5 * BLK
    near = bias_ref.shape[2]
    edge = (window - near) // 2
    lanes = pl.ds(pl.multiple_of(pair * LANES, LANES), LANES)
    lane = iota((BLK, LANES), 1)
    code_row = picked_rows(code_ref[...], 0)
    dk_ref[...] = jnp.zeros_like(dk_ref)
    dv_ref[...] = jnp.zeros_like(dv_ref)
    side = iota((window, LANES), 0)
    side_lane = iota((window, LANES), 1)
    ends = ((side < edge) & (side_lane == 0)) | ((side >= edge + near) & (side_lane == 1))
    ends = ends.astype(BF16)
    end_sums = [jnp.zeros((1, LANES), F32), jnp.zeros((1, LANES), F32)]
    for block in range(blocks):
        rows = slice(block * BLK, (block + 1) * BLK)
        cols = slice(block * BLK, block * BLK + window)
        keys = k_ref[cols, :]
        values = v_ref[cols, :]
        keys_ends = jnp.concatenate([keys, ends], axis=1)
        mine = slice((blocks - block) * BLK, (2 * blocks - block) * BLK)
        first = block * deep
        gctx_all = msg_ref[first : first + BLK, lanes]
        deltas = turned(delta_rows(msg_ref[first + BLK : first + BLK + 24, :BLK]))
        logs = turned(lse_ref[0, :, rows])
        outs = []
        for turn in range(2):
            raw[turn] = nt(own_half(q_ref[rows, :], turn), keys)
            grown[turn] = nt(own_half(gctx_all, turn), values)
        for turn in range(2):
            head = pair * 2 + turn
            delta = jnp.sum(jnp.where(lane == head, deltas, 0.0), axis=1, keepdims=True)
            log = logs[:, turn : turn + 1]
            for start in range(0, BLK, CHUNK):
                part = slice(start, start + CHUNK)
                here = own + block * BLK + start
                mask = code_ref[here : here + CHUNK, 0:1].astype(F32) == code_row[0:1, cols]
                scores = masked_scores(
                    raw[turn, part, :],
                    bias_ref[turn, part, :],
                    far_ref[pl.ds(head, 1), 15:16],
                    far_ref[pl.ds(head, 1), 31:32],
                    mask,
                )
                probs = jnp.exp(scores - log[part])
                low = (probs * (grown[turn, part, :] - delta[part])).astype(BF16)
                prob[turn, part, :] = probs.astype(BF16)
                grads[turn, part, :] = low
                wide = low[:, edge : edge + near].astype(F32)
                if block == 0:
                    near_sum[turn, part, :] = wide
                else:
                    near_sum[turn, part, :] += wide
        for turn in range(2):
            query = own_half(q_ref[rows, :], turn)
            gctx = own_half(gctx_all, turn)
            both = nn(grads[turn], keys_ends)
            outs.append(both[:, :LANES])
            end_sums[turn] = end_sums[turn] + jnp.sum(both[:, LANES:], axis=0, keepdims=True)
            dk_ref[...] += tn(grads[turn, :, mine], query)
            dv_ref[...] += tn(prob[turn, :, mine], gctx)
        dq_ref[rows, :] = jnp.where(lane < LANES // 2, outs[0], outs[1]).astype(BF16)
    apart = iota((BLK, near), 1) - (2 * BLK - edge) - iota((BLK, near), 0)
    tab_lane = iota((1, LANES), 1)
    hot = (bucket_of(iota((near, LANES), 0) - LANES) == iota((near, LANES), 1)).astype(F32)
    for turn in range(2):
        total = near_sum[turn]
        left = end_sums[turn][:, 0:1] + jnp.sum(jnp.where(apart <= -FAR, total, 0.0))
        right = end_sums[turn][:, 1:2] + jnp.sum(jnp.where(apart >= FAR, total, 0.0))
        close = jnp.where(jnp.abs(apart) < FAR, total, 0.0)
        diagonal = diagonal_sums(close)
        sums = lax.dot_general(
            diagonal,
            hot,
            (((1,), (0,)), ((), ())),
            precision=lax.Precision.HIGHEST,
            preferred_element_type=F32,
        )
        sums = sums + jnp.where(tab_lane == 15, left, 0.0) + jnp.where(tab_lane == 31, right, 0.0)
        tab_ref[0, turn : turn + 1, :] = sums


def halo_backward_kernel(
    far_ref,
    qp_ref,
    qn_ref,
    k_ref,
    v_ref,
    gp_ref,
    gn_ref,
    lp_ref,
    ln_ref,
    biasp_ref,
    biasn_ref,
    code_ref,
    dka_ref,
    dva_ref,
    dk_ref,
    dv_ref,
    delta_ref,
):
    pair = pl.program_id(0)
    own = k_ref.shape[0]
    half = LANES
    code_row = picked_rows(code_ref[...], 0)
    lanes = pl.ds(pl.multiple_of(pair * LANES, LANES), LANES)
    deep = gp_ref.shape[0] // 2
    for side, g_side in enumerate((gp_ref, gn_ref)):
        for block in range(2):
            first = block * deep + BLK
            delta_ref[side, :, block * BLK : (block + 1) * BLK] = delta_rows(
                g_side[first : first + 24, :BLK]
            )
    total_k = dka_ref[...]
    total_v = dva_ref[...]
    parts = []
    for side in range(2):
        q_side = qp_ref if side == 0 else qn_ref
        g_side = gp_ref if side == 0 else gn_ref
        for block in range(2):
            far_block = block == side
            rows = slice(block * BLK, (block + 1) * BLK)
            if far_block:
                cols = slice(0, BLK) if side == 0 else slice(own - BLK, own)
            else:
                cols = slice(0, own)
            parts.append((side, rows, cols, far_block, q_side, g_side))
    add_k = [jnp.zeros((BLK, LANES), F32), jnp.zeros((BLK, LANES), F32)]
    add_v = [jnp.zeros((BLK, LANES), F32), jnp.zeros((BLK, LANES), F32)]
    for side, rows, cols, far_block, q_side, g_side in parts:
        keys = k_ref[cols, :]
        values = v_ref[cols, :]
        count = cols.stop - cols.start
        lse_ref = lp_ref if side == 0 else ln_ref
        places = slice(rows.start // BLK * deep, rows.start // BLK * deep + BLK)
        code_col = code_ref[own + cols.start : own + cols.stop, 0:1].astype(F32)
        first = 2 * own * side + rows.start
        mask = code_col == code_row[0:1, first : first + BLK]
        for turn in range(2):
            head = pair * 2 + turn
            query = own_half(q_side[rows, :], turn)
            gctx = own_half(g_side[places, lanes], turn)
            raw = nt(keys, query)
            far = far_ref[pl.ds(head, 1), 15:16] if side else far_ref[pl.ds(head, 1), 31:32]
            if far_block:
                raw = raw + far
            elif side == 0:
                raw = jnp.concatenate(
                    [raw[:half] + biasp_ref[turn].astype(F32), raw[half:] + far], axis=0
                )
            else:
                raw = jnp.concatenate(
                    [raw[: count - half] + far, raw[count - half :] + biasn_ref[turn].astype(F32)],
                    axis=0,
                )
            scores = jnp.where(mask, raw, NEGATIVE)
            logs = lse_ref[0, turn : turn + 1, rows]
            delta = delta_ref[side, pl.ds(head, 1), rows]
            probs = jnp.exp(scores - logs)
            grads = (probs * (nt(values, gctx) - delta)).astype(BF16)
            got_k = nn(grads, query)
            got_v = nn(probs.astype(BF16), gctx)
            for index in range(count // BLK):
                place = (cols.start // BLK) + index
                part = slice(index * BLK, (index + 1) * BLK)
                add_k[place] = add_k[place] + got_k[part]
                add_v[place] = add_v[place] + got_v[part]
    dk_ref[...] = (total_k + jnp.concatenate(add_k, axis=0)).astype(BF16)
    dv_ref[...] = (total_v + jnp.concatenate(add_v, axis=0)).astype(BF16)


def token_columns(meta_ref, probs):
    route_hot = iota(probs.shape, 1) == meta_ref[:, 1:2]
    slot_hot = iota((probs.shape[0], LANES), 1) == meta_ref[:, 2:3]
    gate = jnp.sum(jnp.where(route_hot, probs, 0.0), axis=1, keepdims=True)
    return route_hot, slot_hot, gate


def before_kernel(
    cap,
    depth,
    experts,
    core_ref,
    x_ref,
    own_ref,
    came_ref,
    wonear_ref,
    wofar_ref,
    small_ref,
    gain_ref,
    meta_col_ref,
    meta_row_ref,
    mid_ref,
    hid_ref,
    prob_ref,
    msg_out_ref,
    wo_ref,
    flat,
    msg,
):
    core = core_ref[0]
    tok = x_ref.shape[0]
    width = own_ref.shape[1]
    rows = pl.ds(pl.multiple_of(core * tok, tok), tok)
    side = core_ref[1]
    wo_ref[pl.ds(pl.multiple_of(side * width, width), width), :] = wonear_ref[...]
    wo_ref[pl.ds(pl.multiple_of((1 - side) * width, width), width), :] = wofar_ref[...]
    own_w = wo_ref[pl.ds(pl.multiple_of(core * width, width), width), :]
    other_w = wo_ref[pl.ds(pl.multiple_of((1 - core) * width, width), width), :]
    mid_ref[...] = (
        x_ref[...].astype(F32) + nn(own_ref[rows, :], own_w) + nn(came_ref[rows, :], other_w)
    )
    middle = mid_ref[...]
    scale = lax.rsqrt(jnp.mean(middle * middle, axis=-1, keepdims=True) + EPSILON)
    hidden = (middle * scale * gain_ref[1:2, :]).astype(BF16)
    hid_ref[...] = hidden
    logits = nn(hidden, small_ref[...])
    lane = iota(logits.shape, 1)
    logits = jnp.where(lane < experts, logits, NEGATIVE)
    weight = jnp.exp(logits - jnp.max(logits, axis=1, keepdims=True))
    probs = weight / jnp.sum(weight, axis=1, keepdims=True)
    prob_ref[...] = probs
    _, slot_hot, gate = token_columns(meta_col_ref, probs)
    route_rows = (iota((experts, tok), 0) == meta_row_ref[1:2, :]).astype(BF16)
    values = values_in(route_rows, slot_hot, gate)
    hot = (iota((flat.shape[0], tok), 0) == meta_row_ref[0:1, :]).astype(BF16)
    flat[...] = nn(hot, hidden)
    fill_message(msg_out_ref, flat, msg, cap, depth, values)


def gelu_parts(before):
    square = before * before
    inner = jnp.tanh(before * (GELU_A + (GELU_A * GELU_B) * square))
    half = 0.5 + 0.5 * inner
    slope = half + (before * (1.0 - inner * inner)) * (
        0.5 * GELU_A + (1.5 * GELU_A * GELU_B) * square
    )
    return before * half, slope


def expert_kernel(
    cap,
    depth,
    msg_ref,
    cot_ref,
    win_ref,
    wout_ref,
    earlier_a_ref,
    earlier_b_ref,
    earlier_c_ref,
    rows_ref,
    grad_ref,
    act_ref,
    gbef_ref,
    back_msg_ref,
    made_acc,
    back_acc,
    msg,
):
    del earlier_a_ref, earlier_b_ref, earlier_c_ref
    step = pl.program_id(0)
    count = rows_ref.shape[0]
    groups = count // cap

    @pl.when(step == 0)
    def _():
        values = read_message(msg_ref, made_acc, msg, cap, depth)
        rows_ref[...] = made_acc[...].astype(BF16)
        by_row, _, slot_hot = slot_places(count, groups, cap)
        gate = values_out(by_row, slot_hot, values)
        grad_ref[...] = (gate * cot_ref[...].astype(F32)).astype(BF16)
        made_acc[...] = jnp.zeros_like(made_acc)
        back_acc[...] = jnp.zeros_like(back_acc)

    w_in = win_ref[0]
    w_out = wout_ref[0]
    before = nn(rows_ref[...], w_in)
    grad_active = nt(grad_ref[...], w_out)
    active, slope = gelu_parts(before)
    active = active.astype(BF16)
    grad_before = (grad_active * slope).astype(BF16)
    act_ref[...] = active
    gbef_ref[...] = grad_before
    made_acc[...] += nn(active, w_out)
    back_acc[...] += nt(grad_before, w_in)

    @pl.when(step == pl.num_programs(0) - 1)
    def _():
        produced = made_acc[...].astype(BF16)
        grad_gate = jnp.sum(
            cot_ref[...].astype(F32) * produced.astype(F32), axis=1, keepdims=True
        )
        _, by_col, slot_hot = slot_places(count, groups, cap)
        values = values_in(by_col, slot_hot, grad_gate)
        fill_message(back_msg_ref, back_acc, msg, cap, depth, values, 0, 2)
        made_acc[...] = produced.astype(F32)
        fill_message(back_msg_ref, made_acc, msg, cap, depth, None, 1, 2)


def expert_grads_kernel(
    cap,
    depth,
    rows_ref,
    grad_ref,
    act_ref,
    gbef_ref,
    msgs_ref,
    cots_ref,
    win_ref,
    wout_ref,
    din_ref,
    dout_ref,
    all_rows,
    all_grad,
    flat,
    msg,
):
    count = rows_ref.shape[0]
    size = msg.shape[0]

    @pl.when(pl.program_id(0) == 0)
    def _():
        all_rows[:count, :] = rows_ref[...]
        all_grad[:count, :] = grad_ref[...]
        by_row, _, slot_hot = slot_places(count, count // cap, cap)
        for other in range(msgs_ref.shape[0] // size):
            values = read_message(msgs_ref, flat, msg, cap, depth, start=other * size)
            gate = values_out(by_row, slot_hot, values)
            first = (other + 1) * count
            all_rows[first : first + count, :] = flat[...].astype(BF16)
            cots = cots_ref[other * count : (other + 1) * count, :].astype(F32)
            all_grad[first : first + count, :] = (gate * cots).astype(BF16)

    w_in = win_ref[0]
    w_out = wout_ref[0]
    active, slope = gelu_parts(nn(all_rows[count:, :], w_in))
    grad_before = (nt(all_grad[count:, :], w_out) * slope).astype(BF16)
    actives = jnp.concatenate([act_ref[...], active.astype(BF16)], axis=0)
    grads = jnp.concatenate([gbef_ref[...], grad_before], axis=0)
    din_ref[0] = tn(all_rows[...], grads)
    dout_ref[0] = tn(actives, all_grad[...])


def sums_kernel(
    chip_rows,
    bits_ref,
    hid_ref,
    dq_ref,
    dk_ref,
    dv_ref,
    extra_ref,
    tab_ref,
    senda_ref,
    keepa_ref,
    sendb_ref,
    keepb_ref,
    total,
):
    rows = hid_ref.shape[1]
    half = dq_ref.shape[1]
    split = keepa_ref.shape[1]
    cut = split - half
    hidden = hid_ref[...]
    bit_a = bits_ref[3]
    bit_b = bits_ref[4]
    chunk = keepa_ref.shape[0]
    total[:, :half] = tn(hidden, dq_ref[...])
    total[:, half:] = tn(hidden, dk_ref[:, :cut])
    keepa_ref[...] = total[pl.ds(pl.multiple_of(bit_a * chunk, chunk), chunk), :]
    senda_ref[...] = total[pl.ds(pl.multiple_of((1 - bit_a) * chunk, chunk), chunk), :].astype(BF16)
    total[:, : half - cut] = tn(hidden, dk_ref[:, cut:])
    total[:, half - cut : split - LANES] = tn(hidden, dv_ref[...])
    total[:, split - LANES :] = extra_ref[...]
    chunk = chip_rows
    table = jnp.concatenate([tab_ref[pair, 0:2, :] for pair in range(tab_ref.shape[0])], axis=0)
    table = jnp.where(iota(table.shape, 1) < TABLE, table, 0.0)
    table = pltpu.roll(table, LANES - TABLE, 1)
    for index in range(2 * rows // chunk):
        first = index * chunk // 2
        total[first : first + table.shape[0], split - LANES :] += table
    for index in range(rows // (2 * chunk)):
        first = index * 2 * chunk
        out = slice(index * chunk, (index + 1) * chunk)
        keepb_ref[out, :] = total[pl.ds(pl.multiple_of(first + bit_b * chunk, 8), chunk), :]
        gone = total[pl.ds(pl.multiple_of(first + (1 - bit_b) * chunk, 8), chunk), :]
        sendb_ref[out, :] = gone.astype(BF16)


def join_kernel(
    chip_rows, where_ref, keepa_ref, camea_ref, keepb_ref, cameb_ref, keepo_ref, cameo_ref, later_ref, *refs
):
    del later_ref
    kept_ref, total = refs[0], refs[-1]
    first = 0
    for kept, came in ((keepa_ref, camea_ref), (keepb_ref, cameb_ref), (keepo_ref, cameo_ref)):
        last = first + kept.shape[1]
        total[:, first:last] = kept[...] + came[...].astype(F32)
        first = last
    mine = where_ref[5]
    kept_ref[...] = total[pl.ds(pl.multiple_of(mine * chip_rows, 8), chip_rows), :]
    for other, ref in enumerate(refs[1:-1]):
        place = mine ^ (other + 1)
        ref[...] = total[pl.ds(pl.multiple_of(place * chip_rows, 8), chip_rows), :].astype(BF16)


def input_kernel(core_ref, dq_ref, dk_ref, dv_ref, wa_ref, wb_ref, later_ref, keep_ref, send_ref):
    del later_ref
    core = core_ref[0]
    half = dq_ref.shape[1]
    split = wa_ref.shape[1]
    cut = split - half
    tok = keep_ref.shape[0]
    for out_ref, which in ((send_ref, 1 - core), (keep_ref, core)):
        rows = pl.ds(pl.multiple_of(which * tok, tok), tok)
        out_ref[...] = (
            nt(dq_ref[rows, :], wa_ref[:, :half])
            + nt(dk_ref[rows, :cut], wa_ref[:, half:])
            + nt(dk_ref[rows, cut:], wb_ref[:, : half - cut])
            + nt(dv_ref[rows, :], wb_ref[:, half - cut : split - LANES])
        )


def after_kernel(
    cap,
    depth,
    experts,
    core_ref,
    msg_in_ref,
    cot_ref,
    mid_ref,
    hid_ref,
    prob_ref,
    small_ref,
    gain_ref,
    wo_ref,
    meta_ref,
    own_ref,
    came_ref,
    earlier_ref,
    gmid_ref,
    gmine_ref,
    gtheirs_ref,
    mine_ref,
    theirs_ref,
    sums_ref,
    flat,
    msg,
    low_scr,
):
    del earlier_ref
    core = core_ref[0]
    width = mine_ref.shape[1]
    tok = cot_ref.shape[0]
    values = read_message(msg_in_ref, flat, msg, cap, depth, 0, 2)
    hot = (iota((tok, flat.shape[0]), 1) == meta_ref[:, 0:1]).astype(BF16)
    came = nn(hot, flat[...].astype(BF16))
    probs = prob_ref[...]
    route_hot, slot_hot, gate = token_columns(meta_ref, probs)
    by_route = (iota((tok, experts), 1) == meta_ref[:, 1:2]).astype(BF16)
    grad_gate = values_out(by_route, slot_hot, values)
    grad_logits = (grad_gate * probs * (route_hot.astype(F32) - gate)).astype(BF16)
    grad_hidden = came + nt(grad_logits, small_ref[...])
    middle = mid_ref[...]
    scale = lax.rsqrt(jnp.mean(middle * middle, axis=-1, keepdims=True) + EPSILON)
    normed = middle * scale
    grad_normed = grad_hidden * gain_ref[1:2, :]
    grad_middle = cot_ref[...].astype(F32) + scale * (
        grad_normed - normed * jnp.mean(grad_normed * normed, axis=-1, keepdims=True)
    )
    gmid_ref[...] = grad_middle
    low = grad_middle.astype(BF16)
    low_scr[...] = low
    own_heads = pl.ds(pl.multiple_of(core * width, width), width)
    other_heads = pl.ds(pl.multiple_of((1 - core) * width, width), width)
    gmine_ref[...] = low_scr[:, own_heads]
    gtheirs_ref[...] = low_scr[:, other_heads]
    rows = pl.ds(pl.multiple_of(core * tok, tok), tok)
    pick = (iota((8, width), 1) // (LANES // 2) == iota((8, width), 0)).astype(F32)
    for out_ref, heads, context in (
        (theirs_ref, other_heads, came_ref[rows, :]),
        (mine_ref, own_heads, own_ref[rows, :]),
    ):
        gctx = nt(low, wo_ref[heads, :]).astype(BF16)
        delta = lax.dot_general(
            pick,
            gctx.astype(F32) * context.astype(F32),
            (((1,), (1,)), ((), ())),
            precision=lax.Precision.HIGHEST,
            preferred_element_type=F32,
        )
        out_ref[:tok, :] = gctx
        parts = [piece.astype(F32) for piece in three_parts(delta)]
        parts = jnp.concatenate(parts + [jnp.zeros((8, tok), F32)], axis=0)
        parts = jnp.concatenate([parts, jnp.zeros((32, width - tok), F32)], axis=1)
        out_ref[tok:, :] = parts.astype(BF16)
    router = tn(hid_ref[...], grad_logits)
    gain = lax.dot_general(
        grad_hidden * normed,
        jnp.ones((tok, LANES), F32),
        (((0,), (0,)), ((), ())),
        precision=lax.Precision.HIGHEST,
        preferred_element_type=F32,
    )
    lane = iota(router.shape, 1)
    sums_ref[...] = jnp.where(lane < experts, router, jnp.where(lane == experts, gain, 0.0))


def output_kernel(cap, depth, msg_in_ref, mid_ref, prob_ref, meta_ref, out_ref, flat, msg):
    tok = out_ref.shape[0]
    read_message(msg_in_ref, flat, msg, cap, depth, 1, 2)
    hot = (iota((tok, flat.shape[0]), 1) == meta_ref[:, 0:1]).astype(BF16)
    combined = nn(hot, flat[...].astype(BF16))
    _, _, gate = token_columns(meta_ref, prob_ref[...])
    out_ref[...] = (mid_ref[...] + gate * combined).astype(BF16)


class Place:
    def __init__(self):
        self.n_seq = lax.axis_size("seq")
        self.n_ctx = lax.axis_size("ctx")
        self.count = self.n_seq * self.n_ctx
        self.index = lax.axis_index("seq") * self.n_ctx + lax.axis_index("ctx")
        self.core = self.index % 2
        ctx_bits = (self.n_ctx - 1).bit_length()
        self.bits = (self.count - 1).bit_length()
        self.far_bits = list(range(ctx_bits - 1, 1, -1))
        self.near_bits = [1]
        self.seq_bits = list(range(self.bits - 1, ctx_bits - 1, -1))

    def swap(self, value, bit):
        pairs = [(i, i ^ (1 << bit)) for i in range(self.count)]
        return lax.ppermute(value, AXES, pairs)

    def bit(self, which):
        return (self.index >> which) & 1

    def shift(self, value, steps):
        pairs = []
        for row in range(self.n_seq):
            for col in range(self.n_ctx):
                if 0 <= col + steps < self.n_ctx:
                    pairs.append((row * self.n_ctx + col, row * self.n_ctx + col + steps))
        return lax.ppermute(value, AXES, pairs)

    def ordered(self, own, came, bit, axis, join):
        mine = self.bit(bit) == 1
        return join([jnp.where(mine, came, own), jnp.where(mine, own, came)], axis=axis)

    def stage(self, block, bit, done):
        axis = sum(1 for other in done if other > bit)
        return self.ordered(block, self.swap(block, bit), bit, axis, jnp.stack), done + [bit]

    def several(self, bits):
        index = 0
        for bit in bits:
            index = index * 2 + self.bit(bit)
        masks = []
        for other in range(1, 1 << len(bits)):
            mask = sum(((other >> (len(bits) - 1 - at)) & 1) << bit for at, bit in enumerate(bits))
            masks.append((other, mask))
        return index, masks

    def swap_mask(self, value, mask):
        return lax.ppermute(value, AXES, [(i, i ^ mask) for i in range(self.count)])

    def gather(self, block, order, done=()):
        done = list(done)
        for bit in order:
            block, done = self.stage(block, bit, done)
        return block.reshape((-1,) + block.shape[len(done) + 1 :])

    def halves(self, value, bit, order):
        left = sorted(order, reverse=True)
        axis = left.index(bit)
        value = value.reshape((2,) * len(left) + (-1, value.shape[-1]))
        gone = lax.dynamic_index_in_dim(value, 1 - self.bit(bit), axis, keepdims=False)
        kept = lax.dynamic_index_in_dim(value, self.bit(bit), axis, keepdims=False)
        flat = (-1, value.shape[-1])
        return gone.astype(BF16).reshape(flat), kept.reshape(flat)

    def scatter(self, value, order, keep=()):
        left = sorted(list(order) + list(keep), reverse=True)
        value = value.reshape((2,) * len(left) + (-1,) + value.shape[1:])
        for bit in order:
            axis = left.index(bit)
            mine = self.bit(bit)
            gone = lax.dynamic_index_in_dim(value, 1 - mine, axis, keepdims=False).astype(BF16)
            kept = lax.dynamic_index_in_dim(value, mine, axis, keepdims=False)
            value = kept + self.swap(gone, bit).astype(F32)
            left.remove(bit)
        return value.reshape((-1,) + value.shape[-1:])

    def total(self, value):
        for bit in range(1, self.bits):
            value = value + self.swap(value, bit)
        return value


def call(
    kernel,
    outs,
    *args,
    us=2.0,
    grid=None,
    in_specs=None,
    out_specs=None,
    scratch=(),
    smem_first=False,
    mib=58,
):
    if in_specs is None:
        in_specs = [whole(a.shape) for a in args]
        if smem_first:
            in_specs[0] = smem()
    if out_specs is None:
        out_specs = [whole(o[0]) for o in outs]
    shapes = [jax.ShapeDtypeStruct(*o) for o in outs]
    return pl.pallas_call(
        kernel,
        out_shape=shapes,
        grid=grid if grid is not None else (1,),
        in_specs=in_specs,
        out_specs=out_specs,
        scratch_shapes=list(scratch),
        compiler_params=params(mib),
        cost_estimate=pl.CostEstimate(
            flops=int(us * 1.15e9), transcendentals=0, bytes_accessed=0
        ),
    )(*args)


def local(
    inputs,
    cotangent,
    gain_attn,
    w_query,
    w_key,
    w_value,
    w_output,
    bias_table,
    gain_ffn,
    w_router,
    w_in,
    w_out,
    segments,
    routes,
):
    place = Place()
    core = place.core
    x = inputs[0]
    cot = cotangent[0]
    tok, width = x.shape
    heads = bias_table.shape[1]
    buckets = bias_table.shape[0]
    mine_heads = heads // 2
    half = width // 2
    pairs = half // LANES
    experts = w_router.shape[1]
    hidden_units = w_in.shape[2]
    rows_dev = w_query.shape[0]
    cap = max(2, (9 * tok + 8 * experts - 1) // (8 * experts))
    parts = width // LANES
    depth = -(-(parts * cap + 3) // 16) * 16
    n_ctx = place.n_ctx
    slots = n_ctx * cap
    far, near_bits, seq_bits = place.far_bits, place.near_bits, place.seq_bits
    rows_all = 6 * tok
    own_rows = 2 * tok

    where = jnp.stack(
        [
            core,
            place.bit(seq_bits[-1]),
            place.bit(near_bits[-1]),
            place.bit(seq_bits[0]),
            place.bit(near_bits[0]),
            place.several(far)[0],
        ]
    ).astype(jnp.int32)

    small_w = jnp.concatenate(
        [
            w_router,
            gain_attn[:, None],
            gain_ffn[:, None],
            jnp.zeros((rows_dev, LANES - experts - 2), BF16),
        ],
        axis=1,
    )
    both = [
        jnp.concatenate(
            [w[:, side * half : (side + 1) * half] for w in (w_query, w_key, w_value)]
            + [small_w, w_output[:, side * half : (side + 1) * half]],
            axis=1,
        )
        for side in range(2)
    ]
    ours = jnp.where(core == 0, both[0], both[1])
    theirs = jnp.where(core == 0, both[1], both[0])
    block = place.ordered(ours, place.swap(theirs, 0), 0, 0, jnp.concatenate)
    chip_rows = 2 * rows_dev
    halved = chip_rows % 16 == 0
    split = (block.shape[-1] - half) // 2
    long = tok + CODE_ROWS
    x_ext = call(extend_kernel, [((long, width), BF16)], x, segments)[0]
    around = (place.shift(x_ext, 2), x_ext, place.shift(x_ext, -2))
    near = 2 * BLK
    bias, bias_prev, bias_next, far_bias, meta_col, meta_row = call(
        functools.partial(prepare_kernel, cap, experts),
        [
            ((mine_heads, BLK, near), BF16),
            ((mine_heads, LANES, BLK), BF16),
            ((mine_heads, LANES, BLK), BF16),
            ((8, LANES), F32),
            ((tok, LANES), jnp.int32),
            ((8, tok), jnp.int32),
        ],
        where,
        bias_table,
        routes[0],
        routes[0].reshape(1, tok),
        us=3.0,
        smem_first=True,
    )

    if halved and len(far) == 2:
        came = [place.swap_mask(block, mask) for _, mask in place.several(far)[1]]
        group = 4 * chip_rows
        after_a, after_b, after_o, three = call(
            arrange_kernel,
            [
                ((group, split), BF16),
                ((group, split), BF16),
                ((group, half), BF16),
                ((3 * long, width), BF16),
            ],
            where,
            block,
            *came,
            *around,
            meta_row,
            in_specs=[smem()]
            + [whole(v.shape) for v in (block, *came, *around)]
            + [anywhere()],
        )
        done = list(far)
        after_a = after_a.reshape(2, 2, chip_rows, split)
        after_b = after_b.reshape(2, 2, chip_rows, split)
        after_o = after_o.reshape(2, 2, chip_rows, half)
    else:
        after_far, done = block, []
        for bit in far:
            after_far, done = place.stage(after_far, bit, done)
        after_a, after_b = after_far[..., :split], after_far[..., split : 2 * split]
        after_o = after_far[..., 2 * split :]
        three = call(stack_kernel, [((3 * long, width), BF16)], *around)[0]
    three_came = place.swap(three, 0)
    later_a, done_a = after_a, done
    for bit in near_bits:
        later_a, done_a = place.stage(later_a, bit, done_a)
    later_b, done_b = after_b, done
    for bit in seq_bits:
        later_b, done_b = place.stage(later_b, bit, done_b)
    later_o, done_o = after_o, done
    for bit in near_bits:
        later_o, done_o = place.stage(later_o, bit, done_o)
    later_o = place.ordered(
        later_o, place.swap(later_o, 0), 0, len(later_o.shape) - 1, jnp.concatenate
    )
    for bit in seq_bits[:-1]:
        later_o, done_o = place.stage(later_o, bit, done_o)
    wo_near = later_o.reshape(width // 2, width)
    wo_far = place.swap(wo_near, seq_bits[-1])
    if halved:
        part_rows = width // 2
        pieces_a = (later_a, place.swap(later_a, seq_bits[-1]))
        pieces_b = (later_b, place.swap(later_b, near_bits[-1]))
        pieces = [piece.reshape(part_rows, split) for piece in pieces_a + pieces_b]
    else:
        pieces = [
            place.gather(later_a, seq_bits, done_a),
            place.gather(later_b, near_bits, done_b),
        ]

    def exchange(message):
        shape = message.shape
        message = message.reshape(n_ctx, -1, LANES)
        message = lax.all_to_all(message, "ctx", split_axis=0, concat_axis=0, tiled=True)
        return message.reshape(shape)

    msg_shape = (n_ctx * depth, LANES)
    msg_scratch = [VMEM((slots, width), F32), VMEM(msg_shape, F32)]

    cot_msg = call(
        functools.partial(message_kernel, cap, depth),
        [(msg_shape, BF16)],
        cot,
        meta_row,
        later_a,
        in_specs=[whole((tok, width)), whole((8, tok)), anywhere()],
        scratch=msg_scratch,
    )[0]

    def chip_step(i):
        return jnp.minimum(i, 2)

    def pair_step(i):
        return jnp.maximum(i - 3, 0)

    small_block = pl.BlockSpec((width, LANES), lambda *_: (0, split // LANES - 1))
    hid_all, q_own, k_all, v_all, gains, ctx_low, lse_rows, w_a, w_b, codes = call(
        functools.partial(forward_kernel, experts, chip_rows, len(pieces)),
        [
            ((rows_all, width), BF16),
            ((own_rows, half), BF16),
            ((rows_all, half), BF16),
            ((rows_all, half), BF16),
            ((8, width), F32),
            ((own_rows, half), BF16),
            ((pairs, 8, own_rows), F32),
            ((width, split), BF16),
            ((width, split), BF16),
            ((rows_all, LANES), BF16),
        ],
        far_bias,
        where,
        *pieces,
        three,
        three_came,
        three,
        three_came,
        bias,
        cot_msg,
        us=1.0,
        grid=(3 + pairs,),
        in_specs=[whole((8, LANES)), smem()]
        + [whole(piece.shape) for piece in pieces]
        + [
            pl.BlockSpec((long, width), lambda i: (chip_step(i), 0)),
            pl.BlockSpec((long, width), lambda i: (chip_step(i), 0)),
            pl.BlockSpec((3 * long, tok), lambda *_: (0, 0)),
            pl.BlockSpec((3 * long, tok), lambda *_: (0, 0)),
            pl.BlockSpec((2, BLK, near), lambda i: (pair_step(i), 0, 0)),
            anywhere(),
        ],
        out_specs=[
            pl.BlockSpec((own_rows, width), lambda i: (chip_step(i), 0)),
            whole((own_rows, half)),
            pl.BlockSpec((own_rows, half), lambda i: (chip_step(i), 0)),
            pl.BlockSpec((own_rows, half), lambda i: (chip_step(i), 0)),
            whole((8, width)),
            pl.BlockSpec((own_rows, LANES), lambda i: (0, pair_step(i))),
            pl.BlockSpec((1, 8, own_rows), lambda i: (pair_step(i), 0, 0)),
            whole((width, split)),
            whole((width, split)),
            whole((rows_all, LANES)),
        ],
        scratch=[
            VMEM((own_rows, half), BF16),
            VMEM((rows_all, half), BF16),
            VMEM((rows_all, half), BF16),
            VMEM((8, rows_all), F32),
            VMEM((2, BLK, 5 * BLK), F32),
            VMEM((2, BLK, 5 * BLK), BF16),
        ],
    )

    cot_in = exchange(cot_msg)
    cot_rows = call(
        functools.partial(rows_kernel, cap, depth),
        [((slots, width), BF16)],
        cot_in,
        scratch=msg_scratch,
    )[0]

    hid_block = pl.BlockSpec((own_rows, width), lambda *_: (1, 0))
    code_block = whole((rows_all, LANES))
    far_block = whole((8, LANES))
    own_block = pl.BlockSpec((own_rows, LANES), lambda p: (1, p))
    all_block = pl.BlockSpec((rows_all, LANES), lambda p: (0, p))
    out_block = pl.BlockSpec((own_rows, LANES), lambda p: (0, p))
    bias_block = pl.BlockSpec((2, BLK, near), lambda p: (p, 0, 0))
    lse_block = pl.BlockSpec((1, 8, own_rows), lambda p: (p, 0, 0))

    ctx_came = place.swap(ctx_low, 0)
    mid, hid_two, probs, msg, wo = call(
        functools.partial(before_kernel, cap, depth, experts),
        [
            ((tok, width), F32),
            ((tok, width), BF16),
            ((tok, LANES), F32),
            (msg_shape, BF16),
            ((width, width), BF16),
        ],
        where,
        x,
        ctx_low,
        ctx_came,
        wo_near,
        wo_far,
        w_b,
        gains,
        meta_col,
        meta_row,
        us=4.0,
        in_specs=[
            smem(),
            whole((tok, width)),
            whole((own_rows, half)),
            whole((own_rows, half)),
            whole((width // 2, width)),
            whole((width // 2, width)),
            small_block,
            whole((8, width)),
            whole((tok, LANES)),
            whole((8, tok)),
        ],
        scratch=msg_scratch,
    )
    msg_in = exchange(msg)
    lse_prev = place.shift(lse_rows, 2)
    lse_next = place.shift(lse_rows, -2)
    q_halo = call(
        halo_query_kernel,
        [((2 * own_rows, half), BF16)],
        hid_all,
        w_a,
        us=2.0,
        grid=(2,),
        in_specs=[
            pl.BlockSpec((own_rows, width), lambda i: (2 * i, 0)),
            whole((width, split)),
        ],
        out_specs=[pl.BlockSpec((own_rows, half), lambda i: (i, 0))],
    )[0]

    fblk = 512
    win_block = pl.BlockSpec((1, width, fblk), lambda i: (0, 0, i))
    wout_block = pl.BlockSpec((1, fblk, width), lambda i: (0, i, 0))
    act_block = pl.BlockSpec((slots, fblk), lambda i: (0, i))
    e_rows, e_grad, e_act, e_gbef, back_msg = call(
        functools.partial(expert_kernel, cap, depth),
        [((slots, width), BF16)] * 2
        + [((slots, hidden_units), BF16)] * 2
        + [((2 * msg_shape[0], LANES), BF16)],
        msg_in,
        cot_rows,
        w_in,
        w_out,
        lse_prev,
        lse_next,
        q_halo,
        us=12.0,
        grid=(hidden_units // fblk,),
        in_specs=[
            whole(msg_shape),
            whole((slots, width)),
            win_block,
            wout_block,
            anywhere(),
            anywhere(),
            anywhere(),
        ],
        out_specs=[whole((slots, width))] * 2
        + [act_block] * 2
        + [whole((2 * msg_shape[0], LANES))],
        scratch=[VMEM((slots, width), F32)] + msg_scratch,
    )
    back_in = exchange(back_msg)

    def from_others(value):
        total = value
        for bit in seq_bits:
            total = jnp.concatenate([total, place.swap(total, bit)], axis=0)
        return total[value.shape[0] :]

    if place.n_seq == 2:
        msgs = place.swap(msg_in, seq_bits[0])
        cots = place.swap(cot_rows, seq_bits[0])
    else:
        msgs = from_others(msg_in)
        cots = from_others(cot_rows)
    all_slots = place.n_seq * slots
    grad_w_in, grad_w_out = call(
        functools.partial(expert_grads_kernel, cap, depth),
        [(w_in.shape, F32), (w_out.shape, F32)],
        e_rows,
        e_grad,
        e_act,
        e_gbef,
        msgs,
        cots,
        w_in,
        w_out,
        us=16.0,
        grid=(hidden_units // fblk,),
        in_specs=[
            whole((slots, width)),
            whole((slots, width)),
            act_block,
            act_block,
            whole(msgs.shape),
            whole(cots.shape),
            win_block,
            wout_block,
        ],
        out_specs=[win_block, wout_block],
        scratch=[VMEM((all_slots, width), BF16), VMEM((all_slots, width), BF16)] + msg_scratch,
    )

    grad_mid, gattn_mine, gattn_theirs, gctx_mine, gctx_theirs, extra = call(
        functools.partial(after_kernel, cap, depth, experts),
        [((tok, width), F32)]
        + [((tok, half), BF16)] * 2
        + [((tok + 32, half), BF16)] * 2
        + [((width, LANES), F32)],
        where,
        back_in,
        cot,
        mid,
        hid_two,
        probs,
        w_b,
        gains,
        wo,
        meta_col,
        ctx_low,
        ctx_came,
        grad_w_out,
        us=5.0,
        in_specs=[
            smem(),
            whole(back_in.shape),
            whole((tok, width)),
            whole((tok, width)),
            whole((tok, width)),
            whole((tok, LANES)),
            small_block,
            whole((8, width)),
            whole((width, width)),
            whole((tok, LANES)),
            whole((own_rows, half)),
            whole((own_rows, half)),
            anywhere(),
        ],
        scratch=msg_scratch + [VMEM((tok, width), BF16)],
    )

    gctx = place.ordered(gctx_mine, place.swap(gctx_theirs, 0), 0, 0, jnp.concatenate)
    gctx_prev = place.shift(gctx, 2)
    gctx_next = place.shift(gctx, -2)

    output = call(
        functools.partial(output_kernel, cap, depth),
        [((tok, width), BF16)],
        back_in,
        mid,
        probs,
        meta_col,
        scratch=msg_scratch,
    )[0]

    dq, dk_own, dv_own, tab = call(
        own_backward_kernel,
        [
            ((own_rows, half), BF16),
            ((own_rows, half), F32),
            ((own_rows, half), F32),
            ((pairs, 8, LANES), F32),
        ],
        far_bias,
        q_own,
        k_all,
        v_all,
        gctx,
        lse_rows,
        bias,
        codes,
        us=14.0,
        grid=(pairs,),
        in_specs=[
            far_block,
            out_block,
            all_block,
            all_block,
            whole(gctx.shape),
            lse_block,
            bias_block,
            code_block,
        ],
        out_specs=[out_block] * 3 + [pl.BlockSpec((1, 8, LANES), lambda p: (p, 0, 0))],
        scratch=[
            VMEM((2, BLK, 5 * BLK), F32),
            VMEM((2, BLK, 5 * BLK), F32),
            VMEM((2, BLK, 5 * BLK), BF16),
            VMEM((2, BLK, 5 * BLK), BF16),
            VMEM((2, BLK, near), F32),
        ],
    )

    halo_bias = pl.BlockSpec((2, LANES, BLK), lambda p: (p, 0, 0))
    dk, dv = call(
        halo_backward_kernel,
        [((own_rows, half), BF16)] * 2,
        far_bias,
        q_halo,
        q_halo,
        k_all,
        v_all,
        gctx_prev,
        gctx_next,
        lse_prev,
        lse_next,
        bias_prev,
        bias_next,
        codes,
        dk_own,
        dv_own,
        us=9.0,
        grid=(pairs,),
        in_specs=[
            far_block,
            out_block,
            own_block,
            own_block,
            own_block,
            whole(gctx.shape),
            whole(gctx.shape),
            lse_block,
            lse_block,
            halo_bias,
            halo_bias,
            code_block,
            out_block,
            out_block,
        ],
        out_specs=[out_block] * 2,
        scratch=[VMEM((2, 8, own_rows), F32)],
    )

    ga_cols = place.ordered(gattn_mine, place.swap(gattn_theirs, 0), 0, 0, jnp.concatenate)
    ctx_full = place.ordered(ctx_low, ctx_came, 0, 1, jnp.concatenate)
    back_far = far[::-1]
    total_o = tn(ctx_full, ga_cols)
    order_a = seq_bits + near_bits
    order_b = near_bits + seq_bits
    joined = halved and len(seq_bits) == 1 and len(far) == 2
    if joined:
        chip_bits = seq_bits + near_bits + far
        gone_o, kept_o = place.halves(total_o, order_a[0], chip_bits)
        half_o = kept_o + place.swap(gone_o, order_a[0]).astype(F32)
        gone_o, kept_o = place.halves(half_o, order_a[1], order_a[1:] + far)
        came_o = place.swap(gone_o, order_a[1])
        gone_a, kept_a, gone_b, kept_b = call(
            functools.partial(sums_kernel, chip_rows),
            [
                ((width // 2, split), BF16),
                ((width // 2, split), F32),
                ((width // 2, split), BF16),
                ((width // 2, split), F32),
            ],
            where,
            hid_all,
            dq,
            dk,
            dv,
            extra,
            tab,
            us=4.0,
            in_specs=[
                smem(),
                hid_block,
                whole((own_rows, half)),
                whole((own_rows, half)),
                whole((own_rows, half)),
                whole((width, LANES)),
                whole((pairs, 8, LANES)),
            ],
            scratch=[VMEM((width, split), F32)],
        )
        later = half_a = kept_a + place.swap(gone_a, order_a[0]).astype(F32)
        half_b = kept_b + place.swap(gone_b, order_b[0]).astype(F32)
        gone_a, kept_a = place.halves(half_a, order_a[1], order_a[1:] + far)
        gone_b, kept_b = place.halves(half_b, order_b[1], order_b[1:] + far)
        came_a = place.swap(gone_a, order_a[1])
        came_b = place.swap(gone_b, order_b[1])
    else:
        hid_one = hid_all[own_rows : 2 * own_rows]
        cut = split - half
        total_a = tn(hid_one, jnp.concatenate([dq, dk[:, :cut]], axis=1))
        total_b = tn(hid_one, jnp.concatenate([dk[:, cut:], dv], axis=1))
        later = total_a
        total_b = jnp.concatenate([total_b, extra], axis=1)
        sums = jnp.concatenate([total_a, total_b, total_o], axis=1)
        sums = place.scatter(sums, seq_bits + near_bits + far[::-1])

    part, part_gone = call(
        input_kernel,
        [((tok, width), F32), ((tok, width), F32)],
        where,
        dq,
        dk,
        dv,
        w_a,
        w_b,
        later,
        us=4.0,
        in_specs=[smem()]
        + [whole((own_rows, half))] * 3
        + [whole((width, split))] * 2
        + [anywhere()],
    )
    if joined:
        columns_all = 2 * split + half
        parts_z = call(
            functools.partial(join_kernel, chip_rows),
            [((chip_rows, columns_all), F32)] + [((chip_rows, columns_all), BF16)] * 3,
            where,
            kept_a,
            came_a,
            kept_b,
            came_b,
            kept_o,
            came_o,
            part_gone,
            in_specs=[smem()]
            + [whole(v.shape) for v in (kept_a, came_a, kept_b, came_b, kept_o, came_o)]
            + [anywhere()],
            scratch=[VMEM((kept_a.shape[0], columns_all), F32)],
        )
        sums = parts_z[0]
        for (_, mask), piece in zip(place.several(far)[1], parts_z[1:]):
            sums = sums + place.swap_mask(piece, mask).astype(F32)
    sums = sums.reshape(2, rows_dev, sums.shape[1])
    gone = lax.dynamic_index_in_dim(sums, 1 - core, 0, keepdims=False)
    kept = lax.dynamic_index_in_dim(sums, core, 0, keepdims=False)
    came = place.swap(gone, 0)

    def columns(first):
        return place.ordered(
            kept[:, first : first + half], came[:, first : first + half], 0, 1, jnp.concatenate
        )

    sum_q, sum_k, sum_v = columns(0), columns(half), columns(2 * half)
    sum_out = columns(3 * half + LANES)
    extra_sum = kept[:, 3 * half : 3 * half + LANES] + came[:, 3 * half : 3 * half + LANES]
    grad_router = extra_sum[:, :experts]
    grad_gain_two = extra_sum[:, experts]
    weighted = (
        sum_q * w_query.astype(F32) + sum_k * w_key.astype(F32) + sum_v * w_value.astype(F32)
    )
    grad_gain_one = jnp.sum(weighted, axis=1) / gain_attn.astype(F32)

    grad_hidden = part + place.swap(part_gone, 0)
    tokens = x.astype(F32)
    scale_one = lax.rsqrt(jnp.mean(tokens * tokens, axis=-1, keepdims=True) + EPSILON)
    normed_one = tokens * scale_one
    grad_normed = grad_hidden * gains[0:1]
    grad_tokens = grad_mid + scale_one * (
        grad_normed - normed_one * jnp.mean(grad_normed * normed_one, axis=-1, keepdims=True)
    )

    if joined:
        first = 3 * half + LANES - buckets
        table = kept[:mine_heads, first : first + buckets]
        other = came[:mine_heads, first : first + buckets]
        table_sum = place.ordered(table, other, 0, 0, jnp.concatenate).T
    else:
        table = place.total(tab[:, :2].reshape(mine_heads, LANES))
        table = place.ordered(table, place.swap(table, 0), 0, 0, jnp.concatenate)
        table_sum = table[:, :buckets].T

    return (
        output[None],
        grad_tokens.astype(BF16)[None],
        grad_gain_one,
        sum_q,
        sum_k,
        sum_v,
        sum_out,
        table_sum,
        grad_gain_two,
        grad_router,
        grad_w_in,
        grad_w_out,
    )


def solution(mesh):
    rows = P(("seq", "ctx"), None)
    flat = P(("seq", "ctx"))
    tokens = P("seq", "ctx", None)
    expert = P("ctx", None, None)
    return jax.shard_map(
        local,
        mesh=mesh,
        in_specs=(
            tokens,
            tokens,
            flat,
            rows,
            rows,
            rows,
            rows,
            P(),
            flat,
            rows,
            expert,
            expert,
            P("seq", "ctx"),
            tokens,
        ),
        out_specs=(
            tokens,
            tokens,
            flat,
            rows,
            rows,
            rows,
            rows,
            P(),
            flat,
            rows,
            expert,
            expert,
        ),
        check_vma=False,
    )
```

```python
import functools

import jax
import jax.numpy as jnp
from jax import lax
from jax.experimental import pallas as pl
from jax.experimental.pallas import tpu as pltpu
from jax.sharding import PartitionSpec as P

EPSILON = 1e-06
NEGATIVE = -1e30
THRESHOLDS = (12, 16, 23, 32, 46, 64, 91)
AXES = ("seq", "ctx")
BLK = 256
LANES = 128
FAR = 91
CHUNK = 32
FULL = 58
GRANTS = {
    "extend_kernel": 58,
    "arrange_kernel": 24,
    "prepare_kernel": 58,
    "own_backward_kernel": 24,
    "halo_backward_kernel": 24,
    "sums_kernel": 16,
    "input_kernel": 16,
    "finish_input_kernel": 16,
    "join_kernel": 16,
    "stage_kernel": 16,
    "finish_kernel": 16,
    "output_kernel": 16,
    "output_weight_kernel": 16,
}
TABLE = 32
CODE_ROWS = 16
GELU_A = 0.7978845608028654
GELU_B = 0.044715

BF16 = jnp.bfloat16
F32 = jnp.float32
VMEM = pltpu.VMEM


def params(mib):
    return pltpu.CompilerParams(vmem_limit_bytes=mib * 1024 * 1024)


def whole(shape):
    return pl.BlockSpec(shape, lambda *_: (0,) * len(shape))


def smem():
    return pl.BlockSpec(memory_space=pltpu.SMEM)


def anywhere():
    return pl.BlockSpec(memory_space=pl.ANY)


def nn(a, b):
    return lax.dot_general(a, b, (((1,), (0,)), ((), ())), preferred_element_type=F32)


def nt(a, b):
    return lax.dot_general(a, b, (((1,), (1,)), ((), ())), preferred_element_type=F32)


def tn(a, b):
    return lax.dot_general(a, b, (((0,), (0,)), ((), ())), preferred_element_type=F32)


def exact_nt(a, b):
    return lax.dot_general(
        a,
        b,
        (((1,), (1,)), ((), ())),
        precision=lax.Precision.HIGHEST,
        preferred_element_type=F32,
    )


def iota(shape, dim):
    return lax.broadcasted_iota(jnp.int32, shape, dim)


def bucket_of(offset_pos):
    distance = jnp.abs(offset_pos)
    far_bucket = jnp.full(distance.shape, 8, jnp.int32)
    for border in THRESHOLDS:
        far_bucket = far_bucket + (distance >= border).astype(jnp.int32)
    near_bucket = jnp.where(distance < 8, distance, far_bucket)
    return near_bucket + jnp.where(offset_pos > 0, 16, 0).astype(jnp.int32)


def three_parts(value):
    high = value.astype(BF16)
    rest = value - high.astype(F32)
    middle = rest.astype(BF16)
    return high, middle, (rest - middle.astype(F32)).astype(BF16)


def fill_message(out_ref, flat_ref, msg_ref, cap, depth, values=None, turn=0, turns=1):
    groups = flat_ref.shape[0] // cap
    parts = flat_ref.shape[1] // LANES
    for group in range(groups):
        for part in range(parts):
            first = group * depth + part * cap
            msg_ref[first : first + cap, :] = flat_ref[
                group * cap : (group + 1) * cap, part * LANES : (part + 1) * LANES
            ]
        first = group * depth + parts * cap
        msg_ref[first : (group + 1) * depth, :] = jnp.zeros(
            ((group + 1) * depth - first, LANES), F32
        )
        if values is not None:
            for part, piece in enumerate(values):
                msg_ref[first + part : first + part + 1, :] = piece[group : group + 1, :]
    if turns == 1:
        out_ref[...] = msg_ref[...].astype(BF16)
        return
    for group in range(groups):
        first = (group * turns + turn) * depth
        out_ref[first : first + depth, :] = msg_ref[
            group * depth : (group + 1) * depth, :
        ].astype(BF16)


def read_message(message_ref, flat_ref, msg_ref, cap, depth, turn=0, turns=1, start=0):
    groups = flat_ref.shape[0] // cap
    parts = flat_ref.shape[1] // LANES
    for group in range(groups):
        first = start + (group * turns + turn) * depth
        msg_ref[group * depth : (group + 1) * depth, :] = message_ref[
            first : first + depth, :
        ].astype(F32)
    values = []
    for group in range(groups):
        for part in range(parts):
            first = group * depth + part * cap
            flat_ref[group * cap : (group + 1) * cap, part * LANES : (part + 1) * LANES] = msg_ref[
                first : first + cap, :
            ]
        first = group * depth + parts * cap
        values.append(jnp.sum(msg_ref[first : first + 3, :], axis=0, keepdims=True))
    return jnp.concatenate(values, axis=0)


def values_in(group_hot, slot_hot, value):
    return [
        nn(group_hot, jnp.where(slot_hot, piece, jnp.zeros_like(piece)))
        for piece in three_parts(value)
    ]


def values_out(group_hot, slot_hot, values):
    spread = sum(nn(group_hot, piece) for piece in three_parts(values))
    return jnp.sum(jnp.where(slot_hot, spread, 0.0), axis=1, keepdims=True)


def slot_places(count, groups, cap):
    row = iota((count, 1), 0)
    group = jnp.zeros((count, 1), jnp.int32)
    for border in range(1, groups):
        group = group + (row >= border * cap).astype(jnp.int32)
    by_row = (iota((count, groups), 1) == group).astype(BF16)
    first = iota((groups, count), 0) * cap
    place = iota((groups, count), 1)
    by_col = ((place >= first) & (place < first + cap)).astype(BF16)
    slot_hot = iota((count, LANES), 1) == row - group * cap
    return by_row, by_col, slot_hot


def message_kernel(cap, depth, rows_ref, meta_ref, later_ref, out_ref, flat, msg):
    del later_ref
    hot = (iota((flat.shape[0], rows_ref.shape[0]), 0) == meta_ref[0:1, :]).astype(BF16)
    flat[...] = nn(hot, rows_ref[...])
    fill_message(out_ref, flat, msg, cap, depth)


def rows_kernel(cap, depth, message_ref, out_ref, flat, msg):
    read_message(message_ref, flat, msg, cap, depth)
    out_ref[...] = flat[...].astype(BF16)


def picked_rows(columns, first, count=8):
    pick = (iota((count, LANES), 1) == iota((count, LANES), 0) + first).astype(BF16)
    return nt(pick, columns)


def extend_kernel(x_ref, seg_ref, out_ref):
    tok, width = x_ref.shape
    out_ref[:tok, :] = x_ref[...]
    code = (seg_ref[...] + 1).astype(F32)
    code = jnp.concatenate([code, jnp.zeros((1, width - tok), F32)], axis=1)
    out_ref[tok:, :] = jnp.broadcast_to(code, (CODE_ROWS, width)).astype(BF16)


def arrange_kernel(where_ref, *refs):
    count = len(refs) - 8
    pieces, (before_ref, own_ref, after_ref) = refs[:count], refs[count : count + 3]
    a_ref, b_ref, o_ref, three_ref = refs[count + 4 :]
    rows, split = pieces[0].shape[0], a_ref.shape[1]
    for other, ref in enumerate(pieces):
        place = pl.ds(pl.multiple_of((where_ref[5] ^ other) * rows, 16), rows)
        a_ref[place, :] = ref[:, :split]
        b_ref[place, :] = ref[:, split : 2 * split]
        o_ref[place, :] = ref[:, 2 * split :]
    tok = own_ref.shape[0]
    for place, ref in enumerate((before_ref, own_ref, after_ref)):
        three_ref[place * tok : (place + 1) * tok, :] = ref[...]


def stack_kernel(before_ref, own_ref, after_ref, out_ref):
    tok = own_ref.shape[0]
    for place, ref in enumerate((before_ref, own_ref, after_ref)):
        out_ref[place * tok : (place + 1) * tok, :] = ref[...]


def prepare_kernel(
    cap,
    experts,
    where_ref,
    table_ref,
    route_col_ref,
    route_row_ref,
    bias_ref,
    prev_ref,
    next_ref,
    far_ref,
    col_ref,
    row_ref,
):
    own_heads = bias_ref.shape[0]
    pick = iota((8, 2 * own_heads), 1) == iota((8, 2 * own_heads), 0) + where_ref[0] * own_heads
    table = nt(pick.astype(BF16), table_ref[...])
    far_ref[...] = jnp.concatenate(
        [table, jnp.zeros((8, LANES - table.shape[1]), F32)], axis=1
    )
    fill_bias(table.astype(BF16), bias_ref, prev_ref, next_ref)
    tok = route_col_ref.shape[0]
    route_col = route_col_ref[...]
    route_row = route_row_ref[...]
    hot_col = route_col == iota((tok, LANES), 1)
    earlier = (iota((tok, tok), 1) < iota((tok, tok), 0)).astype(BF16)
    count = nn(earlier, hot_col.astype(F32).astype(BF16))
    slot_col = jnp.sum(jnp.where(hot_col, count, 0.0), axis=1, keepdims=True).astype(jnp.int32)
    lane = iota((tok, LANES), 1)
    col_ref[...] = jnp.where(
        lane == 0,
        route_col * cap + slot_col,
        jnp.where(lane == 1, route_col, jnp.where(lane == 2, slot_col, 0)),
    )
    hot_row = iota((experts, tok), 0) == route_row
    later = (iota((tok, tok), 0) < iota((tok, tok), 1)).astype(BF16)
    count = nn(hot_row.astype(F32).astype(BF16), later)
    slot_row = jnp.sum(jnp.where(hot_row, count, 0.0), axis=0, keepdims=True).astype(jnp.int32)
    line = iota((8, tok), 0)
    row_ref[...] = jnp.where(
        line == 0,
        route_row * cap + slot_row,
        jnp.where(line == 1, route_row, jnp.where(line == 2, slot_row, 0)),
    )


def fill_bias(table, bias_ref, prev_ref, next_ref):
    heads, near = bias_ref.shape[0], bias_ref.shape[2]
    wide = near + BLK
    buckets = table.shape[1]
    apart = iota((buckets, wide), 1) - (wide // 2)
    ahead = nn(table, (bucket_of(apart) == iota((buckets, wide), 0)).astype(BF16))
    behind = nn(table, (bucket_of(-apart) == iota((buckets, wide), 0)).astype(BF16))
    for head in range(heads):
        row = pltpu.roll(ahead[head : head + 1, :], wide - (wide // 2 - LANES), 1)
        full = jnp.broadcast_to(row, (BLK, wide))
        full = pltpu.roll(full, 0, 1, stride=1, stride_axis=0)
        bias_ref[head] = full[:, :near].astype(BF16)
        row = behind[head : head + 1, :]
        for out_ref, ahead_by in ((prev_ref, BLK), (next_ref, -LANES)):
            moved = pltpu.roll(row, (wide // 2 + ahead_by) % wide, 1)
            full = jnp.broadcast_to(moved, (LANES, wide))
            full = pltpu.roll(full, 0, 1, stride=1, stride_axis=0)
            out_ref[head] = full[:, :BLK].astype(BF16)


def own_half(value, turn):
    lane = iota(value.shape, 1)
    keep = (lane < LANES // 2) if turn == 0 else (lane >= LANES // 2)
    return jnp.where(keep, value, jnp.zeros_like(value))


def masked_scores(raw, bias, left, right, mask):
    near = bias.shape[1]
    edge = (raw.shape[1] - near) // 2
    added = jnp.concatenate(
        [
            raw[:, :edge] + left,
            raw[:, edge : edge + near] + bias.astype(F32),
            raw[:, edge + near :] + right,
        ],
        axis=1,
    )
    return jnp.where(mask, added, NEGATIVE)


def join_weights(chip_rows, bits_ref, pieces, wa_ref, wb_ref):
    if len(pieces) == 2:
        wa_ref[...] = pieces[0][...]
        wb_ref[...] = pieces[1][...]
        return
    rows = pieces[0].shape[0]
    for turn in range(2):
        place = bits_ref[1] if turn == 0 else 1 - bits_ref[1]
        wa_ref[pl.ds(pl.multiple_of(place * rows, rows), rows), :] = pieces[turn][...]
        place = bits_ref[2] if turn == 0 else 1 - bits_ref[2]
        for group in range(rows // chip_rows):
            first = pl.multiple_of(group * 2 * chip_rows + place * chip_rows, 16)
            wb_ref[pl.ds(first, chip_rows), :] = pieces[2 + turn][
                group * chip_rows : (group + 1) * chip_rows, :
            ]


def code_columns(code_ref, first, count):
    rows = code_ref[:, first : first + count].astype(BF16)
    pick = (iota((8, LANES), 0) == 0).astype(BF16)
    return tn(rows, pick)


def forward_kernel(experts, chip_rows, count, far_ref, where_ref, *refs):
    forward_body(experts, chip_rows, far_ref, where_ref, refs[:count], *refs[count:])


def forward_body(
    experts,
    chip_rows,
    far_ref,
    where_ref,
    pieces,
    x_ref,
    came_ref,
    bias_ref,
    earlier_ref,
    hid_ref,
    q_ref,
    k_ref,
    v_ref,
    gain_ref,
    small_ref,
    code_ref,
    low_ref,
    lse_ref,
    q_all,
    k_all,
    v_all,
    raw,
    prob,
    wa_ref,
    wb_ref,
    hid_scr,
    code_col,
):
    del earlier_ref
    step = pl.program_id(0)
    own, half = q_ref.shape
    split = wa_ref.shape[1]
    cut = split - half
    core = where_ref[0]
    tok = x_ref.shape[0] - CODE_ROWS

    @pl.when(step == 0)
    def _():
        join_weights(chip_rows, where_ref, pieces, wa_ref, wb_ref)
        small_ref[...] = wb_ref[:, split - LANES :]
        gain_ref[...] = picked_rows(wb_ref[:, split - LANES :], experts)
        code_ref[...] = jnp.zeros_like(code_ref)

    @pl.when(step < 3)
    def _():
        for ref, which in ((x_ref, core), (came_ref, 1 - core)):
            tokens = ref[:tok, :].astype(F32)
            scale = lax.rsqrt(jnp.mean(tokens * tokens, axis=-1, keepdims=True) + EPSILON)
            hid_scr[pl.ds(pl.multiple_of(which * tok, tok), tok), :] = (
                tokens * scale * gain_ref[0:1, :]
            ).astype(BF16)
            first = pl.multiple_of(step * own + which * tok, tok)
            code_ref[:, pl.ds(first, tok)] = ref[tok : tok + 8, :tok].astype(F32)
        hidden = hid_scr[...]
        second = nn(hidden, wb_ref[:, : split - LANES]).astype(BF16)
        k_ref[:, :cut] = nn(hidden, wa_ref[:, half:]).astype(BF16)
        k_ref[:, cut:] = second[:, : half - cut]
        v_ref[...] = second[:, half - cut :]
        rows = pl.ds(pl.multiple_of(step * own, own), own)
        k_all[rows, :] = k_ref[...]
        v_all[rows, :] = v_ref[...]

        @pl.when(step == 1)
        def _():
            query = nn(hidden, wa_ref[:, :half]).astype(BF16)
            q_ref[...] = query
            q_all[...] = query
            hid_ref[...] = hidden
            code_col[...] = code_columns(code_ref, own, own)

    @pl.when(step >= 3)
    def _():
        pair = step - 3
        lanes = pl.ds(pl.multiple_of(pair * LANES, LANES), LANES)
        window = 5 * BLK
        lane = iota((BLK, LANES), 1)
        lse_ref[...] = jnp.zeros_like(lse_ref)
        for block in range(own // BLK):
            rows = slice(block * BLK, (block + 1) * BLK)
            cols = slice(block * BLK, block * BLK + window)
            query = q_all[rows, lanes]
            keys = k_all[cols, lanes]
            values = v_all[cols, lanes]
            outs = []
            for turn in range(2):
                raw[turn] = nt(own_half(query, turn), keys)
            logs = jnp.zeros((BLK, LANES), F32)
            for turn in range(2):
                head = pair * 2 + turn
                found = []
                for first in range(0, BLK, CHUNK):
                    part = slice(first, first + CHUNK)
                    here = block * BLK + first
                    mask = code_col[here : here + CHUNK, 0:1] == code_ref[0:1, cols]
                    scores = masked_scores(
                        raw[turn, part, :],
                        bias_ref[turn, part, :],
                        far_ref[pl.ds(head, 1), 15:16],
                        far_ref[pl.ds(head, 1), 31:32],
                        mask,
                    )
                    top = jnp.max(scores, axis=1, keepdims=True)
                    weight = jnp.exp(scores - top)
                    total = jnp.sum(weight, axis=1, keepdims=True)
                    prob[turn, part, :] = (weight * (1.0 / total)).astype(BF16)
                    found.append(top + jnp.log(total))
                outs.append(nn(prob[turn], values))
                logs = jnp.where(lane == turn, jnp.concatenate(found, axis=0), logs)
            low_ref[rows, :] = jnp.where(lane < LANES // 2, outs[0], outs[1]).astype(BF16)
            lse_ref[0, 0:2, rows] = jnp.transpose(logs)[0:2, :]


def halo_query_kernel(chip_rows, where_ref, x_ref, came_ref, gain_ref, *refs):
    pieces, (q_ref, hid_scr, wa_ref) = refs[:-3], refs[-3:]
    half = q_ref.shape[1]
    core = where_ref[0]
    tok = x_ref.shape[0] - CODE_ROWS

    @pl.when(pl.program_id(0) == 0)
    def _():
        rows = pieces[0].shape[0]
        if len(pieces) == 1:
            wa_ref[...] = pieces[0][...]
        else:
            for turn in range(2):
                place = where_ref[1] if turn == 0 else 1 - where_ref[1]
                wa_ref[pl.ds(pl.multiple_of(place * rows, rows), rows), :] = pieces[turn][...]

    for ref, which in ((x_ref, core), (came_ref, 1 - core)):
        tokens = ref[:tok, :].astype(F32)
        scale = lax.rsqrt(jnp.mean(tokens * tokens, axis=-1, keepdims=True) + EPSILON)
        hid_scr[pl.ds(pl.multiple_of(which * tok, tok), tok), :] = (
            tokens * scale * gain_ref[0:1, :]
        ).astype(BF16)
    q_ref[...] = nn(hid_scr[...], wa_ref[:, :half]).astype(BF16)


def turned(rows):
    parts = jnp.concatenate([piece.astype(F32) for piece in three_parts(rows)], axis=0)
    pick = iota((3 * rows.shape[0], LANES), 0) % rows.shape[0] == iota(
        (3 * rows.shape[0], LANES), 1
    )
    return tn(parts.astype(BF16), pick.astype(BF16))


def packed_rows(rows):
    parts = [piece.astype(F32) for piece in three_parts(rows)]
    halves = [
        jnp.concatenate([part[:, first : first + LANES] for part in parts], axis=1)
        for first in (0, LANES)
    ]
    return jnp.concatenate(halves, axis=0).astype(BF16)


def unpacked_rows(packed):
    packed = packed.astype(F32)
    total = sum(packed[:, first : first + LANES] for first in range(0, 3 * LANES, LANES))
    return jnp.concatenate([total[:8], total[8:]], axis=1)


def rolled_left(value, steps):
    return value if steps == 0 else pltpu.roll(value, value.shape[1] - steps, 1)


def diagonal_sums(value):
    eight = jnp.zeros((8, value.shape[1]), F32)
    for first in range(0, value.shape[0], 8):
        eight = eight + rolled_left(value[first : first + 8], first)
    one = jnp.zeros((1, value.shape[1]), F32)
    for row in range(8):
        one = one + rolled_left(eight[row : row + 1], row)
    return one


def own_backward_kernel(
    far_ref,
    q_ref,
    k_ref,
    v_ref,
    msg_ref,
    lse_ref,
    bias_ref,
    code_ref,
    dq_ref,
    dk_ref,
    dv_ref,
    tab_ref,
    raw,
    grown,
    prob,
    grads,
    near_sum,
):
    pair = pl.program_id(0)
    own = q_ref.shape[0]
    blocks = own // BLK
    deep = msg_ref.shape[0] // blocks
    window = 5 * BLK
    near = bias_ref.shape[2]
    edge = (window - near) // 2
    lanes = pl.ds(pl.multiple_of(pair * LANES, LANES), LANES)
    lane = iota((BLK, LANES), 1)
    codes = code_columns(code_ref, own, own)
    dk_ref[...] = jnp.zeros_like(dk_ref)
    dv_ref[...] = jnp.zeros_like(dv_ref)
    side = iota((window, LANES), 0)
    side_lane = iota((window, LANES), 1)
    ends = ((side < edge) & (side_lane == 0)) | ((side >= edge + near) & (side_lane == 1))
    ends = ends.astype(BF16)
    end_sums = [jnp.zeros((1, LANES), F32), jnp.zeros((1, LANES), F32)]
    for block in range(blocks):
        rows = slice(block * BLK, (block + 1) * BLK)
        cols = slice(block * BLK, block * BLK + window)
        keys = k_ref[cols, :]
        values = v_ref[cols, :]
        keys_ends = jnp.concatenate([keys, ends], axis=1)
        mine = slice((blocks - block) * BLK, (2 * blocks - block) * BLK)
        first = block * deep
        gctx_all = msg_ref[first : first + BLK, lanes]
        deltas = turned(unpacked_rows(msg_ref[first + BLK : first + BLK + 16, :]))
        logs = turned(lse_ref[0, :, rows])
        outs = []
        for turn in range(2):
            raw[turn] = nt(own_half(q_ref[rows, :], turn), keys)
            grown[turn] = nt(own_half(gctx_all, turn), values)
        for turn in range(2):
            head = pair * 2 + turn
            delta = jnp.sum(jnp.where(lane == head, deltas, 0.0), axis=1, keepdims=True)
            log = logs[:, turn : turn + 1]
            for start in range(0, BLK, CHUNK):
                part = slice(start, start + CHUNK)
                here = block * BLK + start
                mask = codes[here : here + CHUNK, 0:1] == code_ref[0:1, cols]
                scores = masked_scores(
                    raw[turn, part, :],
                    bias_ref[turn, part, :],
                    far_ref[pl.ds(head, 1), 15:16],
                    far_ref[pl.ds(head, 1), 31:32],
                    mask,
                )
                probs = jnp.exp(scores - log[part])
                low = (probs * (grown[turn, part, :] - delta[part])).astype(BF16)
                prob[turn, part, :] = probs.astype(BF16)
                grads[turn, part, :] = low
                wide = low[:, edge : edge + near].astype(F32)
                if block == 0:
                    near_sum[turn, part, :] = wide
                else:
                    near_sum[turn, part, :] += wide
        for turn in range(2):
            query = own_half(q_ref[rows, :], turn)
            gctx = own_half(gctx_all, turn)
            both = nn(grads[turn], keys_ends)
            outs.append(both[:, :LANES])
            end_sums[turn] = end_sums[turn] + jnp.sum(both[:, LANES:], axis=0, keepdims=True)
            dk_ref[...] += tn(grads[turn, :, mine], query)
            dv_ref[...] += tn(prob[turn, :, mine], gctx)
        dq_ref[rows, :] = jnp.where(lane < LANES // 2, outs[0], outs[1]).astype(BF16)
    apart = iota((BLK, near), 1) - (2 * BLK - edge) - iota((BLK, near), 0)
    tab_lane = iota((1, LANES), 1)
    hot = (bucket_of(iota((near, LANES), 0) - LANES) == iota((near, LANES), 1)).astype(F32)
    for turn in range(2):
        total = near_sum[turn]
        left = end_sums[turn][:, 0:1] + jnp.sum(jnp.where(apart <= -FAR, total, 0.0))
        right = end_sums[turn][:, 1:2] + jnp.sum(jnp.where(apart >= FAR, total, 0.0))
        close = jnp.where(jnp.abs(apart) < FAR, total, 0.0)
        diagonal = diagonal_sums(close)
        sums = lax.dot_general(
            diagonal,
            hot,
            (((1,), (0,)), ((), ())),
            precision=lax.Precision.HIGHEST,
            preferred_element_type=F32,
        )
        sums = sums + jnp.where(tab_lane == 15, left, 0.0) + jnp.where(tab_lane == 31, right, 0.0)
        tab_ref[0, turn : turn + 1, :] = sums


def halo_backward_kernel(
    far_ref,
    qp_ref,
    qn_ref,
    k_ref,
    v_ref,
    gp_ref,
    gn_ref,
    lp_ref,
    ln_ref,
    biasp_ref,
    biasn_ref,
    code_ref,
    dka_ref,
    dva_ref,
    earlier_ref,
    dk_ref,
    dv_ref,
    delta_ref,
):
    del earlier_ref
    pair = pl.program_id(0)
    own = k_ref.shape[0]
    half = LANES
    codes = code_columns(code_ref, own, own)
    lanes = pl.ds(pl.multiple_of(pair * LANES, LANES), LANES)
    deep = gp_ref.shape[0] // 2
    for side, g_side in enumerate((gp_ref, gn_ref)):
        for block in range(2):
            first = block * deep + BLK
            delta_ref[side, :, block * BLK : (block + 1) * BLK] = unpacked_rows(
                g_side[first : first + 16, :]
            )
    total_k = dka_ref[...]
    total_v = dva_ref[...]
    parts = []
    for side in range(2):
        q_side = qp_ref if side == 0 else qn_ref
        g_side = gp_ref if side == 0 else gn_ref
        for block in range(2):
            far_block = block == side
            rows = slice(block * BLK, (block + 1) * BLK)
            if far_block:
                cols = slice(0, BLK) if side == 0 else slice(own - BLK, own)
            else:
                cols = slice(0, own)
            parts.append((side, rows, cols, far_block, q_side, g_side))
    add_k = [jnp.zeros((BLK, LANES), F32), jnp.zeros((BLK, LANES), F32)]
    add_v = [jnp.zeros((BLK, LANES), F32), jnp.zeros((BLK, LANES), F32)]
    for side, rows, cols, far_block, q_side, g_side in parts:
        keys = k_ref[cols, :]
        values = v_ref[cols, :]
        count = cols.stop - cols.start
        lse_ref = lp_ref if side == 0 else ln_ref
        places = slice(rows.start // BLK * deep, rows.start // BLK * deep + BLK)
        first = 2 * own * side + rows.start
        mask = codes[cols, 0:1] == code_ref[0:1, first : first + BLK]
        for turn in range(2):
            head = pair * 2 + turn
            query = own_half(q_side[rows, :], turn)
            gctx = own_half(g_side[places, lanes], turn)
            raw = nt(keys, query)
            far = far_ref[pl.ds(head, 1), 15:16] if side else far_ref[pl.ds(head, 1), 31:32]
            if far_block:
                raw = raw + far
            elif side == 0:
                raw = jnp.concatenate(
                    [raw[:half] + biasp_ref[turn].astype(F32), raw[half:] + far], axis=0
                )
            else:
                raw = jnp.concatenate(
                    [raw[: count - half] + far, raw[count - half :] + biasn_ref[turn].astype(F32)],
                    axis=0,
                )
            scores = jnp.where(mask, raw, NEGATIVE)
            logs = lse_ref[0, turn : turn + 1, rows]
            delta = delta_ref[side, pl.ds(head, 1), rows]
            probs = jnp.exp(scores - logs)
            grads = (probs * (nt(values, gctx) - delta)).astype(BF16)
            got_k = nn(grads, query)
            got_v = nn(probs.astype(BF16), gctx)
            for index in range(count // BLK):
                place = (cols.start // BLK) + index
                part = slice(index * BLK, (index + 1) * BLK)
                add_k[place] = add_k[place] + got_k[part]
                add_v[place] = add_v[place] + got_v[part]
    dk_ref[...] = (total_k + jnp.concatenate(add_k, axis=0)).astype(BF16)
    dv_ref[...] = (total_v + jnp.concatenate(add_v, axis=0)).astype(BF16)


def token_columns(meta_ref, probs):
    route_hot = iota(probs.shape, 1) == meta_ref[:, 1:2]
    slot_hot = iota((probs.shape[0], LANES), 1) == meta_ref[:, 2:3]
    gate = jnp.sum(jnp.where(route_hot, probs, 0.0), axis=1, keepdims=True)
    return route_hot, slot_hot, gate


def join_halves(where_ref, near_ref, far_ref, out_ref):
    half = near_ref.shape[0]
    side = where_ref[1]
    out_ref[pl.ds(pl.multiple_of(side * half, half), half), :] = near_ref[...]
    out_ref[pl.ds(pl.multiple_of((1 - side) * half, half), half), :] = far_ref[...]


def before_kernel(
    cap,
    depth,
    experts,
    core_ref,
    x_ref,
    own_ref,
    came_ref,
    wonear_ref,
    wofar_ref,
    small_ref,
    gain_ref,
    meta_col_ref,
    meta_row_ref,
    mid_ref,
    hid_ref,
    prob_ref,
    msg_out_ref,
    flat,
    msg,
    wo_ref,
):
    core = core_ref[0]
    tok = x_ref.shape[0]
    width = own_ref.shape[1]
    rows = pl.ds(pl.multiple_of(core * tok, tok), tok)
    join_halves(core_ref, wonear_ref, wofar_ref, wo_ref)
    own_w = wo_ref[pl.ds(pl.multiple_of(core * width, width), width), :]
    other_w = wo_ref[pl.ds(pl.multiple_of((1 - core) * width, width), width), :]
    mid_ref[...] = (
        x_ref[...].astype(F32) + nn(own_ref[rows, :], own_w) + nn(came_ref[rows, :], other_w)
    )
    middle = mid_ref[...]
    scale = lax.rsqrt(jnp.mean(middle * middle, axis=-1, keepdims=True) + EPSILON)
    hidden = (middle * scale * gain_ref[1:2, :]).astype(BF16)
    hid_ref[...] = hidden
    logits = nn(hidden, small_ref[...])
    lane = iota(logits.shape, 1)
    logits = jnp.where(lane < experts, logits, NEGATIVE)
    weight = jnp.exp(logits - jnp.max(logits, axis=1, keepdims=True))
    probs = weight / jnp.sum(weight, axis=1, keepdims=True)
    prob_ref[...] = probs
    _, slot_hot, gate = token_columns(meta_col_ref, probs)
    route_rows = (iota((experts, tok), 0) == meta_row_ref[1:2, :]).astype(BF16)
    values = values_in(route_rows, slot_hot, gate)
    hot = (iota((flat.shape[0], tok), 0) == meta_row_ref[0:1, :]).astype(BF16)
    flat[...] = nn(hot, hidden)
    fill_message(msg_out_ref, flat, msg, cap, depth, values)


def gelu_parts(before):
    square = before * before
    inner = jnp.tanh(before * (GELU_A + (GELU_A * GELU_B) * square))
    half = 0.5 + 0.5 * inner
    slope = half + (before * (1.0 - inner * inner)) * (
        0.5 * GELU_A + (1.5 * GELU_A * GELU_B) * square
    )
    return before * half, slope


def expert_kernel(
    cap,
    depth,
    msg_ref,
    cot_ref,
    win_ref,
    wout_ref,
    earlier_a_ref,
    earlier_b_ref,
    earlier_c_ref,
    rows_ref,
    grad_ref,
    act_ref,
    gbef_ref,
    back_msg_ref,
    made_acc,
    back_acc,
    msg,
):
    del earlier_a_ref, earlier_b_ref, earlier_c_ref
    step = pl.program_id(0)
    count = rows_ref.shape[0]
    groups = count // cap

    @pl.when(step == 0)
    def _():
        values = read_message(msg_ref, made_acc, msg, cap, depth)
        rows_ref[...] = made_acc[...].astype(BF16)
        by_row, _, slot_hot = slot_places(count, groups, cap)
        gate = values_out(by_row, slot_hot, values)
        grad_ref[...] = (gate * cot_ref[...].astype(F32)).astype(BF16)
        made_acc[...] = jnp.zeros_like(made_acc)
        back_acc[...] = jnp.zeros_like(back_acc)

    w_in = win_ref[0]
    w_out = wout_ref[0]
    before = nn(rows_ref[...], w_in)
    grad_active = nt(grad_ref[...], w_out)
    active, slope = gelu_parts(before)
    active = active.astype(BF16)
    grad_before = (grad_active * slope).astype(BF16)
    act_ref[...] = active
    gbef_ref[...] = grad_before
    made_acc[...] += nn(active, w_out)
    back_acc[...] += nt(grad_before, w_in)

    @pl.when(step == pl.num_programs(0) - 1)
    def _():
        produced = made_acc[...].astype(BF16)
        grad_gate = jnp.sum(
            cot_ref[...].astype(F32) * produced.astype(F32), axis=1, keepdims=True
        )
        _, by_col, slot_hot = slot_places(count, groups, cap)
        values = values_in(by_col, slot_hot, grad_gate)
        fill_message(back_msg_ref, back_acc, msg, cap, depth, values, 0, 2)
        made_acc[...] = produced.astype(F32)
        fill_message(back_msg_ref, made_acc, msg, cap, depth, None, 1, 2)


def expert_grads_kernel(
    cap,
    depth,
    rows_ref,
    grad_ref,
    act_ref,
    gbef_ref,
    msgs_ref,
    cots_ref,
    win_ref,
    wout_ref,
    din_ref,
    dout_ref,
    all_rows,
    all_grad,
    flat,
    msg,
):
    count = rows_ref.shape[0]
    size = msg.shape[0]

    @pl.when(pl.program_id(0) == 0)
    def _():
        all_rows[:count, :] = rows_ref[...]
        all_grad[:count, :] = grad_ref[...]
        by_row, _, slot_hot = slot_places(count, count // cap, cap)
        for other in range(msgs_ref.shape[0] // size):
            values = read_message(msgs_ref, flat, msg, cap, depth, start=other * size)
            gate = values_out(by_row, slot_hot, values)
            first = (other + 1) * count
            all_rows[first : first + count, :] = flat[...].astype(BF16)
            cots = cots_ref[other * count : (other + 1) * count, :].astype(F32)
            all_grad[first : first + count, :] = (gate * cots).astype(BF16)

    w_in = win_ref[0]
    w_out = wout_ref[0]
    active, slope = gelu_parts(nn(all_rows[count:, :], w_in))
    grad_before = (nt(all_grad[count:, :], w_out) * slope).astype(BF16)
    actives = jnp.concatenate([act_ref[...], active.astype(BF16)], axis=0)
    grads = jnp.concatenate([gbef_ref[...], grad_before], axis=0)
    din_ref[0] = tn(all_rows[...], grads)
    dout_ref[0] = tn(actives, all_grad[...])


def sums_kernel(
    chip_rows,
    bits_ref,
    hid_ref,
    dq_ref,
    dk_ref,
    dv_ref,
    extra_ref,
    tab_ref,
    earlier_ref,
    senda_ref,
    keepa_ref,
    sendb_ref,
    keepb_ref,
    total,
):
    del earlier_ref
    rows = hid_ref.shape[1]
    half = dq_ref.shape[1]
    split = keepa_ref.shape[1]
    cut = split - half
    hidden = hid_ref[...]
    bit_a = bits_ref[3]
    bit_b = bits_ref[4]
    chunk = keepa_ref.shape[0]
    total[:, :half] = tn(hidden, dq_ref[...])
    total[:, half:] = tn(hidden, dk_ref[:, :cut])
    keepa_ref[...] = total[pl.ds(pl.multiple_of(bit_a * chunk, chunk), chunk), :]
    senda_ref[...] = total[pl.ds(pl.multiple_of((1 - bit_a) * chunk, chunk), chunk), :].astype(BF16)
    total[:, : half - cut] = tn(hidden, dk_ref[:, cut:])
    total[:, half - cut : split - LANES] = tn(hidden, dv_ref[...])
    total[:, split - LANES :] = extra_ref[...]
    chunk = chip_rows
    table = jnp.concatenate([tab_ref[pair, 0:2, :] for pair in range(tab_ref.shape[0])], axis=0)
    table = jnp.where(iota(table.shape, 1) < TABLE, table, 0.0)
    table = pltpu.roll(table, LANES - TABLE, 1)
    for index in range(2 * rows // chunk):
        first = index * chunk // 2
        total[first : first + table.shape[0], split - LANES :] += table
    for index in range(rows // (2 * chunk)):
        first = index * 2 * chunk
        out = slice(index * chunk, (index + 1) * chunk)
        keepb_ref[out, :] = total[pl.ds(pl.multiple_of(first + bit_b * chunk, 8), chunk), :]
        gone = total[pl.ds(pl.multiple_of(first + (1 - bit_b) * chunk, 8), chunk), :]
        sendb_ref[out, :] = gone.astype(BF16)


def add_blocks(counts, refs, total):
    first, at = 0, 0
    for count in counts:
        value = refs[at][...]
        for ref in refs[at + 1 : at + count]:
            value = value + ref[...].astype(F32)
        last = first + value.shape[1]
        total[:, first:last] = value
        first, at = last, at + count


def stage_kernel(counts, groups, rows, where_at, where_ref, later_ref, *refs):
    del later_ref
    blocks, (gone_ref, kept_ref, total) = refs[:-3], refs[-3:]
    add_blocks(counts, blocks, total)
    mine = where_ref[where_at]
    for group in range(groups):
        out = slice(group * rows, (group + 1) * rows)
        base = group * 2 * rows
        kept_ref[out, :] = total[pl.ds(pl.multiple_of(base + mine * rows, 8), rows), :]
        gone = total[pl.ds(pl.multiple_of(base + (1 - mine) * rows, 8), rows), :]
        gone_ref[out, :] = gone.astype(gone_ref.dtype)


def join_kernel(counts, groups, rows, where_ref, later_ref, *refs):
    del later_ref
    blocks, outs, total = refs[: sum(counts)], refs[sum(counts) : -1], refs[-1]
    add_blocks(counts, blocks, total)
    for other, ref in enumerate(outs):
        place = where_ref[5] ^ other
        for group in range(groups):
            first = pl.multiple_of((group * len(outs) + place) * rows, 8)
            ref[group * rows : (group + 1) * rows, :] = total[pl.ds(first, rows), :].astype(
                ref.dtype
            )


def input_kernel(chip_rows, where_ref, dq_ref, dk_ref, dv_ref, later_ref, *refs):
    del later_ref
    pieces, (keep_ref, send_ref, token_ref, wa_ref, wb_ref) = refs[:-5], refs[-5:]
    token_ref[...] = jnp.zeros_like(token_ref)
    join_weights(chip_rows, where_ref, pieces, wa_ref, wb_ref)
    core = where_ref[0]
    half = dq_ref.shape[1]
    split = wa_ref.shape[1]
    cut = split - half
    tok = keep_ref.shape[0]
    for out_ref, which in ((send_ref, 1 - core), (keep_ref, core)):
        rows = pl.ds(pl.multiple_of(which * tok, tok), tok)
        out_ref[...] = (
            nt(dq_ref[rows, :], wa_ref[:, :half])
            + nt(dk_ref[rows, :cut], wa_ref[:, half:])
            + nt(dk_ref[rows, cut:], wb_ref[:, : half - cut])
            + nt(dv_ref[rows, :], wb_ref[:, half - cut : split - LANES])
        )


def finish_input_kernel(part_ref, came_ref, x_ref, gain_ref, mid_ref, out_ref, token_ref):
    token_ref[...] = jnp.zeros_like(token_ref)
    grad_hidden = part_ref[...] + came_ref[...]
    tokens = x_ref[...].astype(F32)
    scale = lax.rsqrt(jnp.mean(tokens * tokens, axis=-1, keepdims=True) + EPSILON)
    normed = tokens * scale
    grad_normed = grad_hidden * gain_ref[0:1, :]
    out_ref[...] = (
        mid_ref[...]
        + scale
        * (grad_normed - normed * jnp.mean(grad_normed * normed, axis=-1, keepdims=True))
    ).astype(BF16)


def output_weight_kernel(
    where_ref, ctx_ref, ctx_came_ref, ga_ref, ga_came_ref, later_ref, gone_ref, kept_ref, token_ref, ga, total
):
    del later_ref
    token_ref[...] = jnp.zeros_like(token_ref)
    core = where_ref[0]
    tok = ga_ref.shape[0]
    half = ctx_ref.shape[1]
    ga[pl.ds(pl.multiple_of(core * tok, tok), tok), :] = ga_ref[...]
    ga[pl.ds(pl.multiple_of((1 - core) * tok, tok), tok), :] = ga_came_ref[...]
    cols = ga[...]
    total[pl.ds(pl.multiple_of(core * half, half), half), :] = tn(ctx_ref[...], cols)
    total[pl.ds(pl.multiple_of((1 - core) * half, half), half), :] = tn(ctx_came_ref[...], cols)
    mine = where_ref[3]
    gone_ref[...] = total[pl.ds(pl.multiple_of((1 - mine) * half, half), half), :].astype(BF16)
    kept_ref[...] = total[pl.ds(pl.multiple_of(mine * half, half), half), :]


def finish_kernel(
    experts,
    buckets,
    where_ref,
    kept_ref,
    came_ref,
    wq_ref,
    wk_ref,
    wv_ref,
    gain_ref,
    q_ref,
    k_ref,
    v_ref,
    o_ref,
    router_ref,
    gains_ref,
    table_ref,
):
    core = where_ref[0]
    half = q_ref.shape[1] // 2
    split = (kept_ref.shape[1] - half) // 2
    cut = split - half
    last = kept_ref.shape[1] - LANES
    for source, which in ((kept_ref, core), (came_ref, 1 - core)):
        cols = pl.ds(pl.multiple_of(which * half, half), half)
        q_ref[:, cols] = source[:, :half]
        k_ref[:, cols] = jnp.concatenate(
            [source[:, half:split], source[:, split + half : split + 2 * half - cut]], axis=1
        )
        o_ref[:, cols] = source[:, split : split + half]
        v_ref[:, cols] = source[:, last - half : last]
    kept = kept_ref[:, last:]
    came = came_ref[:, last:]
    both = kept + came
    router_ref[...] = both[:, :experts]
    weighted = (
        q_ref[...] * wq_ref[...].astype(F32)
        + k_ref[...] * wk_ref[...].astype(F32)
        + v_ref[...] * wv_ref[...].astype(F32)
    )
    gain_one = jnp.sum(weighted, axis=1, keepdims=True) / gain_ref[...].astype(F32)
    lane = iota(both.shape, 1)
    cols = jnp.where(lane == 0, gain_one, jnp.where(lane == 1, both[:, experts : experts + 1], 0.0))
    gains_ref[...] = exact_nt((iota((8, LANES), 0) == iota((8, LANES), 1)).astype(F32), cols)
    heads = table_ref.shape[1] // 2
    own = kept[:heads, LANES - buckets :]
    other = came[:heads, LANES - buckets :]
    first = jnp.where(core == 0, own, other)
    second = jnp.where(core == 0, other, own)
    eye = (iota((buckets, buckets), 0) == iota((buckets, buckets), 1)).astype(F32)
    table_ref[...] = exact_nt(eye, jnp.concatenate([first, second], axis=0))


def after_kernel(
    cap,
    depth,
    experts,
    core_ref,
    msg_in_ref,
    cot_ref,
    mid_ref,
    hid_ref,
    prob_ref,
    small_ref,
    gain_ref,
    wonear_ref,
    wofar_ref,
    meta_ref,
    own_ref,
    came_ref,
    earlier_ref,
    gmid_ref,
    gmine_ref,
    gtheirs_ref,
    mine_ref,
    theirs_ref,
    sums_ref,
    flat,
    msg,
    low_scr,
    wo_ref,
):
    del earlier_ref
    core = core_ref[0]
    width = mine_ref.shape[1]
    tok = cot_ref.shape[0]
    values = read_message(msg_in_ref, flat, msg, cap, depth, 0, 2)
    hot = (iota((tok, flat.shape[0]), 1) == meta_ref[:, 0:1]).astype(BF16)
    came = nn(hot, flat[...].astype(BF16))
    probs = prob_ref[...]
    route_hot, slot_hot, gate = token_columns(meta_ref, probs)
    by_route = (iota((tok, experts), 1) == meta_ref[:, 1:2]).astype(BF16)
    grad_gate = values_out(by_route, slot_hot, values)
    grad_logits = (grad_gate * probs * (route_hot.astype(F32) - gate)).astype(BF16)
    grad_hidden = came + nt(grad_logits, small_ref[...])
    middle = mid_ref[...]
    scale = lax.rsqrt(jnp.mean(middle * middle, axis=-1, keepdims=True) + EPSILON)
    normed = middle * scale
    grad_normed = grad_hidden * gain_ref[1:2, :]
    grad_middle = cot_ref[...].astype(F32) + scale * (
        grad_normed - normed * jnp.mean(grad_normed * normed, axis=-1, keepdims=True)
    )
    gmid_ref[...] = grad_middle
    low = grad_middle.astype(BF16)
    low_scr[...] = low
    join_halves(core_ref, wonear_ref, wofar_ref, wo_ref)
    own_heads = pl.ds(pl.multiple_of(core * width, width), width)
    other_heads = pl.ds(pl.multiple_of((1 - core) * width, width), width)
    gmine_ref[...] = low_scr[:, own_heads]
    gtheirs_ref[...] = low_scr[:, other_heads]
    rows = pl.ds(pl.multiple_of(core * tok, tok), tok)
    pick = (iota((8, width), 1) // (LANES // 2) == iota((8, width), 0)).astype(F32)
    for out_ref, heads, context in (
        (theirs_ref, other_heads, came_ref[rows, :]),
        (mine_ref, own_heads, own_ref[rows, :]),
    ):
        gctx = nt(low, wo_ref[heads, :]).astype(BF16)
        delta = lax.dot_general(
            pick,
            gctx.astype(F32) * context.astype(F32),
            (((1,), (1,)), ((), ())),
            precision=lax.Precision.HIGHEST,
            preferred_element_type=F32,
        )
        out_ref[:tok, :] = gctx
        out_ref[tok:, :] = packed_rows(delta)
    router = tn(hid_ref[...], grad_logits)
    gain = lax.dot_general(
        grad_hidden * normed,
        jnp.ones((tok, LANES), F32),
        (((0,), (0,)), ((), ())),
        precision=lax.Precision.HIGHEST,
        preferred_element_type=F32,
    )
    lane = iota(router.shape, 1)
    sums_ref[...] = jnp.where(lane < experts, router, jnp.where(lane == experts, gain, 0.0))


def output_kernel(cap, depth, msg_in_ref, mid_ref, prob_ref, meta_ref, out_ref, token_ref, flat, msg):
    token_ref[...] = jnp.zeros_like(token_ref)
    tok = out_ref.shape[0]
    read_message(msg_in_ref, flat, msg, cap, depth, 1, 2)
    hot = (iota((tok, flat.shape[0]), 1) == meta_ref[:, 0:1]).astype(BF16)
    combined = nn(hot, flat[...].astype(BF16))
    _, _, gate = token_columns(meta_ref, prob_ref[...])
    out_ref[...] = (mid_ref[...] + gate * combined).astype(BF16)


class Place:
    def __init__(self):
        self.n_seq = lax.axis_size("seq")
        self.n_ctx = lax.axis_size("ctx")
        self.count = self.n_seq * self.n_ctx
        self.index = lax.axis_index("seq") * self.n_ctx + lax.axis_index("ctx")
        self.core = self.index % 2
        ctx_bits = (self.n_ctx - 1).bit_length()
        self.bits = (self.count - 1).bit_length()
        self.far_bits = list(range(ctx_bits - 1, 1, -1))
        self.near_bits = [1]
        self.seq_bits = list(range(self.bits - 1, ctx_bits - 1, -1))

    def swap(self, value, bit):
        pairs = [(i, i ^ (1 << bit)) for i in range(self.count)]
        return lax.ppermute(value, AXES, pairs)

    def bit(self, which):
        return (self.index >> which) & 1

    def shift(self, value, steps):
        pairs = []
        for row in range(self.n_seq):
            for col in range(self.n_ctx):
                if 0 <= col + steps < self.n_ctx:
                    pairs.append((row * self.n_ctx + col, row * self.n_ctx + col + steps))
        return lax.ppermute(value, AXES, pairs)

    def ordered(self, own, came, bit, axis, join):
        mine = self.bit(bit) == 1
        return join([jnp.where(mine, came, own), jnp.where(mine, own, came)], axis=axis)

    def stage(self, block, bit, done):
        axis = sum(1 for other in done if other > bit)
        return self.ordered(block, self.swap(block, bit), bit, axis, jnp.stack), done + [bit]

    def several(self, bits):
        index = 0
        for bit in bits:
            index = index * 2 + self.bit(bit)
        masks = []
        for other in range(1, 1 << len(bits)):
            mask = sum(((other >> (len(bits) - 1 - at)) & 1) << bit for at, bit in enumerate(bits))
            masks.append((other, mask))
        return index, masks

    def swap_mask(self, value, mask):
        return lax.ppermute(value, AXES, [(i, i ^ mask) for i in range(self.count)])

    def gather(self, block, order, done=()):
        done = list(done)
        for bit in order:
            block, done = self.stage(block, bit, done)
        return block.reshape((-1,) + block.shape[len(done) + 1 :])

    def halves(self, value, bit, order):
        left = sorted(order, reverse=True)
        axis = left.index(bit)
        value = value.reshape((2,) * len(left) + (-1, value.shape[-1]))
        gone = lax.dynamic_index_in_dim(value, 1 - self.bit(bit), axis, keepdims=False)
        kept = lax.dynamic_index_in_dim(value, self.bit(bit), axis, keepdims=False)
        flat = (-1, value.shape[-1])
        return gone.astype(BF16).reshape(flat), kept.reshape(flat)

    def scatter(self, value, order, keep=()):
        left = sorted(list(order) + list(keep), reverse=True)
        value = value.reshape((2,) * len(left) + (-1,) + value.shape[1:])
        for bit in order:
            axis = left.index(bit)
            mine = self.bit(bit)
            gone = lax.dynamic_index_in_dim(value, 1 - mine, axis, keepdims=False).astype(BF16)
            kept = lax.dynamic_index_in_dim(value, mine, axis, keepdims=False)
            value = kept + self.swap(gone, bit).astype(F32)
            left.remove(bit)
        return value.reshape((-1,) + value.shape[-1:])

    def total(self, value):
        for bit in range(1, self.bits):
            value = value + self.swap(value, bit)
        return value


def call(
    kernel,
    outs,
    *args,
    us=0.3,
    grid=None,
    in_specs=None,
    out_specs=None,
    scratch=(),
    smem_first=False,
):
    if in_specs is None:
        in_specs = [whole(a.shape) for a in args]
        if smem_first:
            in_specs[0] = smem()
    if out_specs is None:
        out_specs = [whole(o[0]) for o in outs]
    shapes = [jax.ShapeDtypeStruct(*o) for o in outs]
    inner = kernel
    while isinstance(inner, functools.partial):
        inner = inner.func
    mib = GRANTS.get(inner.__name__, FULL)
    return pl.pallas_call(
        kernel,
        out_shape=shapes,
        grid=grid if grid is not None else (1,),
        in_specs=in_specs,
        out_specs=out_specs,
        scratch_shapes=list(scratch),
        compiler_params=params(mib),
        cost_estimate=pl.CostEstimate(
            flops=int(us * 1.15e9), transcendentals=0, bytes_accessed=0
        ),
    )(*args)


def local(
    inputs,
    cotangent,
    gain_attn,
    w_query,
    w_key,
    w_value,
    w_output,
    bias_table,
    gain_ffn,
    w_router,
    w_in,
    w_out,
    segments,
    routes,
):
    place = Place()
    core = place.core
    x = inputs[0]
    cot = cotangent[0]
    tok, width = x.shape
    heads = bias_table.shape[1]
    buckets = bias_table.shape[0]
    mine_heads = heads // 2
    half = width // 2
    pairs = half // LANES
    experts = w_router.shape[1]
    hidden_units = w_in.shape[2]
    rows_dev = w_query.shape[0]
    cap = max(2, (9 * tok + 8 * experts - 1) // (8 * experts))
    parts = width // LANES
    depth = -(-(parts * cap + 3) // 16) * 16
    n_ctx = place.n_ctx
    slots = n_ctx * cap
    far, near_bits, seq_bits = place.far_bits, place.near_bits, place.seq_bits
    rows_all = 6 * tok
    own_rows = 2 * tok

    where = jnp.stack(
        [
            core,
            place.bit(seq_bits[-1]),
            place.bit(near_bits[-1]),
            place.bit(seq_bits[0]),
            place.bit(near_bits[0]),
            place.several(far)[0],
        ]
    ).astype(jnp.int32)

    small_w = jnp.concatenate(
        [
            w_router,
            gain_attn[:, None],
            gain_ffn[:, None],
            jnp.zeros((rows_dev, LANES - experts - 2), BF16),
        ],
        axis=1,
    )
    both = [
        jnp.concatenate(
            [w[:, side * half : (side + 1) * half] for w in (w_query, w_key, w_value)]
            + [small_w, w_output[:, side * half : (side + 1) * half]],
            axis=1,
        )
        for side in range(2)
    ]
    ours = jnp.where(core == 0, both[0], both[1])
    theirs = jnp.where(core == 0, both[1], both[0])
    block = place.ordered(ours, place.swap(theirs, 0), 0, 0, jnp.concatenate)
    chip_rows = 2 * rows_dev
    halved = chip_rows % 16 == 0
    split = (block.shape[-1] - half) // 2
    long = tok + CODE_ROWS
    x_ext = call(extend_kernel, [((long, width), BF16)], x, segments)[0]
    around = (place.shift(x_ext, 2), x_ext, place.shift(x_ext, -2))
    near = 2 * BLK
    bias, bias_prev, bias_next, far_bias, meta_col, meta_row = call(
        functools.partial(prepare_kernel, cap, experts),
        [
            ((mine_heads, BLK, near), BF16),
            ((mine_heads, LANES, BLK), BF16),
            ((mine_heads, LANES, BLK), BF16),
            ((8, LANES), F32),
            ((tok, LANES), jnp.int32),
            ((8, tok), jnp.int32),
        ],
        where,
        bias_table,
        routes[0],
        routes[0].reshape(1, tok),
        us=0.3,
        smem_first=True,
    )

    if halved and len(far) == 2:
        came = [place.swap_mask(block, mask) for _, mask in place.several(far)[1]]
        group = 4 * chip_rows
        after_a, after_b, after_o, three = call(
            arrange_kernel,
            [
                ((group, split), BF16),
                ((group, split), BF16),
                ((group, half), BF16),
                ((3 * long, width), BF16),
            ],
            where,
            block,
            *came,
            *around,
            meta_row,
            in_specs=[smem()]
            + [whole(v.shape) for v in (block, *came, *around)]
            + [anywhere()],
        )
        done = list(far)
        after_a = after_a.reshape(2, 2, chip_rows, split)
        after_b = after_b.reshape(2, 2, chip_rows, split)
        after_o = after_o.reshape(2, 2, chip_rows, half)
    else:
        after_far, done = block, []
        for bit in far:
            after_far, done = place.stage(after_far, bit, done)
        after_a, after_b = after_far[..., :split], after_far[..., split : 2 * split]
        after_o = after_far[..., 2 * split :]
        three = call(stack_kernel, [((3 * long, width), BF16)], *around)[0]
    three_came = place.swap(three, 0)
    later_a, done_a = after_a, done
    for bit in near_bits:
        later_a, done_a = place.stage(later_a, bit, done_a)
    later_b, done_b = after_b, done
    for bit in seq_bits:
        later_b, done_b = place.stage(later_b, bit, done_b)
    later_o, done_o = after_o, done
    for bit in near_bits:
        later_o, done_o = place.stage(later_o, bit, done_o)
    later_o = place.ordered(
        later_o, place.swap(later_o, 0), 0, len(later_o.shape) - 1, jnp.concatenate
    )
    for bit in seq_bits[:-1]:
        later_o, done_o = place.stage(later_o, bit, done_o)
    wo_near = later_o.reshape(width // 2, width)
    wo_far = place.swap(wo_near, seq_bits[-1])
    if halved:
        part_rows = width // 2
        pieces_a = (later_a, place.swap(later_a, seq_bits[-1]))
        pieces_b = (later_b, place.swap(later_b, near_bits[-1]))
        pieces = [piece.reshape(part_rows, split) for piece in pieces_a + pieces_b]
    else:
        pieces = [
            place.gather(later_a, seq_bits, done_a),
            place.gather(later_b, near_bits, done_b),
        ]

    def exchange(message):
        shape = message.shape
        message = message.reshape(n_ctx, -1, LANES)
        message = lax.all_to_all(message, "ctx", split_axis=0, concat_axis=0, tiled=True)
        return message.reshape(shape)

    msg_shape = (n_ctx * depth, LANES)
    msg_scratch = [VMEM((slots, width), F32), VMEM(msg_shape, F32)]

    cot_msg = call(
        functools.partial(message_kernel, cap, depth),
        [(msg_shape, BF16)],
        cot,
        meta_row,
        later_a,
        in_specs=[whole((tok, width)), whole((8, tok)), anywhere()],
        scratch=msg_scratch,
    )[0]

    def chip_step(i):
        return jnp.minimum(i, 2)

    def pair_step(i):
        return jnp.maximum(i - 3, 0)

    small_block = whole((width, LANES))
    hid_own, q_own, k_all, v_all, gains, small, codes, ctx_low, lse_rows = call(
        functools.partial(forward_kernel, experts, chip_rows, len(pieces)),
        [
            ((own_rows, width), BF16),
            ((own_rows, half), BF16),
            ((rows_all, half), BF16),
            ((rows_all, half), BF16),
            ((8, width), F32),
            ((width, LANES), BF16),
            ((8, rows_all), F32),
            ((own_rows, half), BF16),
            ((pairs, 8, own_rows), F32),
        ],
        far_bias,
        where,
        *pieces,
        three,
        three_came,
        bias,
        cot_msg,
        us=1.0,
        grid=(3 + pairs,),
        in_specs=[whole((8, LANES)), smem()]
        + [whole(piece.shape) for piece in pieces]
        + [
            pl.BlockSpec((long, width), lambda i: (chip_step(i), 0)),
            pl.BlockSpec((long, width), lambda i: (chip_step(i), 0)),
            pl.BlockSpec((2, BLK, near), lambda i: (pair_step(i), 0, 0)),
            anywhere(),
        ],
        out_specs=[
            whole((own_rows, width)),
            whole((own_rows, half)),
            pl.BlockSpec((own_rows, half), lambda i: (chip_step(i), 0)),
            pl.BlockSpec((own_rows, half), lambda i: (chip_step(i), 0)),
            whole((8, width)),
            whole((width, LANES)),
            whole((8, rows_all)),
            pl.BlockSpec((own_rows, LANES), lambda i: (0, pair_step(i))),
            pl.BlockSpec((1, 8, own_rows), lambda i: (pair_step(i), 0, 0)),
        ],
        scratch=[
            VMEM((own_rows, half), BF16),
            VMEM((rows_all, half), BF16),
            VMEM((rows_all, half), BF16),
            VMEM((2, BLK, 5 * BLK), F32),
            VMEM((2, BLK, 5 * BLK), BF16),
            VMEM((width, split), BF16),
            VMEM((width, split), BF16),
            VMEM((own_rows, width), BF16),
            VMEM((own_rows, LANES), F32),
        ],
    )

    cot_in = exchange(cot_msg)
    cot_rows = call(
        functools.partial(rows_kernel, cap, depth),
        [((slots, width), BF16)],
        cot_in,
        scratch=msg_scratch,
    )[0]

    code_block = whole((8, rows_all))
    far_block = whole((8, LANES))
    own_block = pl.BlockSpec((own_rows, LANES), lambda p: (1, p))
    all_block = pl.BlockSpec((rows_all, LANES), lambda p: (0, p))
    out_block = pl.BlockSpec((own_rows, LANES), lambda p: (0, p))
    bias_block = pl.BlockSpec((2, BLK, near), lambda p: (p, 0, 0))
    lse_block = pl.BlockSpec((1, 8, own_rows), lambda p: (p, 0, 0))

    ctx_came = place.swap(ctx_low, 0)
    mid, hid_two, probs, msg = call(
        functools.partial(before_kernel, cap, depth, experts),
        [
            ((tok, width), F32),
            ((tok, width), BF16),
            ((tok, LANES), F32),
            (msg_shape, BF16),
        ],
        where,
        x,
        ctx_low,
        ctx_came,
        wo_near,
        wo_far,
        small,
        gains,
        meta_col,
        meta_row,
        us=4.0,
        in_specs=[
            smem(),
            whole((tok, width)),
            whole((own_rows, half)),
            whole((own_rows, half)),
            whole((width // 2, width)),
            whole((width // 2, width)),
            small_block,
            whole((8, width)),
            whole((tok, LANES)),
            whole((8, tok)),
        ],
        scratch=msg_scratch + [VMEM((width, width), BF16)],
    )
    msg_in = exchange(msg)
    lse_prev = place.shift(lse_rows, 2)
    lse_next = place.shift(lse_rows, -2)
    pieces_q = pieces[: len(pieces) // 2]
    q_halo = call(
        functools.partial(halo_query_kernel, chip_rows),
        [((2 * own_rows, half), BF16)],
        where,
        three,
        three_came,
        gains,
        *pieces_q,
        us=0.3,
        grid=(2,),
        in_specs=[
            smem(),
            pl.BlockSpec((long, width), lambda i: (2 * i, 0)),
            pl.BlockSpec((long, width), lambda i: (2 * i, 0)),
            whole((8, width)),
        ]
        + [whole(piece.shape) for piece in pieces_q],
        out_specs=[pl.BlockSpec((own_rows, half), lambda i: (i, 0))],
        scratch=[VMEM((own_rows, width), BF16), VMEM((width, split), BF16)],
    )[0]

    fblk = 512
    win_block = pl.BlockSpec((1, width, fblk), lambda i: (0, 0, i))
    wout_block = pl.BlockSpec((1, fblk, width), lambda i: (0, i, 0))
    act_block = pl.BlockSpec((slots, fblk), lambda i: (0, i))
    e_rows, e_grad, e_act, e_gbef, back_msg = call(
        functools.partial(expert_kernel, cap, depth),
        [((slots, width), BF16)] * 2
        + [((slots, hidden_units), BF16)] * 2
        + [((2 * msg_shape[0], LANES), BF16)],
        msg_in,
        cot_rows,
        w_in,
        w_out,
        q_halo,
        lse_prev,
        lse_next,
        us=12.0,
        grid=(hidden_units // fblk,),
        in_specs=[
            whole(msg_shape),
            whole((slots, width)),
            win_block,
            wout_block,
            anywhere(),
            anywhere(),
            anywhere(),
        ],
        out_specs=[whole((slots, width))] * 2
        + [act_block] * 2
        + [whole((2 * msg_shape[0], LANES))],
        scratch=[VMEM((slots, width), F32)] + msg_scratch,
    )
    back_in = exchange(back_msg)

    def from_others(value):
        total = value
        for bit in seq_bits:
            total = jnp.concatenate([total, place.swap(total, bit)], axis=0)
        return total[value.shape[0] :]

    if place.n_seq == 2:
        msgs = place.swap(msg_in, seq_bits[0])
        cots = place.swap(cot_rows, seq_bits[0])
    else:
        msgs = from_others(msg_in)
        cots = from_others(cot_rows)
    all_slots = place.n_seq * slots
    grad_w_in, grad_w_out = call(
        functools.partial(expert_grads_kernel, cap, depth),
        [(w_in.shape, F32), (w_out.shape, F32)],
        e_rows,
        e_grad,
        e_act,
        e_gbef,
        msgs,
        cots,
        w_in,
        w_out,
        us=16.0,
        grid=(hidden_units // fblk,),
        in_specs=[
            whole((slots, width)),
            whole((slots, width)),
            act_block,
            act_block,
            whole(msgs.shape),
            whole(cots.shape),
            win_block,
            wout_block,
        ],
        out_specs=[win_block, wout_block],
        scratch=[VMEM((all_slots, width), BF16), VMEM((all_slots, width), BF16)] + msg_scratch,
    )

    grad_mid, gattn_mine, gattn_theirs, gctx_mine, gctx_theirs, extra = call(
        functools.partial(after_kernel, cap, depth, experts),
        [((tok, width), F32)]
        + [((tok, half), BF16)] * 2
        + [((tok + 16, half), BF16)] * 2
        + [((width, LANES), F32)],
        where,
        back_in,
        cot,
        mid,
        hid_two,
        probs,
        small,
        gains,
        wo_near,
        wo_far,
        meta_col,
        ctx_low,
        ctx_came,
        grad_w_out,
        us=5.0,
        in_specs=[
            smem(),
            whole(back_in.shape),
            whole((tok, width)),
            whole((tok, width)),
            whole((tok, width)),
            whole((tok, LANES)),
            small_block,
            whole((8, width)),
            whole((width // 2, width)),
            whole((width // 2, width)),
            whole((tok, LANES)),
            whole((own_rows, half)),
            whole((own_rows, half)),
            anywhere(),
        ],
        scratch=msg_scratch + [VMEM((tok, width), BF16), VMEM((width, width), BF16)],
    )

    gctx = place.ordered(gctx_mine, place.swap(gctx_theirs, 0), 0, 0, jnp.concatenate)
    gctx_prev = place.shift(gctx, 2)
    gctx_next = place.shift(gctx, -2)

    token = ((8, LANES), F32)
    output, output_made = call(
        functools.partial(output_kernel, cap, depth),
        [((tok, width), BF16), token],
        back_in,
        mid,
        probs,
        meta_col,
        scratch=msg_scratch,
    )

    dq, dk_own, dv_own, tab = call(
        own_backward_kernel,
        [
            ((own_rows, half), BF16),
            ((own_rows, half), F32),
            ((own_rows, half), F32),
            ((pairs, 8, LANES), F32),
        ],
        far_bias,
        q_own,
        k_all,
        v_all,
        gctx,
        lse_rows,
        bias,
        codes,
        us=14.0,
        grid=(pairs,),
        in_specs=[
            far_block,
            out_block,
            all_block,
            all_block,
            whole(gctx.shape),
            lse_block,
            bias_block,
            code_block,
        ],
        out_specs=[out_block] * 3 + [pl.BlockSpec((1, 8, LANES), lambda p: (p, 0, 0))],
        scratch=[
            VMEM((2, BLK, 5 * BLK), F32),
            VMEM((2, BLK, 5 * BLK), F32),
            VMEM((2, BLK, 5 * BLK), BF16),
            VMEM((2, BLK, 5 * BLK), BF16),
            VMEM((2, BLK, near), F32),
        ],
    )

    order_a = seq_bits + near_bits
    order_b = near_bits + seq_bits
    joined = halved and len(seq_bits) == 1 and len(far) == 2
    ga_came = place.swap(gattn_theirs, 0)
    if joined:
        gone_o, kept_o, sooner = call(
            output_weight_kernel,
            [((width // 2, half), BF16), ((width // 2, half), F32), token],
            where,
            ctx_low,
            ctx_came,
            gattn_mine,
            ga_came,
            tab,
            in_specs=[smem()]
            + [whole((own_rows, half))] * 2
            + [whole((tok, half))] * 2
            + [anywhere()],
            scratch=[VMEM((own_rows, half), BF16), VMEM((width, half), F32)],
        )
    else:
        sooner = tab
    halo_bias = pl.BlockSpec((2, LANES, BLK), lambda p: (p, 0, 0))
    dk, dv = call(
        halo_backward_kernel,
        [((own_rows, half), BF16)] * 2,
        far_bias,
        q_halo,
        q_halo,
        k_all,
        v_all,
        gctx_prev,
        gctx_next,
        lse_prev,
        lse_next,
        bias_prev,
        bias_next,
        codes,
        dk_own,
        dv_own,
        sooner,
        us=7.0,
        grid=(pairs,),
        in_specs=[
            far_block,
            out_block,
            own_block,
            own_block,
            own_block,
            whole(gctx.shape),
            whole(gctx.shape),
            lse_block,
            lse_block,
            halo_bias,
            halo_bias,
            code_block,
            out_block,
            out_block,
            anywhere(),
        ],
        out_specs=[out_block] * 2,
        scratch=[VMEM((2, 8, own_rows), F32)],
    )


    def input_parts(later):
        return call(
            functools.partial(input_kernel, chip_rows),
            [((tok, width), F32), ((tok, width), F32), token],
            where,
            dq,
            dk,
            dv,
            later,
            *pieces,
            us=0.3,
            in_specs=[smem()]
            + [whole((own_rows, half))] * 3
            + [anywhere()]
            + [whole(piece.shape) for piece in pieces],
            scratch=[VMEM((width, split), BF16), VMEM((width, split), BF16)],
        )

    def input_gradient(part, part_gone):
        return call(
            finish_input_kernel,
            [((tok, width), BF16), token],
            part,
            place.swap(part_gone, 0),
            x,
            gains,
            grad_mid,
        )

    if joined:
        came_o = place.swap(gone_o, order_a[0])
        gone_a, kept_a, gone_b, kept_b = call(
            functools.partial(sums_kernel, chip_rows),
            [
                ((width // 2, split), BF16),
                ((width // 2, split), F32),
                ((width // 2, split), BF16),
                ((width // 2, split), F32),
            ],
            where,
            hid_own,
            dq,
            dk,
            dv,
            extra,
            tab,
            came_o,
            us=0.3,
            in_specs=[
                smem(),
                whole((own_rows, width)),
                whole((own_rows, half)),
                whole((own_rows, half)),
                whole((own_rows, half)),
                whole((width, LANES)),
                whole((pairs, 8, LANES)),
                anywhere(),
            ],
            scratch=[VMEM((width, split), F32)],
        )
        came_a = place.swap(gone_a, order_a[0])
        came_b = place.swap(gone_b, order_b[0])

        masks = [mask for _, mask in place.several(far)[1]]
        far_count = len(masks) + 1

        def added(kernel, later, counts, blocks, outs, *how):
            columns_all = sum(blocks[sum(counts[:at])].shape[1] for at in range(len(counts)))
            height = blocks[0].shape[0]
            return call(
                functools.partial(kernel, counts, *how),
                [((height // out, columns_all), dtype) for out, dtype in outs],
                where,
                later,
                *blocks,
                us=0.3,
                in_specs=[smem(), anywhere()] + [whole(block.shape) for block in blocks],
                scratch=[VMEM((height, columns_all), F32)],
            )

        def swapped(pieces):
            return [place.swap_mask(piece, mask) for piece, mask in zip(pieces, masks)]

        two = [(2, BF16), (2, F32)]
        four = [(far_count, F32)] + [(far_count, BF16)] * len(masks)
        gone_a, kept_a = added(
            stage_kernel,
            came_b,
            (2, 2),
            (kept_a, came_a, kept_o, came_o),
            two,
            far_count,
            chip_rows,
            4,
        )
        part, part_gone, part_made = input_parts(output_made)
        pieces_z = added(
            join_kernel, far_bias, (2,), (kept_b, came_b), four, 2, chip_rows
        )
        came_a = place.swap(gone_a, order_a[1])
        came_z = swapped(pieces_z[1:])
        grad_tokens, ended = input_gradient(part, part_gone)
        pieces_a = added(join_kernel, part_made, (2,), (kept_a, came_a), four, 1, chip_rows)
        gone_b, kept_b = added(
            stage_kernel, ended, (far_count,), (pieces_z[0], *came_z), two, 1, chip_rows, 3
        )
        came_b = place.swap(gone_b, seq_bits[0])
        came_z = swapped(pieces_a[1:])
        gone, kept = added(
            stage_kernel,
            ended,
            (far_count, 2),
            (pieces_a[0], *came_z, kept_b, came_b),
            [(2, F32), (2, F32)],
            1,
            rows_dev,
            0,
        )
    else:
        ga_cols = place.ordered(gattn_mine, ga_came, 0, 0, jnp.concatenate)
        ctx_full = place.ordered(ctx_low, ctx_came, 0, 1, jnp.concatenate)
        cut = split - half
        total_a = tn(hid_own, jnp.concatenate([dq, dk[:, :cut]], axis=1))
        total_b = tn(hid_own, jnp.concatenate([dk[:, cut:], dv], axis=1))
        grad_tokens, _ = input_gradient(*input_parts(total_a)[:2])
        total_b = jnp.concatenate([total_b, extra], axis=1)
        sums = jnp.concatenate([total_a, total_b, tn(ctx_full, ga_cols)], axis=1)
        sums = place.scatter(sums, seq_bits + near_bits + far[::-1])
        sums = sums.reshape(2, rows_dev, sums.shape[1])
        gone = lax.dynamic_index_in_dim(sums, 1 - core, 0, keepdims=False)
        kept = lax.dynamic_index_in_dim(sums, core, 0, keepdims=False)
    came = place.swap(gone, 0)
    if joined:
        sum_q, sum_k, sum_v, sum_out, grad_router, gain_rows, table_sum = call(
            functools.partial(finish_kernel, experts, buckets),
            [((rows_dev, width), F32)] * 4
            + [((rows_dev, experts), F32), ((8, rows_dev), F32), ((buckets, heads), F32)],
            where,
            kept,
            came,
            w_query,
            w_key,
            w_value,
            gain_attn[:, None],
            smem_first=True,
        )
        grad_gain_one, grad_gain_two = gain_rows[0], gain_rows[1]
    else:

        def columns(first):
            return place.ordered(
                kept[:, first : first + half], came[:, first : first + half], 0, 1, jnp.concatenate
            )

        sum_q, sum_k, sum_v = columns(0), columns(half), columns(2 * half)
        sum_out = columns(3 * half + LANES)
        extra_sum = kept[:, 3 * half : 3 * half + LANES] + came[:, 3 * half : 3 * half + LANES]
        grad_router = extra_sum[:, :experts]
        grad_gain_two = extra_sum[:, experts]
        weighted = (
            sum_q * w_query.astype(F32) + sum_k * w_key.astype(F32) + sum_v * w_value.astype(F32)
        )
        grad_gain_one = jnp.sum(weighted, axis=1) / gain_attn.astype(F32)
        table = place.total(tab[:, :2].reshape(mine_heads, LANES))
        table = place.ordered(table, place.swap(table, 0), 0, 0, jnp.concatenate)
        table_sum = table[:, :buckets].T

    return (
        output[None],
        grad_tokens[None],
        grad_gain_one,
        sum_q,
        sum_k,
        sum_v,
        sum_out,
        table_sum,
        grad_gain_two,
        grad_router,
        grad_w_in,
        grad_w_out,
    )


def solution(mesh):
    rows = P(("seq", "ctx"), None)
    flat = P(("seq", "ctx"))
    tokens = P("seq", "ctx", None)
    expert = P("ctx", None, None)
    return jax.shard_map(
        local,
        mesh=mesh,
        in_specs=(
            tokens,
            tokens,
            flat,
            rows,
            rows,
            rows,
            rows,
            P(),
            flat,
            rows,
            expert,
            expert,
            P("seq", "ctx"),
            tokens,
        ),
        out_specs=(
            tokens,
            tokens,
            flat,
            rows,
            rows,
            rows,
            rows,
            P(),
            flat,
            rows,
            expert,
            expert,
        ),
        check_vma=False,
    )
```

```python
import functools

import jax
import jax.numpy as jnp
from jax import lax
from jax.experimental import pallas as pl
from jax.experimental.pallas import tpu as pltpu
from jax.sharding import PartitionSpec as P

EPSILON = 1e-06
NEGATIVE = -1e30
THRESHOLDS = (12, 16, 23, 32, 46, 64, 91)
AXES = ("seq", "ctx")
BLK = 256
LANES = 128
FAR = 91
CHUNK = 32
FULL = 58
GRANTS = {
    "extend_kernel": 58,
    "arrange_kernel": 24,
    "prepare_kernel": 58,
    "own_backward_kernel": 24,
    "halo_backward_kernel": 24,
    "sums_kernel": 16,
    "input_kernel": 16,
    "finish_input_kernel": 16,
    "join_kernel": 16,
    "stage_kernel": 16,
    "finish_kernel": 16,
    "output_kernel": 16,
    "output_weight_kernel": 16,
}
TABLE = 32
CODE_ROWS = 16
GELU_A = 0.7978845608028654
GELU_B = 0.044715

BF16 = jnp.bfloat16
F32 = jnp.float32
VMEM = pltpu.VMEM


def params(mib):
    return pltpu.CompilerParams(vmem_limit_bytes=mib * 1024 * 1024)


def whole(shape):
    return pl.BlockSpec(shape, lambda *_: (0,) * len(shape))


def smem():
    return pl.BlockSpec(memory_space=pltpu.SMEM)


def anywhere():
    return pl.BlockSpec(memory_space=pl.ANY)


def nn(a, b):
    return lax.dot_general(a, b, (((1,), (0,)), ((), ())), preferred_element_type=F32)


def nt(a, b):
    return lax.dot_general(a, b, (((1,), (1,)), ((), ())), preferred_element_type=F32)


def tn(a, b):
    return lax.dot_general(a, b, (((0,), (0,)), ((), ())), preferred_element_type=F32)


def exact_nt(a, b):
    return lax.dot_general(
        a,
        b,
        (((1,), (1,)), ((), ())),
        precision=lax.Precision.HIGHEST,
        preferred_element_type=F32,
    )


def iota(shape, dim):
    return lax.broadcasted_iota(jnp.int32, shape, dim)


def bucket_of(offset_pos):
    distance = jnp.abs(offset_pos)
    far_bucket = jnp.full(distance.shape, 8, jnp.int32)
    for border in THRESHOLDS:
        far_bucket = far_bucket + (distance >= border).astype(jnp.int32)
    near_bucket = jnp.where(distance < 8, distance, far_bucket)
    return near_bucket + jnp.where(offset_pos > 0, 16, 0).astype(jnp.int32)


def three_parts(value):
    high = value.astype(BF16)
    rest = value - high.astype(F32)
    middle = rest.astype(BF16)
    return high, middle, (rest - middle.astype(F32)).astype(BF16)


def fill_message(out_ref, flat_ref, msg_ref, cap, depth, values=None, turn=0, turns=1):
    groups = flat_ref.shape[0] // cap
    parts = flat_ref.shape[1] // LANES
    for group in range(groups):
        for part in range(parts):
            first = group * depth + part * cap
            msg_ref[first : first + cap, :] = flat_ref[
                group * cap : (group + 1) * cap, part * LANES : (part + 1) * LANES
            ]
        first = group * depth + parts * cap
        msg_ref[first : (group + 1) * depth, :] = jnp.zeros(
            ((group + 1) * depth - first, LANES), F32
        )
        if values is not None:
            for part, piece in enumerate(values):
                msg_ref[first + part : first + part + 1, :] = piece[group : group + 1, :]
    if turns == 1:
        out_ref[...] = msg_ref[...].astype(BF16)
        return
    for group in range(groups):
        first = (group * turns + turn) * depth
        out_ref[first : first + depth, :] = msg_ref[
            group * depth : (group + 1) * depth, :
        ].astype(BF16)


def read_message(message_ref, flat_ref, msg_ref, cap, depth, turn=0, turns=1, start=0):
    groups = flat_ref.shape[0] // cap
    parts = flat_ref.shape[1] // LANES
    for group in range(groups):
        first = start + (group * turns + turn) * depth
        msg_ref[group * depth : (group + 1) * depth, :] = message_ref[
            first : first + depth, :
        ].astype(F32)
    values = []
    for group in range(groups):
        for part in range(parts):
            first = group * depth + part * cap
            flat_ref[group * cap : (group + 1) * cap, part * LANES : (part + 1) * LANES] = msg_ref[
                first : first + cap, :
            ]
        first = group * depth + parts * cap
        values.append(jnp.sum(msg_ref[first : first + 3, :], axis=0, keepdims=True))
    return jnp.concatenate(values, axis=0)


def values_in(group_hot, slot_hot, value):
    return [
        nn(group_hot, jnp.where(slot_hot, piece, jnp.zeros_like(piece)))
        for piece in three_parts(value)
    ]


def values_out(group_hot, slot_hot, values):
    spread = sum(nn(group_hot, piece) for piece in three_parts(values))
    return jnp.sum(jnp.where(slot_hot, spread, 0.0), axis=1, keepdims=True)


def slot_places(count, groups, cap):
    row = iota((count, 1), 0)
    group = jnp.zeros((count, 1), jnp.int32)
    for border in range(1, groups):
        group = group + (row >= border * cap).astype(jnp.int32)
    by_row = (iota((count, groups), 1) == group).astype(BF16)
    first = iota((groups, count), 0) * cap
    place = iota((groups, count), 1)
    by_col = ((place >= first) & (place < first + cap)).astype(BF16)
    slot_hot = iota((count, LANES), 1) == row - group * cap
    return by_row, by_col, slot_hot


def message_kernel(cap, depth, rows_ref, meta_ref, later_ref, out_ref, flat, msg):
    del later_ref
    hot = (iota((flat.shape[0], rows_ref.shape[0]), 0) == meta_ref[0:1, :]).astype(BF16)
    flat[...] = nn(hot, rows_ref[...])
    fill_message(out_ref, flat, msg, cap, depth)


def rows_kernel(cap, depth, message_ref, out_ref, flat, msg):
    read_message(message_ref, flat, msg, cap, depth)
    out_ref[...] = flat[...].astype(BF16)


def picked_rows(columns, first, count=8):
    pick = (iota((count, LANES), 1) == iota((count, LANES), 0) + first).astype(BF16)
    return nt(pick, columns)


def start_kernel(
    experts,
    where_ref,
    wq_ref,
    wk_ref,
    wv_ref,
    wo_ref,
    router_ref,
    gains_ref,
    x_ref,
    seg_ref,
    ours_ref,
    theirs_ref,
    ext_ref,
):
    core = where_ref[0]
    half = wq_ref.shape[1] // 2
    rows = wq_ref.shape[0]
    pick = iota((experts, LANES), 0) == iota((experts, LANES), 1)
    small = tn(router_ref[...], pick.astype(BF16))
    gains = jnp.concatenate([gains_ref[...].astype(F32), jnp.zeros((6, rows), F32)], axis=0)
    pick = iota((8, LANES), 0) + experts == iota((8, LANES), 1)
    small = (small + tn(gains.astype(BF16), pick.astype(BF16))).astype(BF16)
    for out_ref, which in ((ours_ref, core), (theirs_ref, 1 - core)):
        cols = pl.ds(pl.multiple_of(which * half, half), half)
        out_ref[:, :half] = wq_ref[:, cols]
        out_ref[:, half : 2 * half] = wk_ref[:, cols]
        out_ref[:, 2 * half : 3 * half] = wv_ref[:, cols]
        out_ref[:, 3 * half : 3 * half + LANES] = small
        out_ref[:, 3 * half + LANES :] = wo_ref[:, cols]
    tok, width = x_ref.shape
    ext_ref[:tok, :] = x_ref[...]
    code = (seg_ref[...] + 1).astype(F32)
    code = jnp.concatenate([code, jnp.zeros((1, width - tok), F32)], axis=1)
    ext_ref[tok:, :] = jnp.broadcast_to(code, (CODE_ROWS, width)).astype(BF16)


def arrange_kernel(where_ref, *refs):
    count = len(refs) - 8
    pieces, (before_ref, own_ref, after_ref) = refs[:count], refs[count : count + 3]
    a_ref, b_ref, o_ref, three_ref = refs[count + 4 :]
    rows, split = pieces[0].shape[0], a_ref.shape[1]
    for other, ref in enumerate(pieces):
        place = pl.ds(pl.multiple_of((where_ref[5] ^ other) * rows, 16), rows)
        a_ref[place, :] = ref[:, :split]
        b_ref[place, :] = ref[:, split : 2 * split]
        o_ref[place, :] = ref[:, 2 * split :]
    tok = own_ref.shape[0]
    for place, ref in enumerate((before_ref, own_ref, after_ref)):
        three_ref[place * tok : (place + 1) * tok, :] = ref[...]


def stack_kernel(before_ref, own_ref, after_ref, out_ref):
    tok = own_ref.shape[0]
    for place, ref in enumerate((before_ref, own_ref, after_ref)):
        out_ref[place * tok : (place + 1) * tok, :] = ref[...]


def prepare_kernel(
    cap,
    experts,
    where_ref,
    table_ref,
    route_col_ref,
    route_row_ref,
    bias_ref,
    prev_ref,
    next_ref,
    far_ref,
    col_ref,
    row_ref,
):
    own_heads = bias_ref.shape[0]
    pick = iota((8, 2 * own_heads), 1) == iota((8, 2 * own_heads), 0) + where_ref[0] * own_heads
    table = nt(pick.astype(BF16), table_ref[...])
    far_ref[...] = jnp.concatenate(
        [table, jnp.zeros((8, LANES - table.shape[1]), F32)], axis=1
    )
    fill_bias(table.astype(BF16), bias_ref, prev_ref, next_ref)
    tok = route_col_ref.shape[0]
    route_col = route_col_ref[...]
    route_row = route_row_ref[...]
    hot_col = route_col == iota((tok, LANES), 1)
    earlier = (iota((tok, tok), 1) < iota((tok, tok), 0)).astype(BF16)
    count = nn(earlier, hot_col.astype(F32).astype(BF16))
    slot_col = jnp.sum(jnp.where(hot_col, count, 0.0), axis=1, keepdims=True).astype(jnp.int32)
    lane = iota((tok, LANES), 1)
    col_ref[...] = jnp.where(
        lane == 0,
        route_col * cap + slot_col,
        jnp.where(lane == 1, route_col, jnp.where(lane == 2, slot_col, 0)),
    )
    hot_row = iota((experts, tok), 0) == route_row
    later = (iota((tok, tok), 0) < iota((tok, tok), 1)).astype(BF16)
    count = nn(hot_row.astype(F32).astype(BF16), later)
    slot_row = jnp.sum(jnp.where(hot_row, count, 0.0), axis=0, keepdims=True).astype(jnp.int32)
    line = iota((8, tok), 0)
    row_ref[...] = jnp.where(
        line == 0,
        route_row * cap + slot_row,
        jnp.where(line == 1, route_row, jnp.where(line == 2, slot_row, 0)),
    )


def fill_bias(table, bias_ref, prev_ref, next_ref):
    heads, near = bias_ref.shape[0], bias_ref.shape[2]
    wide = near + BLK
    buckets = table.shape[1]
    apart = iota((buckets, wide), 1) - (wide // 2)
    ahead = nn(table, (bucket_of(apart) == iota((buckets, wide), 0)).astype(BF16))
    behind = nn(table, (bucket_of(-apart) == iota((buckets, wide), 0)).astype(BF16))
    for head in range(heads):
        row = pltpu.roll(ahead[head : head + 1, :], wide - (wide // 2 - LANES), 1)
        full = jnp.broadcast_to(row, (BLK, wide))
        full = pltpu.roll(full, 0, 1, stride=1, stride_axis=0)
        bias_ref[head] = full[:, :near].astype(BF16)
        row = behind[head : head + 1, :]
        for out_ref, ahead_by in ((prev_ref, BLK), (next_ref, -LANES)):
            moved = pltpu.roll(row, (wide // 2 + ahead_by) % wide, 1)
            full = jnp.broadcast_to(moved, (LANES, wide))
            full = pltpu.roll(full, 0, 1, stride=1, stride_axis=0)
            out_ref[head] = full[:, :BLK].astype(BF16)


def own_half(value, turn):
    lane = iota(value.shape, 1)
    keep = (lane < LANES // 2) if turn == 0 else (lane >= LANES // 2)
    return jnp.where(keep, value, jnp.zeros_like(value))


def masked_scores(raw, bias, left, right, mask):
    near = bias.shape[1]
    edge = (raw.shape[1] - near) // 2
    added = jnp.concatenate(
        [
            raw[:, :edge] + left,
            raw[:, edge : edge + near] + bias.astype(F32),
            raw[:, edge + near :] + right,
        ],
        axis=1,
    )
    return jnp.where(mask, added, NEGATIVE)


def join_weights(chip_rows, bits_ref, pieces, wa_ref, wb_ref):
    if len(pieces) == 2:
        wa_ref[...] = pieces[0][...]
        wb_ref[...] = pieces[1][...]
        return
    rows = pieces[0].shape[0]
    for turn in range(2):
        place = bits_ref[1] if turn == 0 else 1 - bits_ref[1]
        wa_ref[pl.ds(pl.multiple_of(place * rows, rows), rows), :] = pieces[turn][...]
        place = bits_ref[2] if turn == 0 else 1 - bits_ref[2]
        for group in range(rows // chip_rows):
            first = pl.multiple_of(group * 2 * chip_rows + place * chip_rows, 16)
            wb_ref[pl.ds(first, chip_rows), :] = pieces[2 + turn][
                group * chip_rows : (group + 1) * chip_rows, :
            ]


def code_columns(code_ref, first, count):
    rows = code_ref[:, first : first + count].astype(BF16)
    pick = (iota((8, LANES), 0) == 0).astype(BF16)
    return tn(rows, pick)


def forward_kernel(experts, chip_rows, count, far_ref, where_ref, *refs):
    forward_body(experts, chip_rows, far_ref, where_ref, refs[:count], *refs[count:])


def forward_body(
    experts,
    chip_rows,
    far_ref,
    where_ref,
    pieces,
    x_ref,
    came_ref,
    bias_ref,
    earlier_ref,
    hid_ref,
    q_ref,
    k_ref,
    v_ref,
    gain_ref,
    small_ref,
    code_ref,
    low_ref,
    lse_ref,
    q_all,
    k_all,
    v_all,
    raw,
    prob,
    wa_ref,
    wb_ref,
    hid_scr,
    code_col,
):
    del earlier_ref
    step = pl.program_id(0)
    own, half = q_ref.shape
    split = wa_ref.shape[1]
    cut = split - half
    core = where_ref[0]
    tok = x_ref.shape[0] - CODE_ROWS

    @pl.when(step == 0)
    def _():
        join_weights(chip_rows, where_ref, pieces, wa_ref, wb_ref)
        small_ref[...] = wb_ref[:, split - LANES :]
        gain_ref[...] = picked_rows(wb_ref[:, split - LANES :], experts)
        code_ref[...] = jnp.zeros_like(code_ref)

    @pl.when(step < 3)
    def _():
        for ref, which in ((x_ref, core), (came_ref, 1 - core)):
            tokens = ref[:tok, :].astype(F32)
            scale = lax.rsqrt(jnp.mean(tokens * tokens, axis=-1, keepdims=True) + EPSILON)
            hid_scr[pl.ds(pl.multiple_of(which * tok, tok), tok), :] = (
                tokens * scale * gain_ref[0:1, :]
            ).astype(BF16)
            first = pl.multiple_of(step * own + which * tok, tok)
            code_ref[:, pl.ds(first, tok)] = ref[tok : tok + 8, :tok].astype(F32)
        hidden = hid_scr[...]
        second = nn(hidden, wb_ref[:, : split - LANES]).astype(BF16)
        k_ref[:, :cut] = nn(hidden, wa_ref[:, half:]).astype(BF16)
        k_ref[:, cut:] = second[:, : half - cut]
        v_ref[...] = second[:, half - cut :]
        rows = pl.ds(pl.multiple_of(step * own, own), own)
        k_all[rows, :] = k_ref[...]
        v_all[rows, :] = v_ref[...]

        @pl.when(step == 1)
        def _():
            query = nn(hidden, wa_ref[:, :half]).astype(BF16)
            q_ref[...] = query
            q_all[...] = query
            hid_ref[...] = hidden
            code_col[...] = code_columns(code_ref, own, own)

    @pl.when(step >= 3)
    def _():
        pair = step - 3
        lanes = pl.ds(pl.multiple_of(pair * LANES, LANES), LANES)
        window = 5 * BLK
        lane = iota((BLK, LANES), 1)
        lse_ref[...] = jnp.zeros_like(lse_ref)
        for block in range(own // BLK):
            rows = slice(block * BLK, (block + 1) * BLK)
            cols = slice(block * BLK, block * BLK + window)
            query = q_all[rows, lanes]
            keys = k_all[cols, lanes]
            values = v_all[cols, lanes]
            outs = []
            for turn in range(2):
                raw[turn] = nt(own_half(query, turn), keys)
            logs = jnp.zeros((BLK, LANES), F32)
            for turn in range(2):
                head = pair * 2 + turn
                found = []
                for first in range(0, BLK, CHUNK):
                    part = slice(first, first + CHUNK)
                    here = block * BLK + first
                    mask = code_col[here : here + CHUNK, 0:1] == code_ref[0:1, cols]
                    scores = masked_scores(
                        raw[turn, part, :],
                        bias_ref[turn, part, :],
                        far_ref[pl.ds(head, 1), 15:16],
                        far_ref[pl.ds(head, 1), 31:32],
                        mask,
                    )
                    top = jnp.max(scores, axis=1, keepdims=True)
                    weight = jnp.exp(scores - top)
                    total = jnp.sum(weight, axis=1, keepdims=True)
                    prob[turn, part, :] = (weight * (1.0 / total)).astype(BF16)
                    found.append(top + jnp.log(total))
                outs.append(nn(prob[turn], values))
                logs = jnp.where(lane == turn, jnp.concatenate(found, axis=0), logs)
            low_ref[rows, :] = jnp.where(lane < LANES // 2, outs[0], outs[1]).astype(BF16)
            lse_ref[0, 0:2, rows] = jnp.transpose(logs)[0:2, :]


def halo_query_kernel(chip_rows, where_ref, x_ref, came_ref, gain_ref, *refs):
    pieces, (q_ref, hid_scr, wa_ref) = refs[:-3], refs[-3:]
    half = q_ref.shape[1]
    core = where_ref[0]
    tok = x_ref.shape[0] - CODE_ROWS

    @pl.when(pl.program_id(0) == 0)
    def _():
        rows = pieces[0].shape[0]
        if len(pieces) == 1:
            wa_ref[...] = pieces[0][...]
        else:
            for turn in range(2):
                place = where_ref[1] if turn == 0 else 1 - where_ref[1]
                wa_ref[pl.ds(pl.multiple_of(place * rows, rows), rows), :] = pieces[turn][...]

    for ref, which in ((x_ref, core), (came_ref, 1 - core)):
        tokens = ref[:tok, :].astype(F32)
        scale = lax.rsqrt(jnp.mean(tokens * tokens, axis=-1, keepdims=True) + EPSILON)
        hid_scr[pl.ds(pl.multiple_of(which * tok, tok), tok), :] = (
            tokens * scale * gain_ref[0:1, :]
        ).astype(BF16)
    q_ref[...] = nn(hid_scr[...], wa_ref[:, :half]).astype(BF16)


def turned(rows):
    parts = jnp.concatenate([piece.astype(F32) for piece in three_parts(rows)], axis=0)
    pick = iota((3 * rows.shape[0], LANES), 0) % rows.shape[0] == iota(
        (3 * rows.shape[0], LANES), 1
    )
    return tn(parts.astype(BF16), pick.astype(BF16))


def packed_rows(rows):
    parts = [piece.astype(F32) for piece in three_parts(rows)]
    halves = [
        jnp.concatenate([part[:, first : first + LANES] for part in parts], axis=1)
        for first in (0, LANES)
    ]
    return jnp.concatenate(halves, axis=0).astype(BF16)


def unpacked_rows(packed):
    packed = packed.astype(F32)
    total = sum(packed[:, first : first + LANES] for first in range(0, 3 * LANES, LANES))
    return jnp.concatenate([total[:8], total[8:]], axis=1)


def rolled_left(value, steps):
    return value if steps == 0 else pltpu.roll(value, value.shape[1] - steps, 1)


def diagonal_sums(value):
    eight = jnp.zeros((8, value.shape[1]), F32)
    for first in range(0, value.shape[0], 8):
        eight = eight + rolled_left(value[first : first + 8], first)
    one = jnp.zeros((1, value.shape[1]), F32)
    for row in range(8):
        one = one + rolled_left(eight[row : row + 1], row)
    return one


def own_backward_kernel(
    far_ref,
    q_ref,
    k_ref,
    v_ref,
    msg_ref,
    lse_ref,
    bias_ref,
    code_ref,
    dq_ref,
    dk_ref,
    dv_ref,
    tab_ref,
    raw,
    grown,
    prob,
    grads,
    near_sum,
):
    pair = pl.program_id(0)
    own = q_ref.shape[0]
    blocks = own // BLK
    deep = msg_ref.shape[0] // blocks
    window = 5 * BLK
    near = bias_ref.shape[2]
    edge = (window - near) // 2
    lanes = pl.ds(pl.multiple_of(pair * LANES, LANES), LANES)
    lane = iota((BLK, LANES), 1)
    codes = code_columns(code_ref, own, own)
    dk_ref[...] = jnp.zeros_like(dk_ref)
    dv_ref[...] = jnp.zeros_like(dv_ref)
    side = iota((window, LANES), 0)
    side_lane = iota((window, LANES), 1)
    ends = ((side < edge) & (side_lane == 0)) | ((side >= edge + near) & (side_lane == 1))
    ends = ends.astype(BF16)
    end_sums = [jnp.zeros((1, LANES), F32), jnp.zeros((1, LANES), F32)]
    for block in range(blocks):
        rows = slice(block * BLK, (block + 1) * BLK)
        cols = slice(block * BLK, block * BLK + window)
        keys = k_ref[cols, :]
        values = v_ref[cols, :]
        keys_ends = jnp.concatenate([keys, ends], axis=1)
        mine = slice((blocks - block) * BLK, (2 * blocks - block) * BLK)
        first = block * deep
        gctx_all = msg_ref[first : first + BLK, lanes]
        deltas = turned(unpacked_rows(msg_ref[first + BLK : first + BLK + 16, :]))
        logs = turned(lse_ref[0, :, rows])
        outs = []
        for turn in range(2):
            raw[turn] = nt(own_half(q_ref[rows, :], turn), keys)
            grown[turn] = nt(own_half(gctx_all, turn), values)
        for turn in range(2):
            head = pair * 2 + turn
            delta = jnp.sum(jnp.where(lane == head, deltas, 0.0), axis=1, keepdims=True)
            log = logs[:, turn : turn + 1]
            for start in range(0, BLK, CHUNK):
                part = slice(start, start + CHUNK)
                here = block * BLK + start
                mask = codes[here : here + CHUNK, 0:1] == code_ref[0:1, cols]
                scores = masked_scores(
                    raw[turn, part, :],
                    bias_ref[turn, part, :],
                    far_ref[pl.ds(head, 1), 15:16],
                    far_ref[pl.ds(head, 1), 31:32],
                    mask,
                )
                probs = jnp.exp(scores - log[part])
                low = (probs * (grown[turn, part, :] - delta[part])).astype(BF16)
                prob[turn, part, :] = probs.astype(BF16)
                grads[turn, part, :] = low
                wide = low[:, edge : edge + near].astype(F32)
                if block == 0:
                    near_sum[turn, part, :] = wide
                else:
                    near_sum[turn, part, :] += wide
        for turn in range(2):
            query = own_half(q_ref[rows, :], turn)
            gctx = own_half(gctx_all, turn)
            both = nn(grads[turn], keys_ends)
            outs.append(both[:, :LANES])
            end_sums[turn] = end_sums[turn] + jnp.sum(both[:, LANES:], axis=0, keepdims=True)
            dk_ref[...] += tn(grads[turn, :, mine], query)
            dv_ref[...] += tn(prob[turn, :, mine], gctx)
        dq_ref[rows, :] = jnp.where(lane < LANES // 2, outs[0], outs[1]).astype(BF16)
    apart = iota((BLK, near), 1) - (2 * BLK - edge) - iota((BLK, near), 0)
    tab_lane = iota((1, LANES), 1)
    hot = (bucket_of(iota((near, LANES), 0) - LANES) == iota((near, LANES), 1)).astype(F32)
    for turn in range(2):
        total = near_sum[turn]
        left = end_sums[turn][:, 0:1] + jnp.sum(jnp.where(apart <= -FAR, total, 0.0))
        right = end_sums[turn][:, 1:2] + jnp.sum(jnp.where(apart >= FAR, total, 0.0))
        close = jnp.where(jnp.abs(apart) < FAR, total, 0.0)
        diagonal = diagonal_sums(close)
        sums = lax.dot_general(
            diagonal,
            hot,
            (((1,), (0,)), ((), ())),
            precision=lax.Precision.HIGHEST,
            preferred_element_type=F32,
        )
        sums = sums + jnp.where(tab_lane == 15, left, 0.0) + jnp.where(tab_lane == 31, right, 0.0)
        tab_ref[0, turn : turn + 1, :] = sums


def halo_backward_kernel(
    far_ref,
    qp_ref,
    qn_ref,
    k_ref,
    v_ref,
    gp_ref,
    gn_ref,
    lp_ref,
    ln_ref,
    biasp_ref,
    biasn_ref,
    code_ref,
    dka_ref,
    dva_ref,
    earlier_ref,
    dk_ref,
    dv_ref,
    delta_ref,
):
    del earlier_ref
    pair = pl.program_id(0)
    own = k_ref.shape[0]
    half = LANES
    codes = code_columns(code_ref, own, own)
    lanes = pl.ds(pl.multiple_of(pair * LANES, LANES), LANES)
    deep = gp_ref.shape[0] // 2
    for side, g_side in enumerate((gp_ref, gn_ref)):
        for block in range(2):
            first = block * deep + BLK
            delta_ref[side, :, block * BLK : (block + 1) * BLK] = unpacked_rows(
                g_side[first : first + 16, :]
            )
    total_k = dka_ref[...]
    total_v = dva_ref[...]
    parts = []
    for side in range(2):
        q_side = qp_ref if side == 0 else qn_ref
        g_side = gp_ref if side == 0 else gn_ref
        for block in range(2):
            far_block = block == side
            rows = slice(block * BLK, (block + 1) * BLK)
            if far_block:
                cols = slice(0, BLK) if side == 0 else slice(own - BLK, own)
            else:
                cols = slice(0, own)
            parts.append((side, rows, cols, far_block, q_side, g_side))
    add_k = [jnp.zeros((BLK, LANES), F32), jnp.zeros((BLK, LANES), F32)]
    add_v = [jnp.zeros((BLK, LANES), F32), jnp.zeros((BLK, LANES), F32)]
    for side, rows, cols, far_block, q_side, g_side in parts:
        keys = k_ref[cols, :]
        values = v_ref[cols, :]
        count = cols.stop - cols.start
        lse_ref = lp_ref if side == 0 else ln_ref
        places = slice(rows.start // BLK * deep, rows.start // BLK * deep + BLK)
        first = 2 * own * side + rows.start
        mask = codes[cols, 0:1] == code_ref[0:1, first : first + BLK]
        for turn in range(2):
            head = pair * 2 + turn
            query = own_half(q_side[rows, :], turn)
            gctx = own_half(g_side[places, lanes], turn)
            raw = nt(keys, query)
            far = far_ref[pl.ds(head, 1), 15:16] if side else far_ref[pl.ds(head, 1), 31:32]
            if far_block:
                raw = raw + far
            elif side == 0:
                raw = jnp.concatenate(
                    [raw[:half] + biasp_ref[turn].astype(F32), raw[half:] + far], axis=0
                )
            else:
                raw = jnp.concatenate(
                    [raw[: count - half] + far, raw[count - half :] + biasn_ref[turn].astype(F32)],
                    axis=0,
                )
            scores = jnp.where(mask, raw, NEGATIVE)
            logs = lse_ref[0, turn : turn + 1, rows]
            delta = delta_ref[side, pl.ds(head, 1), rows]
            probs = jnp.exp(scores - logs)
            grads = (probs * (nt(values, gctx) - delta)).astype(BF16)
            got_k = nn(grads, query)
            got_v = nn(probs.astype(BF16), gctx)
            for index in range(count // BLK):
                place = (cols.start // BLK) + index
                part = slice(index * BLK, (index + 1) * BLK)
                add_k[place] = add_k[place] + got_k[part]
                add_v[place] = add_v[place] + got_v[part]
    dk_ref[...] = (total_k + jnp.concatenate(add_k, axis=0)).astype(BF16)
    dv_ref[...] = (total_v + jnp.concatenate(add_v, axis=0)).astype(BF16)


def token_columns(meta_ref, probs):
    route_hot = iota(probs.shape, 1) == meta_ref[:, 1:2]
    slot_hot = iota((probs.shape[0], LANES), 1) == meta_ref[:, 2:3]
    gate = jnp.sum(jnp.where(route_hot, probs, 0.0), axis=1, keepdims=True)
    return route_hot, slot_hot, gate


def join_halves(where_ref, near_ref, far_ref, out_ref):
    half = near_ref.shape[0]
    side = where_ref[1]
    out_ref[pl.ds(pl.multiple_of(side * half, half), half), :] = near_ref[...]
    out_ref[pl.ds(pl.multiple_of((1 - side) * half, half), half), :] = far_ref[...]


def before_kernel(
    cap,
    depth,
    experts,
    core_ref,
    x_ref,
    own_ref,
    came_ref,
    wonear_ref,
    wofar_ref,
    small_ref,
    gain_ref,
    meta_col_ref,
    meta_row_ref,
    mid_ref,
    hid_ref,
    prob_ref,
    msg_out_ref,
    flat,
    msg,
    wo_ref,
):
    core = core_ref[0]
    tok = x_ref.shape[0]
    width = own_ref.shape[1]
    rows = pl.ds(pl.multiple_of(core * tok, tok), tok)
    join_halves(core_ref, wonear_ref, wofar_ref, wo_ref)
    own_w = wo_ref[pl.ds(pl.multiple_of(core * width, width), width), :]
    other_w = wo_ref[pl.ds(pl.multiple_of((1 - core) * width, width), width), :]
    mid_ref[...] = (
        x_ref[...].astype(F32) + nn(own_ref[rows, :], own_w) + nn(came_ref[rows, :], other_w)
    )
    middle = mid_ref[...]
    scale = lax.rsqrt(jnp.mean(middle * middle, axis=-1, keepdims=True) + EPSILON)
    hidden = (middle * scale * gain_ref[1:2, :]).astype(BF16)
    hid_ref[...] = hidden
    logits = nn(hidden, small_ref[...])
    lane = iota(logits.shape, 1)
    logits = jnp.where(lane < experts, logits, NEGATIVE)
    weight = jnp.exp(logits - jnp.max(logits, axis=1, keepdims=True))
    probs = weight / jnp.sum(weight, axis=1, keepdims=True)
    prob_ref[...] = probs
    _, slot_hot, gate = token_columns(meta_col_ref, probs)
    route_rows = (iota((experts, tok), 0) == meta_row_ref[1:2, :]).astype(BF16)
    values = values_in(route_rows, slot_hot, gate)
    hot = (iota((flat.shape[0], tok), 0) == meta_row_ref[0:1, :]).astype(BF16)
    flat[...] = nn(hot, hidden)
    fill_message(msg_out_ref, flat, msg, cap, depth, values)


def gelu_parts(before):
    square = before * before
    inner = jnp.tanh(before * (GELU_A + (GELU_A * GELU_B) * square))
    half = 0.5 + 0.5 * inner
    slope = half + (before * (1.0 - inner * inner)) * (
        0.5 * GELU_A + (1.5 * GELU_A * GELU_B) * square
    )
    return before * half, slope


def expert_kernel(
    cap,
    depth,
    msg_ref,
    cot_ref,
    win_ref,
    wout_ref,
    earlier_a_ref,
    earlier_b_ref,
    earlier_c_ref,
    rows_ref,
    grad_ref,
    act_ref,
    gbef_ref,
    back_msg_ref,
    made_acc,
    back_acc,
    msg,
):
    del earlier_a_ref, earlier_b_ref, earlier_c_ref
    step = pl.program_id(0)
    count = rows_ref.shape[0]
    groups = count // cap

    @pl.when(step == 0)
    def _():
        values = read_message(msg_ref, made_acc, msg, cap, depth)
        rows_ref[...] = made_acc[...].astype(BF16)
        by_row, _, slot_hot = slot_places(count, groups, cap)
        gate = values_out(by_row, slot_hot, values)
        grad_ref[...] = (gate * cot_ref[...].astype(F32)).astype(BF16)
        made_acc[...] = jnp.zeros_like(made_acc)
        back_acc[...] = jnp.zeros_like(back_acc)

    w_in = win_ref[0]
    w_out = wout_ref[0]
    before = nn(rows_ref[...], w_in)
    grad_active = nt(grad_ref[...], w_out)
    active, slope = gelu_parts(before)
    active = active.astype(BF16)
    grad_before = (grad_active * slope).astype(BF16)
    act_ref[...] = active
    gbef_ref[...] = grad_before
    made_acc[...] += nn(active, w_out)
    back_acc[...] += nt(grad_before, w_in)

    @pl.when(step == pl.num_programs(0) - 1)
    def _():
        produced = made_acc[...].astype(BF16)
        grad_gate = jnp.sum(
            cot_ref[...].astype(F32) * produced.astype(F32), axis=1, keepdims=True
        )
        _, by_col, slot_hot = slot_places(count, groups, cap)
        values = values_in(by_col, slot_hot, grad_gate)
        fill_message(back_msg_ref, back_acc, msg, cap, depth, values, 0, 2)
        made_acc[...] = produced.astype(F32)
        fill_message(back_msg_ref, made_acc, msg, cap, depth, None, 1, 2)


def expert_grads_kernel(
    cap,
    depth,
    rows_ref,
    grad_ref,
    act_ref,
    gbef_ref,
    msgs_ref,
    cots_ref,
    win_ref,
    wout_ref,
    din_ref,
    dout_ref,
    all_rows,
    all_grad,
    flat,
    msg,
):
    count = rows_ref.shape[0]
    size = msg.shape[0]

    @pl.when(pl.program_id(0) == 0)
    def _():
        all_rows[:count, :] = rows_ref[...]
        all_grad[:count, :] = grad_ref[...]
        by_row, _, slot_hot = slot_places(count, count // cap, cap)
        for other in range(msgs_ref.shape[0] // size):
            values = read_message(msgs_ref, flat, msg, cap, depth, start=other * size)
            gate = values_out(by_row, slot_hot, values)
            first = (other + 1) * count
            all_rows[first : first + count, :] = flat[...].astype(BF16)
            cots = cots_ref[other * count : (other + 1) * count, :].astype(F32)
            all_grad[first : first + count, :] = (gate * cots).astype(BF16)

    w_in = win_ref[0]
    w_out = wout_ref[0]
    active, slope = gelu_parts(nn(all_rows[count:, :], w_in))
    grad_before = (nt(all_grad[count:, :], w_out) * slope).astype(BF16)
    actives = jnp.concatenate([act_ref[...], active.astype(BF16)], axis=0)
    grads = jnp.concatenate([gbef_ref[...], grad_before], axis=0)
    din_ref[0] = tn(all_rows[...], grads)
    dout_ref[0] = tn(actives, all_grad[...])


def sums_kernel(
    chip_rows,
    bits_ref,
    hid_ref,
    dq_ref,
    dk_ref,
    dv_ref,
    extra_ref,
    tab_ref,
    earlier_ref,
    senda_ref,
    keepa_ref,
    sendb_ref,
    keepb_ref,
    total,
):
    del earlier_ref
    rows = hid_ref.shape[1]
    half = dq_ref.shape[1]
    split = keepa_ref.shape[1]
    cut = split - half
    hidden = hid_ref[...]
    bit_a = bits_ref[3]
    bit_b = bits_ref[4]
    chunk = keepa_ref.shape[0]
    total[:, :half] = tn(hidden, dq_ref[...])
    total[:, half:] = tn(hidden, dk_ref[:, :cut])
    keepa_ref[...] = total[pl.ds(pl.multiple_of(bit_a * chunk, chunk), chunk), :]
    senda_ref[...] = total[pl.ds(pl.multiple_of((1 - bit_a) * chunk, chunk), chunk), :].astype(BF16)
    total[:, : half - cut] = tn(hidden, dk_ref[:, cut:])
    total[:, half - cut : split - LANES] = tn(hidden, dv_ref[...])
    total[:, split - LANES :] = extra_ref[...]
    chunk = chip_rows
    table = jnp.concatenate([tab_ref[pair, 0:2, :] for pair in range(tab_ref.shape[0])], axis=0)
    table = jnp.where(iota(table.shape, 1) < TABLE, table, 0.0)
    table = pltpu.roll(table, LANES - TABLE, 1)
    for index in range(2 * rows // chunk):
        first = index * chunk // 2
        total[first : first + table.shape[0], split - LANES :] += table
    for index in range(rows // (2 * chunk)):
        first = index * 2 * chunk
        out = slice(index * chunk, (index + 1) * chunk)
        keepb_ref[out, :] = total[pl.ds(pl.multiple_of(first + bit_b * chunk, 8), chunk), :]
        gone = total[pl.ds(pl.multiple_of(first + (1 - bit_b) * chunk, 8), chunk), :]
        sendb_ref[out, :] = gone.astype(BF16)


def add_blocks(counts, refs, total):
    first, at = 0, 0
    for count in counts:
        value = refs[at][...]
        for ref in refs[at + 1 : at + count]:
            value = value + ref[...].astype(F32)
        last = first + value.shape[1]
        total[:, first:last] = value
        first, at = last, at + count


def stage_kernel(counts, groups, rows, where_at, where_ref, later_ref, *refs):
    del later_ref
    blocks, (gone_ref, kept_ref, total) = refs[:-3], refs[-3:]
    add_blocks(counts, blocks, total)
    mine = where_ref[where_at]
    for group in range(groups):
        out = slice(group * rows, (group + 1) * rows)
        base = group * 2 * rows
        kept_ref[out, :] = total[pl.ds(pl.multiple_of(base + mine * rows, 8), rows), :]
        gone = total[pl.ds(pl.multiple_of(base + (1 - mine) * rows, 8), rows), :]
        gone_ref[out, :] = gone.astype(gone_ref.dtype)


def join_kernel(counts, groups, rows, where_ref, later_ref, *refs):
    del later_ref
    blocks, outs, total = refs[: sum(counts)], refs[sum(counts) : -1], refs[-1]
    add_blocks(counts, blocks, total)
    for other, ref in enumerate(outs):
        place = where_ref[5] ^ other
        for group in range(groups):
            first = pl.multiple_of((group * len(outs) + place) * rows, 8)
            ref[group * rows : (group + 1) * rows, :] = total[pl.ds(first, rows), :].astype(
                ref.dtype
            )


def input_kernel(chip_rows, where_ref, dq_ref, dk_ref, dv_ref, later_ref, *refs):
    del later_ref
    pieces, (keep_ref, send_ref, token_ref, wa_ref, wb_ref) = refs[:-5], refs[-5:]
    token_ref[...] = jnp.zeros_like(token_ref)
    join_weights(chip_rows, where_ref, pieces, wa_ref, wb_ref)
    core = where_ref[0]
    half = dq_ref.shape[1]
    split = wa_ref.shape[1]
    cut = split - half
    tok = keep_ref.shape[0]
    for out_ref, which in ((send_ref, 1 - core), (keep_ref, core)):
        rows = pl.ds(pl.multiple_of(which * tok, tok), tok)
        out_ref[...] = (
            nt(dq_ref[rows, :], wa_ref[:, :half])
            + nt(dk_ref[rows, :cut], wa_ref[:, half:])
            + nt(dk_ref[rows, cut:], wb_ref[:, : half - cut])
            + nt(dv_ref[rows, :], wb_ref[:, half - cut : split - LANES])
        )


def finish_input_kernel(part_ref, came_ref, x_ref, gain_ref, mid_ref, out_ref, token_ref):
    token_ref[...] = jnp.zeros_like(token_ref)
    grad_hidden = part_ref[...] + came_ref[...]
    tokens = x_ref[...].astype(F32)
    scale = lax.rsqrt(jnp.mean(tokens * tokens, axis=-1, keepdims=True) + EPSILON)
    normed = tokens * scale
    grad_normed = grad_hidden * gain_ref[0:1, :]
    out_ref[...] = (
        mid_ref[...]
        + scale
        * (grad_normed - normed * jnp.mean(grad_normed * normed, axis=-1, keepdims=True))
    ).astype(BF16)


def output_weight_kernel(
    where_ref, ctx_ref, ctx_came_ref, ga_ref, ga_came_ref, later_ref, gone_ref, kept_ref, token_ref, ga, total
):
    del later_ref
    token_ref[...] = jnp.zeros_like(token_ref)
    core = where_ref[0]
    tok = ga_ref.shape[0]
    half = ctx_ref.shape[1]
    ga[pl.ds(pl.multiple_of(core * tok, tok), tok), :] = ga_ref[...]
    ga[pl.ds(pl.multiple_of((1 - core) * tok, tok), tok), :] = ga_came_ref[...]
    cols = ga[...]
    total[pl.ds(pl.multiple_of(core * half, half), half), :] = tn(ctx_ref[...], cols)
    total[pl.ds(pl.multiple_of((1 - core) * half, half), half), :] = tn(ctx_came_ref[...], cols)
    mine = where_ref[3]
    gone_ref[...] = total[pl.ds(pl.multiple_of((1 - mine) * half, half), half), :].astype(BF16)
    kept_ref[...] = total[pl.ds(pl.multiple_of(mine * half, half), half), :]


def finish_kernel(
    experts,
    buckets,
    where_ref,
    kept_ref,
    came_ref,
    wq_ref,
    wk_ref,
    wv_ref,
    gain_ref,
    q_ref,
    k_ref,
    v_ref,
    o_ref,
    router_ref,
    gains_ref,
    table_ref,
):
    core = where_ref[0]
    half = q_ref.shape[1] // 2
    split = (kept_ref.shape[1] - half) // 2
    cut = split - half
    last = kept_ref.shape[1] - LANES
    for source, which in ((kept_ref, core), (came_ref, 1 - core)):
        cols = pl.ds(pl.multiple_of(which * half, half), half)
        q_ref[:, cols] = source[:, :half]
        k_ref[:, cols] = jnp.concatenate(
            [source[:, half:split], source[:, split + half : split + 2 * half - cut]], axis=1
        )
        o_ref[:, cols] = source[:, split : split + half]
        v_ref[:, cols] = source[:, last - half : last]
    kept = kept_ref[:, last:]
    came = came_ref[:, last:]
    both = kept + came
    pick = iota((experts, LANES), 0) == iota((experts, LANES), 1)
    router_ref[...] = exact_nt(pick.astype(F32), both)
    weighted = (
        q_ref[...] * wq_ref[...].astype(F32)
        + k_ref[...] * wk_ref[...].astype(F32)
        + v_ref[...] * wv_ref[...].astype(F32)
    )
    gain_one = jnp.sum(weighted, axis=1, keepdims=True) / gain_ref[...].astype(F32)
    lane = iota(both.shape, 1)
    cols = jnp.where(lane == 0, gain_one, jnp.where(lane == 1, both[:, experts : experts + 1], 0.0))
    gains_ref[...] = exact_nt((iota((8, LANES), 0) == iota((8, LANES), 1)).astype(F32), cols)
    heads = table_ref.shape[0] // 2
    own = kept[:heads, LANES - buckets :]
    other = came[:heads, LANES - buckets :]
    first = jnp.where(core == 0, own, other)
    second = jnp.where(core == 0, other, own)
    table_ref[...] = jnp.concatenate([first, second], axis=0)


def after_kernel(
    cap,
    depth,
    experts,
    core_ref,
    msg_in_ref,
    cot_ref,
    mid_ref,
    hid_ref,
    prob_ref,
    small_ref,
    gain_ref,
    wonear_ref,
    wofar_ref,
    meta_ref,
    own_ref,
    came_ref,
    earlier_ref,
    gmid_ref,
    gmine_ref,
    gtheirs_ref,
    mine_ref,
    theirs_ref,
    sums_ref,
    flat,
    msg,
    low_scr,
    wo_ref,
):
    del earlier_ref
    core = core_ref[0]
    width = mine_ref.shape[1]
    tok = cot_ref.shape[0]
    values = read_message(msg_in_ref, flat, msg, cap, depth, 0, 2)
    hot = (iota((tok, flat.shape[0]), 1) == meta_ref[:, 0:1]).astype(BF16)
    came = nn(hot, flat[...].astype(BF16))
    probs = prob_ref[...]
    route_hot, slot_hot, gate = token_columns(meta_ref, probs)
    by_route = (iota((tok, experts), 1) == meta_ref[:, 1:2]).astype(BF16)
    grad_gate = values_out(by_route, slot_hot, values)
    grad_logits = (grad_gate * probs * (route_hot.astype(F32) - gate)).astype(BF16)
    grad_hidden = came + nt(grad_logits, small_ref[...])
    middle = mid_ref[...]
    scale = lax.rsqrt(jnp.mean(middle * middle, axis=-1, keepdims=True) + EPSILON)
    normed = middle * scale
    grad_normed = grad_hidden * gain_ref[1:2, :]
    grad_middle = cot_ref[...].astype(F32) + scale * (
        grad_normed - normed * jnp.mean(grad_normed * normed, axis=-1, keepdims=True)
    )
    gmid_ref[...] = grad_middle
    low = grad_middle.astype(BF16)
    low_scr[...] = low
    join_halves(core_ref, wonear_ref, wofar_ref, wo_ref)
    own_heads = pl.ds(pl.multiple_of(core * width, width), width)
    other_heads = pl.ds(pl.multiple_of((1 - core) * width, width), width)
    gmine_ref[...] = low_scr[:, own_heads]
    gtheirs_ref[...] = low_scr[:, other_heads]
    rows = pl.ds(pl.multiple_of(core * tok, tok), tok)
    pick = (iota((8, width), 1) // (LANES // 2) == iota((8, width), 0)).astype(F32)
    for out_ref, heads, context in (
        (theirs_ref, other_heads, came_ref[rows, :]),
        (mine_ref, own_heads, own_ref[rows, :]),
    ):
        gctx = nt(low, wo_ref[heads, :]).astype(BF16)
        delta = lax.dot_general(
            pick,
            gctx.astype(F32) * context.astype(F32),
            (((1,), (1,)), ((), ())),
            precision=lax.Precision.HIGHEST,
            preferred_element_type=F32,
        )
        out_ref[:tok, :] = gctx
        out_ref[tok:, :] = packed_rows(delta)
    router = tn(hid_ref[...], grad_logits)
    gain = lax.dot_general(
        grad_hidden * normed,
        jnp.ones((tok, LANES), F32),
        (((0,), (0,)), ((), ())),
        precision=lax.Precision.HIGHEST,
        preferred_element_type=F32,
    )
    lane = iota(router.shape, 1)
    sums_ref[...] = jnp.where(lane < experts, router, jnp.where(lane == experts, gain, 0.0))


def output_kernel(cap, depth, msg_in_ref, mid_ref, prob_ref, meta_ref, out_ref, token_ref, flat, msg):
    token_ref[...] = jnp.zeros_like(token_ref)
    tok = out_ref.shape[0]
    read_message(msg_in_ref, flat, msg, cap, depth, 1, 2)
    hot = (iota((tok, flat.shape[0]), 1) == meta_ref[:, 0:1]).astype(BF16)
    combined = nn(hot, flat[...].astype(BF16))
    _, _, gate = token_columns(meta_ref, prob_ref[...])
    out_ref[...] = (mid_ref[...] + gate * combined).astype(BF16)


class Place:
    def __init__(self):
        self.n_seq = lax.axis_size("seq")
        self.n_ctx = lax.axis_size("ctx")
        self.count = self.n_seq * self.n_ctx
        self.index = lax.axis_index("seq") * self.n_ctx + lax.axis_index("ctx")
        self.core = self.index % 2
        ctx_bits = (self.n_ctx - 1).bit_length()
        self.bits = (self.count - 1).bit_length()
        self.far_bits = list(range(ctx_bits - 1, 1, -1))
        self.near_bits = [1]
        self.seq_bits = list(range(self.bits - 1, ctx_bits - 1, -1))

    def swap(self, value, bit):
        pairs = [(i, i ^ (1 << bit)) for i in range(self.count)]
        return lax.ppermute(value, AXES, pairs)

    def bit(self, which):
        return (self.index >> which) & 1

    def shift(self, value, steps):
        pairs = []
        for row in range(self.n_seq):
            for col in range(self.n_ctx):
                if 0 <= col + steps < self.n_ctx:
                    pairs.append((row * self.n_ctx + col, row * self.n_ctx + col + steps))
        return lax.ppermute(value, AXES, pairs)

    def ordered(self, own, came, bit, axis, join):
        mine = self.bit(bit) == 1
        return join([jnp.where(mine, came, own), jnp.where(mine, own, came)], axis=axis)

    def stage(self, block, bit, done):
        axis = sum(1 for other in done if other > bit)
        return self.ordered(block, self.swap(block, bit), bit, axis, jnp.stack), done + [bit]

    def several(self, bits):
        index = 0
        for bit in bits:
            index = index * 2 + self.bit(bit)
        masks = []
        for other in range(1, 1 << len(bits)):
            mask = sum(((other >> (len(bits) - 1 - at)) & 1) << bit for at, bit in enumerate(bits))
            masks.append((other, mask))
        return index, masks

    def swap_mask(self, value, mask):
        return lax.ppermute(value, AXES, [(i, i ^ mask) for i in range(self.count)])

    def gather(self, block, order, done=()):
        done = list(done)
        for bit in order:
            block, done = self.stage(block, bit, done)
        return block.reshape((-1,) + block.shape[len(done) + 1 :])

    def halves(self, value, bit, order):
        left = sorted(order, reverse=True)
        axis = left.index(bit)
        value = value.reshape((2,) * len(left) + (-1, value.shape[-1]))
        gone = lax.dynamic_index_in_dim(value, 1 - self.bit(bit), axis, keepdims=False)
        kept = lax.dynamic_index_in_dim(value, self.bit(bit), axis, keepdims=False)
        flat = (-1, value.shape[-1])
        return gone.astype(BF16).reshape(flat), kept.reshape(flat)

    def scatter(self, value, order, keep=()):
        left = sorted(list(order) + list(keep), reverse=True)
        value = value.reshape((2,) * len(left) + (-1,) + value.shape[1:])
        for bit in order:
            axis = left.index(bit)
            mine = self.bit(bit)
            gone = lax.dynamic_index_in_dim(value, 1 - mine, axis, keepdims=False).astype(BF16)
            kept = lax.dynamic_index_in_dim(value, mine, axis, keepdims=False)
            value = kept + self.swap(gone, bit).astype(F32)
            left.remove(bit)
        return value.reshape((-1,) + value.shape[-1:])

    def total(self, value):
        for bit in range(1, self.bits):
            value = value + self.swap(value, bit)
        return value


def call(
    kernel,
    outs,
    *args,
    us=0.3,
    grid=None,
    in_specs=None,
    out_specs=None,
    scratch=(),
    smem_first=False,
):
    if in_specs is None:
        in_specs = [whole(a.shape) for a in args]
        if smem_first:
            in_specs[0] = smem()
    if out_specs is None:
        out_specs = [whole(o[0]) for o in outs]
    shapes = [jax.ShapeDtypeStruct(*o) for o in outs]
    inner = kernel
    while isinstance(inner, functools.partial):
        inner = inner.func
    mib = GRANTS.get(inner.__name__, FULL)
    return pl.pallas_call(
        kernel,
        out_shape=shapes,
        grid=grid if grid is not None else (1,),
        in_specs=in_specs,
        out_specs=out_specs,
        scratch_shapes=list(scratch),
        compiler_params=params(mib),
        cost_estimate=pl.CostEstimate(
            flops=int(us * 1.15e9), transcendentals=0, bytes_accessed=0
        ),
    )(*args)


def local(
    inputs,
    cotangent,
    gain_attn,
    w_query,
    w_key,
    w_value,
    w_output,
    bias_table,
    gain_ffn,
    w_router,
    w_in,
    w_out,
    segments,
    routes,
):
    place = Place()
    core = place.core
    x = inputs[0]
    cot = cotangent[0]
    tok, width = x.shape
    heads = bias_table.shape[1]
    buckets = bias_table.shape[0]
    mine_heads = heads // 2
    half = width // 2
    pairs = half // LANES
    experts = w_router.shape[1]
    hidden_units = w_in.shape[2]
    rows_dev = w_query.shape[0]
    cap = max(2, (9 * tok + 8 * experts - 1) // (8 * experts))
    parts = width // LANES
    depth = -(-(parts * cap + 3) // 16) * 16
    n_ctx = place.n_ctx
    slots = n_ctx * cap
    far, near_bits, seq_bits = place.far_bits, place.near_bits, place.seq_bits
    rows_all = 6 * tok
    own_rows = 2 * tok

    where = jnp.stack(
        [
            core,
            place.bit(seq_bits[-1]),
            place.bit(near_bits[-1]),
            place.bit(seq_bits[0]),
            place.bit(near_bits[0]),
            place.several(far)[0],
        ]
    ).astype(jnp.int32)

    long = tok + CODE_ROWS
    columns_all = 4 * half + LANES
    ours, theirs, x_ext = call(
        functools.partial(start_kernel, experts),
        [((rows_dev, columns_all), BF16)] * 2 + [((long, width), BF16)],
        where,
        w_query,
        w_key,
        w_value,
        w_output,
        w_router.T,
        jnp.stack([gain_attn, gain_ffn]),
        x,
        segments,
        smem_first=True,
    )
    block = place.ordered(ours, place.swap(theirs, 0), 0, 0, jnp.concatenate)
    chip_rows = 2 * rows_dev
    halved = chip_rows % 16 == 0
    split = (block.shape[-1] - half) // 2
    around = (place.shift(x_ext, 2), x_ext, place.shift(x_ext, -2))
    near = 2 * BLK
    bias, bias_prev, bias_next, far_bias, meta_col, meta_row = call(
        functools.partial(prepare_kernel, cap, experts),
        [
            ((mine_heads, BLK, near), BF16),
            ((mine_heads, LANES, BLK), BF16),
            ((mine_heads, LANES, BLK), BF16),
            ((8, LANES), F32),
            ((tok, LANES), jnp.int32),
            ((8, tok), jnp.int32),
        ],
        where,
        bias_table,
        routes[0],
        routes[0].reshape(1, tok),
        us=0.3,
        smem_first=True,
    )

    if halved and len(far) == 2:
        came = [place.swap_mask(block, mask) for _, mask in place.several(far)[1]]
        group = 4 * chip_rows
        after_a, after_b, after_o, three = call(
            arrange_kernel,
            [
                ((group, split), BF16),
                ((group, split), BF16),
                ((group, half), BF16),
                ((3 * long, width), BF16),
            ],
            where,
            block,
            *came,
            *around,
            meta_row,
            in_specs=[smem()]
            + [whole(v.shape) for v in (block, *came, *around)]
            + [anywhere()],
        )
        done = list(far)
        after_a = after_a.reshape(2, 2, chip_rows, split)
        after_b = after_b.reshape(2, 2, chip_rows, split)
        after_o = after_o.reshape(2, 2, chip_rows, half)
    else:
        after_far, done = block, []
        for bit in far:
            after_far, done = place.stage(after_far, bit, done)
        after_a, after_b = after_far[..., :split], after_far[..., split : 2 * split]
        after_o = after_far[..., 2 * split :]
        three = call(stack_kernel, [((3 * long, width), BF16)], *around)[0]
    three_came = place.swap(three, 0)
    later_a, done_a = after_a, done
    for bit in near_bits:
        later_a, done_a = place.stage(later_a, bit, done_a)
    later_b, done_b = after_b, done
    for bit in seq_bits:
        later_b, done_b = place.stage(later_b, bit, done_b)
    later_o, done_o = after_o, done
    for bit in near_bits:
        later_o, done_o = place.stage(later_o, bit, done_o)
    later_o = place.ordered(
        later_o, place.swap(later_o, 0), 0, len(later_o.shape) - 1, jnp.concatenate
    )
    for bit in seq_bits[:-1]:
        later_o, done_o = place.stage(later_o, bit, done_o)
    wo_near = later_o.reshape(width // 2, width)
    wo_far = place.swap(wo_near, seq_bits[-1])
    if halved:
        part_rows = width // 2
        pieces_a = (later_a, place.swap(later_a, seq_bits[-1]))
        pieces_b = (later_b, place.swap(later_b, near_bits[-1]))
        pieces = [piece.reshape(part_rows, split) for piece in pieces_a + pieces_b]
    else:
        pieces = [
            place.gather(later_a, seq_bits, done_a),
            place.gather(later_b, near_bits, done_b),
        ]

    def exchange(message):
        shape = message.shape
        message = message.reshape(n_ctx, -1, LANES)
        message = lax.all_to_all(message, "ctx", split_axis=0, concat_axis=0, tiled=True)
        return message.reshape(shape)

    msg_shape = (n_ctx * depth, LANES)
    msg_scratch = [VMEM((slots, width), F32), VMEM(msg_shape, F32)]

    cot_msg = call(
        functools.partial(message_kernel, cap, depth),
        [(msg_shape, BF16)],
        cot,
        meta_row,
        later_a,
        in_specs=[whole((tok, width)), whole((8, tok)), anywhere()],
        scratch=msg_scratch,
    )[0]

    def chip_step(i):
        return jnp.minimum(i, 2)

    def pair_step(i):
        return jnp.maximum(i - 3, 0)

    small_block = whole((width, LANES))
    hid_own, q_own, k_all, v_all, gains, small, codes, ctx_low, lse_rows = call(
        functools.partial(forward_kernel, experts, chip_rows, len(pieces)),
        [
            ((own_rows, width), BF16),
            ((own_rows, half), BF16),
            ((rows_all, half), BF16),
            ((rows_all, half), BF16),
            ((8, width), F32),
            ((width, LANES), BF16),
            ((8, rows_all), F32),
            ((own_rows, half), BF16),
            ((pairs, 8, own_rows), F32),
        ],
        far_bias,
        where,
        *pieces,
        three,
        three_came,
        bias,
        cot_msg,
        us=1.0,
        grid=(3 + pairs,),
        in_specs=[whole((8, LANES)), smem()]
        + [whole(piece.shape) for piece in pieces]
        + [
            pl.BlockSpec((long, width), lambda i: (chip_step(i), 0)),
            pl.BlockSpec((long, width), lambda i: (chip_step(i), 0)),
            pl.BlockSpec((2, BLK, near), lambda i: (pair_step(i), 0, 0)),
            anywhere(),
        ],
        out_specs=[
            whole((own_rows, width)),
            whole((own_rows, half)),
            pl.BlockSpec((own_rows, half), lambda i: (chip_step(i), 0)),
            pl.BlockSpec((own_rows, half), lambda i: (chip_step(i), 0)),
            whole((8, width)),
            whole((width, LANES)),
            whole((8, rows_all)),
            pl.BlockSpec((own_rows, LANES), lambda i: (0, pair_step(i))),
            pl.BlockSpec((1, 8, own_rows), lambda i: (pair_step(i), 0, 0)),
        ],
        scratch=[
            VMEM((own_rows, half), BF16),
            VMEM((rows_all, half), BF16),
            VMEM((rows_all, half), BF16),
            VMEM((2, BLK, 5 * BLK), F32),
            VMEM((2, BLK, 5 * BLK), BF16),
            VMEM((width, split), BF16),
            VMEM((width, split), BF16),
            VMEM((own_rows, width), BF16),
            VMEM((own_rows, LANES), F32),
        ],
    )

    cot_in = exchange(cot_msg)
    cot_rows = call(
        functools.partial(rows_kernel, cap, depth),
        [((slots, width), BF16)],
        cot_in,
        scratch=msg_scratch,
    )[0]

    code_block = whole((8, rows_all))
    far_block = whole((8, LANES))
    own_block = pl.BlockSpec((own_rows, LANES), lambda p: (1, p))
    all_block = pl.BlockSpec((rows_all, LANES), lambda p: (0, p))
    out_block = pl.BlockSpec((own_rows, LANES), lambda p: (0, p))
    bias_block = pl.BlockSpec((2, BLK, near), lambda p: (p, 0, 0))
    lse_block = pl.BlockSpec((1, 8, own_rows), lambda p: (p, 0, 0))

    ctx_came = place.swap(ctx_low, 0)
    mid, hid_two, probs, msg = call(
        functools.partial(before_kernel, cap, depth, experts),
        [
            ((tok, width), F32),
            ((tok, width), BF16),
            ((tok, LANES), F32),
            (msg_shape, BF16),
        ],
        where,
        x,
        ctx_low,
        ctx_came,
        wo_near,
        wo_far,
        small,
        gains,
        meta_col,
        meta_row,
        us=4.0,
        in_specs=[
            smem(),
            whole((tok, width)),
            whole((own_rows, half)),
            whole((own_rows, half)),
            whole((width // 2, width)),
            whole((width // 2, width)),
            small_block,
            whole((8, width)),
            whole((tok, LANES)),
            whole((8, tok)),
        ],
        scratch=msg_scratch + [VMEM((width, width), BF16)],
    )
    msg_in = exchange(msg)
    lse_prev = place.shift(lse_rows, 2)
    lse_next = place.shift(lse_rows, -2)
    pieces_q = pieces[: len(pieces) // 2]
    q_halo = call(
        functools.partial(halo_query_kernel, chip_rows),
        [((2 * own_rows, half), BF16)],
        where,
        three,
        three_came,
        gains,
        *pieces_q,
        us=0.3,
        grid=(2,),
        in_specs=[
            smem(),
            pl.BlockSpec((long, width), lambda i: (2 * i, 0)),
            pl.BlockSpec((long, width), lambda i: (2 * i, 0)),
            whole((8, width)),
        ]
        + [whole(piece.shape) for piece in pieces_q],
        out_specs=[pl.BlockSpec((own_rows, half), lambda i: (i, 0))],
        scratch=[VMEM((own_rows, width), BF16), VMEM((width, split), BF16)],
    )[0]

    fblk = 512
    win_block = pl.BlockSpec((1, width, fblk), lambda i: (0, 0, i))
    wout_block = pl.BlockSpec((1, fblk, width), lambda i: (0, i, 0))
    act_block = pl.BlockSpec((slots, fblk), lambda i: (0, i))
    e_rows, e_grad, e_act, e_gbef, back_msg = call(
        functools.partial(expert_kernel, cap, depth),
        [((slots, width), BF16)] * 2
        + [((slots, hidden_units), BF16)] * 2
        + [((2 * msg_shape[0], LANES), BF16)],
        msg_in,
        cot_rows,
        w_in,
        w_out,
        q_halo,
        lse_prev,
        lse_next,
        us=12.0,
        grid=(hidden_units // fblk,),
        in_specs=[
            whole(msg_shape),
            whole((slots, width)),
            win_block,
            wout_block,
            anywhere(),
            anywhere(),
            anywhere(),
        ],
        out_specs=[whole((slots, width))] * 2
        + [act_block] * 2
        + [whole((2 * msg_shape[0], LANES))],
        scratch=[VMEM((slots, width), F32)] + msg_scratch,
    )
    back_in = exchange(back_msg)

    def from_others(value):
        total = value
        for bit in seq_bits:
            total = jnp.concatenate([total, place.swap(total, bit)], axis=0)
        return total[value.shape[0] :]

    if place.n_seq == 2:
        msgs = place.swap(msg_in, seq_bits[0])
        cots = place.swap(cot_rows, seq_bits[0])
    else:
        msgs = from_others(msg_in)
        cots = from_others(cot_rows)
    all_slots = place.n_seq * slots
    grad_w_in, grad_w_out = call(
        functools.partial(expert_grads_kernel, cap, depth),
        [(w_in.shape, F32), (w_out.shape, F32)],
        e_rows,
        e_grad,
        e_act,
        e_gbef,
        msgs,
        cots,
        w_in,
        w_out,
        us=16.0,
        grid=(hidden_units // fblk,),
        in_specs=[
            whole((slots, width)),
            whole((slots, width)),
            act_block,
            act_block,
            whole(msgs.shape),
            whole(cots.shape),
            win_block,
            wout_block,
        ],
        out_specs=[win_block, wout_block],
        scratch=[VMEM((all_slots, width), BF16), VMEM((all_slots, width), BF16)] + msg_scratch,
    )

    grad_mid, gattn_mine, gattn_theirs, gctx_mine, gctx_theirs, extra = call(
        functools.partial(after_kernel, cap, depth, experts),
        [((tok, width), F32)]
        + [((tok, half), BF16)] * 2
        + [((tok + 16, half), BF16)] * 2
        + [((width, LANES), F32)],
        where,
        back_in,
        cot,
        mid,
        hid_two,
        probs,
        small,
        gains,
        wo_near,
        wo_far,
        meta_col,
        ctx_low,
        ctx_came,
        grad_w_out,
        us=5.0,
        in_specs=[
            smem(),
            whole(back_in.shape),
            whole((tok, width)),
            whole((tok, width)),
            whole((tok, width)),
            whole((tok, LANES)),
            small_block,
            whole((8, width)),
            whole((width // 2, width)),
            whole((width // 2, width)),
            whole((tok, LANES)),
            whole((own_rows, half)),
            whole((own_rows, half)),
            anywhere(),
        ],
        scratch=msg_scratch + [VMEM((tok, width), BF16), VMEM((width, width), BF16)],
    )

    gctx = place.ordered(gctx_mine, place.swap(gctx_theirs, 0), 0, 0, jnp.concatenate)
    gctx_prev = place.shift(gctx, 2)
    gctx_next = place.shift(gctx, -2)

    token = ((8, LANES), F32)
    output, output_made = call(
        functools.partial(output_kernel, cap, depth),
        [((tok, width), BF16), token],
        back_in,
        mid,
        probs,
        meta_col,
        scratch=msg_scratch,
    )

    dq, dk_own, dv_own, tab = call(
        own_backward_kernel,
        [
            ((own_rows, half), BF16),
            ((own_rows, half), F32),
            ((own_rows, half), F32),
            ((pairs, 8, LANES), F32),
        ],
        far_bias,
        q_own,
        k_all,
        v_all,
        gctx,
        lse_rows,
        bias,
        codes,
        us=14.0,
        grid=(pairs,),
        in_specs=[
            far_block,
            out_block,
            all_block,
            all_block,
            whole(gctx.shape),
            lse_block,
            bias_block,
            code_block,
        ],
        out_specs=[out_block] * 3 + [pl.BlockSpec((1, 8, LANES), lambda p: (p, 0, 0))],
        scratch=[
            VMEM((2, BLK, 5 * BLK), F32),
            VMEM((2, BLK, 5 * BLK), F32),
            VMEM((2, BLK, 5 * BLK), BF16),
            VMEM((2, BLK, 5 * BLK), BF16),
            VMEM((2, BLK, near), F32),
        ],
    )

    order_a = seq_bits + near_bits
    order_b = near_bits + seq_bits
    joined = halved and len(seq_bits) == 1 and len(far) == 2
    ga_came = place.swap(gattn_theirs, 0)
    if joined:
        gone_o, kept_o, sooner = call(
            output_weight_kernel,
            [((width // 2, half), BF16), ((width // 2, half), F32), token],
            where,
            ctx_low,
            ctx_came,
            gattn_mine,
            ga_came,
            tab,
            in_specs=[smem()]
            + [whole((own_rows, half))] * 2
            + [whole((tok, half))] * 2
            + [anywhere()],
            scratch=[VMEM((own_rows, half), BF16), VMEM((width, half), F32)],
        )
    else:
        sooner = tab
    halo_bias = pl.BlockSpec((2, LANES, BLK), lambda p: (p, 0, 0))
    dk, dv = call(
        halo_backward_kernel,
        [((own_rows, half), BF16)] * 2,
        far_bias,
        q_halo,
        q_halo,
        k_all,
        v_all,
        gctx_prev,
        gctx_next,
        lse_prev,
        lse_next,
        bias_prev,
        bias_next,
        codes,
        dk_own,
        dv_own,
        sooner,
        us=7.0,
        grid=(pairs,),
        in_specs=[
            far_block,
            out_block,
            own_block,
            own_block,
            own_block,
            whole(gctx.shape),
            whole(gctx.shape),
            lse_block,
            lse_block,
            halo_bias,
            halo_bias,
            code_block,
            out_block,
            out_block,
            anywhere(),
        ],
        out_specs=[out_block] * 2,
        scratch=[VMEM((2, 8, own_rows), F32)],
    )


    def input_parts(later):
        return call(
            functools.partial(input_kernel, chip_rows),
            [((tok, width), F32), ((tok, width), F32), token],
            where,
            dq,
            dk,
            dv,
            later,
            *pieces,
            us=0.3,
            in_specs=[smem()]
            + [whole((own_rows, half))] * 3
            + [anywhere()]
            + [whole(piece.shape) for piece in pieces],
            scratch=[VMEM((width, split), BF16), VMEM((width, split), BF16)],
        )

    def input_gradient(part, part_gone):
        return call(
            finish_input_kernel,
            [((tok, width), BF16), token],
            part,
            place.swap(part_gone, 0),
            x,
            gains,
            grad_mid,
        )

    if joined:
        came_o = place.swap(gone_o, order_a[0])
        gone_a, kept_a, gone_b, kept_b = call(
            functools.partial(sums_kernel, chip_rows),
            [
                ((width // 2, split), BF16),
                ((width // 2, split), F32),
                ((width // 2, split), BF16),
                ((width // 2, split), F32),
            ],
            where,
            hid_own,
            dq,
            dk,
            dv,
            extra,
            tab,
            came_o,
            us=0.3,
            in_specs=[
                smem(),
                whole((own_rows, width)),
                whole((own_rows, half)),
                whole((own_rows, half)),
                whole((own_rows, half)),
                whole((width, LANES)),
                whole((pairs, 8, LANES)),
                anywhere(),
            ],
            scratch=[VMEM((width, split), F32)],
        )
        came_a = place.swap(gone_a, order_a[0])
        came_b = place.swap(gone_b, order_b[0])

        masks = [mask for _, mask in place.several(far)[1]]
        far_count = len(masks) + 1

        def added(kernel, later, counts, blocks, outs, *how):
            columns_all = sum(blocks[sum(counts[:at])].shape[1] for at in range(len(counts)))
            height = blocks[0].shape[0]
            return call(
                functools.partial(kernel, counts, *how),
                [((height // out, columns_all), dtype) for out, dtype in outs],
                where,
                later,
                *blocks,
                us=0.3,
                in_specs=[smem(), anywhere()] + [whole(block.shape) for block in blocks],
                scratch=[VMEM((height, columns_all), F32)],
            )

        def swapped(pieces):
            return [place.swap_mask(piece, mask) for piece, mask in zip(pieces, masks)]

        two = [(2, BF16), (2, F32)]
        four = [(far_count, F32)] + [(far_count, BF16)] * len(masks)
        gone_a, kept_a = added(
            stage_kernel,
            came_b,
            (2, 2),
            (kept_a, came_a, kept_o, came_o),
            two,
            far_count,
            chip_rows,
            4,
        )
        part, part_gone, part_made = input_parts(output_made)
        pieces_z = added(
            join_kernel, far_bias, (2,), (kept_b, came_b), four, 2, chip_rows
        )
        came_a = place.swap(gone_a, order_a[1])
        came_z = swapped(pieces_z[1:])
        grad_tokens, ended = input_gradient(part, part_gone)
        pieces_a = added(join_kernel, part_made, (2,), (kept_a, came_a), four, 1, chip_rows)
        gone_b, kept_b = added(
            stage_kernel, ended, (far_count,), (pieces_z[0], *came_z), two, 1, chip_rows, 3
        )
        came_b = place.swap(gone_b, seq_bits[0])
        came_z = swapped(pieces_a[1:])
        gone, kept = added(
            stage_kernel,
            ended,
            (far_count, 2),
            (pieces_a[0], *came_z, kept_b, came_b),
            [(2, F32), (2, F32)],
            1,
            rows_dev,
            0,
        )
    else:
        ga_cols = place.ordered(gattn_mine, ga_came, 0, 0, jnp.concatenate)
        ctx_full = place.ordered(ctx_low, ctx_came, 0, 1, jnp.concatenate)
        cut = split - half
        total_a = tn(hid_own, jnp.concatenate([dq, dk[:, :cut]], axis=1))
        total_b = tn(hid_own, jnp.concatenate([dk[:, cut:], dv], axis=1))
        grad_tokens, _ = input_gradient(*input_parts(total_a)[:2])
        total_b = jnp.concatenate([total_b, extra], axis=1)
        sums = jnp.concatenate([total_a, total_b, tn(ctx_full, ga_cols)], axis=1)
        sums = place.scatter(sums, seq_bits + near_bits + far[::-1])
        sums = sums.reshape(2, rows_dev, sums.shape[1])
        gone = lax.dynamic_index_in_dim(sums, 1 - core, 0, keepdims=False)
        kept = lax.dynamic_index_in_dim(sums, core, 0, keepdims=False)
    came = place.swap(gone, 0)
    if joined:
        sum_q, sum_k, sum_v, sum_out, grad_router, gain_rows, table_sum = call(
            functools.partial(finish_kernel, experts, buckets),
            [((rows_dev, width), F32)] * 4
            + [((experts, rows_dev), F32), ((8, rows_dev), F32), ((heads, buckets), F32)],
            where,
            kept,
            came,
            w_query,
            w_key,
            w_value,
            gain_attn[:, None],
            smem_first=True,
        )
        grad_gain_one, grad_gain_two = gain_rows[0], gain_rows[1]
        grad_router, table_sum = grad_router.T, table_sum.T
    else:

        def columns(first):
            return place.ordered(
                kept[:, first : first + half], came[:, first : first + half], 0, 1, jnp.concatenate
            )

        sum_q, sum_k, sum_v = columns(0), columns(half), columns(2 * half)
        sum_out = columns(3 * half + LANES)
        extra_sum = kept[:, 3 * half : 3 * half + LANES] + came[:, 3 * half : 3 * half + LANES]
        grad_router = extra_sum[:, :experts]
        grad_gain_two = extra_sum[:, experts]
        weighted = (
            sum_q * w_query.astype(F32) + sum_k * w_key.astype(F32) + sum_v * w_value.astype(F32)
        )
        grad_gain_one = jnp.sum(weighted, axis=1) / gain_attn.astype(F32)
        table = place.total(tab[:, :2].reshape(mine_heads, LANES))
        table = place.ordered(table, place.swap(table, 0), 0, 0, jnp.concatenate)
        table_sum = table[:, :buckets].T

    return (
        output[None],
        grad_tokens[None],
        grad_gain_one,
        sum_q,
        sum_k,
        sum_v,
        sum_out,
        table_sum,
        grad_gain_two,
        grad_router,
        grad_w_in,
        grad_w_out,
    )


def solution(mesh):
    rows = P(("seq", "ctx"), None)
    flat = P(("seq", "ctx"))
    tokens = P("seq", "ctx", None)
    expert = P("ctx", None, None)
    return jax.shard_map(
        local,
        mesh=mesh,
        in_specs=(
            tokens,
            tokens,
            flat,
            rows,
            rows,
            rows,
            rows,
            P(),
            flat,
            rows,
            expert,
            expert,
            P("seq", "ctx"),
            tokens,
        ),
        out_specs=(
            tokens,
            tokens,
            flat,
            rows,
            rows,
            rows,
            rows,
            P(),
            flat,
            rows,
            expert,
            expert,
        ),
        check_vma=False,
    )
```
